32 devices in a mesh: req: 4 (over z), ctx: 4 (over x, core), kvh: 2 (over y).
Axes of the slice: x: 2, y: 2, z: 4, core: 2. Of those that a mesh axis runs over, the one named last changes fastest.
Arguments:
- query: bfloat16 [16, 8, 16, 128], P('req', 'kvh', 'ctx'), may hold values from -15 to 15
- kv_pool: bfloat16 [8192, 16, 8, 256], P(('req', 'ctx'), None, 'kvh'), may hold values from -4 to 4
- page_table: int32 [16, 512], P('req', 'ctx'), may hold values from 0 to 511, as said below
- context_len: int32 [16], P('req'), may hold values from 1024 to 8192
- fresh_kv: bfloat16 [1792, 16, 8, 256], P(('req', 'ctx'), None, 'kvh'), may hold values from -4 to 4
- fresh_bucket: int32 [1792], P(('req', 'ctx')), may hold values from 0 to 63, as said below
Outputs:
- attended: bfloat16 [16, 8, 16, 128], P('req', 'kvh', 'ctx')
The draws below stay inside these ranges and needn't reach their ends.
Inputs may be any that keep to these rules, and one draw needn't show every extreme that they name: `page_table`: within the block of 4 requests and 128 logical pages that one device holds, the entries are a permutation of 0 to 511. `fresh_bucket`: the 112 entries of one device name no bucket more than 2 times.
All inputs are finite; a program needn't handle non-finite values.
Results may differ from the reference program's by a relative error of at most 0.0055.
Values may be sent and summed in bfloat16 or wider, within the bound.
No kernel may reach another device: no remote copies, remote signals or barrier semaphores. Data moves between devices by JAX's collectives and lax.ppermute only.
A program may use at most 128 MiB of HBM per device.

```python
import jax
import jax.numpy as jnp
from jax import lax

KV_HEADS = 8
HEAD_DIM = 128
REQ_DEV = 4
PAGE = 16
PAGES_DEV = 128
NEW_DEV = 112
CAP = 2
GROUP = 16
REQS = 16
POOL = 512
SOURCES = 16
BUCKETS = 64
MAXLEN = 8192
POOL_TOTAL = 8192
FRESH_TOTAL = 1792
N_REQ = 4
N_CTX = 4


def draw_query(key, part):
    key = jax.random.fold_in(key, 5)
    full_shape = (REQS, KV_HEADS, GROUP, HEAD_DIM)
    values = jnp.clip(2.5 * jax.random.normal(key, full_shape, jnp.float32), -15.0, 15.0)
    return values.astype(jnp.bfloat16)


def draw_kv_pool(key, part):
    key = jax.random.fold_in(key, 7)
    full_shape = (POOL_TOTAL, PAGE, KV_HEADS, 2 * HEAD_DIM)
    values = jnp.clip(jax.random.normal(key, full_shape, jnp.float32), -4.0, 4.0)
    return values.astype(jnp.bfloat16)


def draw_page_table(key, part):
    key = jax.random.fold_in(key, 9)
    block_keys = jax.random.split(key, SOURCES)
    orders = jax.vmap(lambda single: jax.random.permutation(single, POOL))(block_keys)
    orders = orders.astype(jnp.int32).reshape(N_REQ, N_CTX, REQ_DEV, PAGES_DEV)
    return jnp.transpose(orders, (0, 2, 1, 3)).reshape(REQS, N_CTX * PAGES_DEV)


def draw_context_len(key, part):
    key = jax.random.fold_in(key, 13)
    first_key, second_key = jax.random.split(key)
    lengths = jax.random.randint(first_key, (REQS,), MAXLEN // 8, MAXLEN + 1, dtype=jnp.int32)
    longest = jax.random.randint(second_key, (), 0, REQS, dtype=jnp.int32)
    return lengths.at[longest].set(MAXLEN)


def draw_fresh_bucket(key, part):
    key = jax.random.fold_in(key, 17)
    star_key, list_key = jax.random.split(key)
    star = jax.random.randint(star_key, (), 0, BUCKETS, dtype=jnp.int32)
    others = jnp.arange((BUCKETS - 1) * CAP, dtype=jnp.int32) // CAP
    others = others + (others >= star).astype(jnp.int32)

    def one_list(single):
        pick_key, order_key = jax.random.split(single)
        picked = jax.random.permutation(pick_key, others)[:NEW_DEV - CAP]
        listed = jnp.concatenate([jnp.full((CAP,), star, jnp.int32), picked])
        return jax.random.permutation(order_key, listed)
    lists = jax.vmap(one_list)(jax.random.split(list_key, SOURCES))
    return lists.reshape(SOURCES * NEW_DEV).astype(jnp.int32)


def steps_of(stream_key, extent, cuts, smallest, largest):
    loudness, own = 1.0, jax.random.fold_in(stream_key, 6)
    for dim, blocks in cuts:
        steps = jnp.exp(jax.random.uniform(jax.random.fold_in(own, dim), (blocks,), jnp.float32, smallest / len(cuts), largest / len(cuts)))
        loudness = loudness * jnp.repeat(steps, extent[dim] // blocks).reshape([-1 if axis == dim else 1 for axis in range(len(extent))])
    return loudness


def gaussian(key, dims, spread, most, shards=(), kind=jnp.bfloat16):
    result = spread * jax.random.normal(key, dims, jnp.float32)
    if shards:
        result = result * steps_of(key, dims, shards, -0.22, 0.18)
    return jnp.clip(result, -most, most).astype(kind)


def setup_inputs(seed: int = 0) -> dict:
    arg_keys = jax.random.split(jax.random.key(seed), 7)
    return {
        "query": draw_query(jax.random.fold_in(arg_keys[6], 71), 0),
        "kv_pool": draw_kv_pool(jax.random.fold_in(arg_keys[6], 71), 0),
        "page_table": draw_page_table(jax.random.fold_in(arg_keys[6], 71), 0),
        "context_len": draw_context_len(jax.random.fold_in(arg_keys[6], 71), 0),
        "fresh_kv": gaussian(arg_keys[4], (FRESH_TOTAL, PAGE, KV_HEADS, 2 * HEAD_DIM), 1.0, 4.0, ((0, 16), (2, 2))),
        "fresh_bucket": draw_fresh_bucket(jax.random.fold_in(arg_keys[6], 71), 0),
    }


NEG = -1.0e30


def reference(query, kv_pool, page_table, context_len, fresh_kv, fresh_bucket):
    score_scale = HEAD_DIM ** -0.5
    page_count = N_CTX * PAGES_DEV
    fresh_keys = fresh_kv.reshape(FRESH_TOTAL * PAGE, KV_HEADS, 2 * HEAD_DIM).astype(jnp.float32)
    fresh_owner = jnp.repeat((fresh_bucket // N_CTX).astype(jnp.int32), PAGE)
    holder = jnp.arange(page_count, dtype=jnp.int32) // PAGES_DEV
    token_index = jnp.arange(page_count * PAGE, dtype=jnp.int32)

    def attend_request(request):
        pool_rows = ((request // REQ_DEV) * N_CTX + holder) * POOL + page_table[request]
        resident = kv_pool[pool_rows].reshape(page_count * PAGE, KV_HEADS, 2 * HEAD_DIM).astype(jnp.float32)
        queries = query[request].astype(jnp.float32)
        near_mask = token_index < context_len[request]
        fresh_mask = fresh_owner == request
        res_scores = jnp.einsum("hgd,thd->hgt", queries, resident[..., :HEAD_DIM]) * score_scale
        res_scores = jnp.where(near_mask, res_scores, NEG)
        new_scores = jnp.einsum("hgd,thd->hgt", queries, fresh_keys[..., :HEAD_DIM]) * score_scale
        new_scores = jnp.where(fresh_mask, new_scores, NEG)
        row_top = jnp.maximum(jnp.max(res_scores, axis=-1), jnp.max(new_scores, axis=-1))[..., None]
        res_weights = jnp.where(near_mask, jnp.exp(res_scores - row_top), 0.0)
        new_weights = jnp.where(fresh_mask, jnp.exp(new_scores - row_top), 0.0)
        totals = jnp.sum(res_weights, axis=-1) + jnp.sum(new_weights, axis=-1)
        res_round = lax.optimization_barrier(res_weights.astype(jnp.bfloat16)).astype(jnp.float32)
        new_round = lax.optimization_barrier(new_weights.astype(jnp.bfloat16)).astype(jnp.float32)
        weighted = jnp.einsum("hgt,thd->hgd", res_round, resident[..., HEAD_DIM:])
        weighted = weighted + jnp.einsum("hgt,thd->hgd", new_round, fresh_keys[..., HEAD_DIM:])
        return (weighted / totals[..., None]).astype(jnp.bfloat16)

    return lax.map(attend_request, jnp.arange(REQS, dtype=jnp.int32))
```

```python
import functools
import math

import jax
import jax.numpy as jnp
from jax import lax
from jax.experimental import pallas as pl
from jax.experimental.pallas import tpu as pltpu
from jax.sharding import PartitionSpec as P

NEG = -1e30
CAP = 2
LOG2E = math.log2(math.e)
LANES = 128


def attend_kernel(
    dims, own_ref, table_ref, left_ref, slots_ref, counts_ref, q_ref, kpool_ref, vpool_ref,
    kfresh_ref, vfresh_ref, out_ref, lse_ref, kb, vb, kf, vf, acc_s, top_s, tot_s, sem,
):
    (n_req, n_ctx, req_dev, heads, group, page, slots, pages_dev, split, chunk_pages) = dims
    n_reqs = n_req * req_dev
    rows = n_ctx * heads * group
    block = heads * group
    page_rows = page * heads
    scale = LOG2E / math.sqrt(LANES)

    def copy(index, source, target, half):
        where = source.at[:, :, :, pl.ds(half * LANES, LANES)] if split else source
        return pltpu.make_async_copy(where, target, sem.at[index])

    copies = [
        copy(0, kfresh_ref, kf, 0), copy(1, vfresh_ref, vf, 1),
        copy(2, kpool_ref, kb, 0), copy(3, vpool_ref, vb, 1),
    ]
    for one in copies:
        one.start()

    def page_of(ref, index):
        return ref[index].reshape(page_rows, LANES)

    def query_of(request):
        return q_ref[request]

    def scores_of(request, keys, limit, per):
        s = lax.dot_general(
            query_of(request), keys, (((1,), (1,)), ((), ())), preferred_element_type=jnp.float32
        )
        row = lax.broadcasted_iota(jnp.int32, s.shape, 0)
        col = lax.broadcasted_iota(jnp.int32, s.shape, 1)
        keep = ((row // group) % heads == col % heads) & (col < limit * per)
        return jnp.where(keep, s * scale, NEG)

    def fold(state, s, values):
        top, tot, acc = state
        new_top = jnp.maximum(top, jnp.max(s, axis=1, keepdims=True))
        p = jnp.exp2(s - new_top)
        fade = jnp.exp2(top - new_top)
        tot = tot * fade + jnp.sum(p, axis=1, keepdims=True)
        acc = acc * fade + jnp.dot(
            p.astype(jnp.bfloat16), values, preferred_element_type=jnp.float32
        )
        return new_top, tot, acc

    start = (
        jnp.full((rows, 1), NEG, jnp.float32),
        jnp.zeros((rows, 1), jnp.float32),
        jnp.zeros((rows, LANES), jnp.float32),
    )

    copies[0].wait()
    copies[1].wait()

    def fresh_step(request, _):
        places = [slots_ref[request * slots + n] for n in range(slots)]
        keys = jnp.concatenate([page_of(kf, n) for n in places], axis=0)
        values = jnp.concatenate([page_of(vf, n) for n in places], axis=0)
        s = scores_of(request, keys, counts_ref[request], page_rows)
        top, tot, acc = fold(start, s, values)
        acc_s[request] = acc
        top_s[request] = jnp.broadcast_to(top, (rows, LANES))
        tot_s[request] = jnp.broadcast_to(tot, (rows, LANES))
        return 0

    lax.fori_loop(0, n_reqs, fresh_step, 0)

    copies[2].wait()
    copies[3].wait()

    def resident_step(i, _):
        request = own_ref[0] * req_dev + i

        def chunk_step(chunk, state):
            first = chunk * chunk_pages
            places = [table_ref[i * pages_dev + first + n] for n in range(chunk_pages)]
            keys = jnp.concatenate([page_of(kb, n) for n in places], axis=0)
            values = jnp.concatenate([page_of(vb, n) for n in places], axis=0)
            s = scores_of(request, keys, left_ref[i] - first * page, heads)
            return fold(state, s, values)

        state = (top_s[request][:, :1], tot_s[request][:, :1], acc_s[request])
        top, tot, acc = lax.fori_loop(0, pages_dev // chunk_pages, chunk_step, state)
        acc_s[request] = acc
        top_s[request] = jnp.broadcast_to(top, (rows, LANES))
        tot_s[request] = jnp.broadcast_to(tot, (rows, LANES))
        return 0

    lax.fori_loop(0, req_dev, resident_step, 0)

    lane = lax.broadcasted_iota(jnp.int32, (rows, LANES), 1)
    lse = jnp.zeros((rows, LANES), jnp.float32)
    for request in range(n_reqs):
        tot = tot_s[request]
        out_ref[request] = (acc_s[request] / tot).astype(jnp.bfloat16)
        lse = jnp.where(lane == request, top_s[request] + jnp.log2(tot), lse)
    lse_ref[...] = lse


def merge_kernel(dims, own_ref, got_ref, lse_ref, out_ref, w_s):
    n_src, req_dev, block, n_ctx = dims
    base = pl.multiple_of(own_ref[0] * block, block)
    lse = lse_ref[...]
    top = jnp.max(lse, axis=0, keepdims=True)
    w = jnp.exp2(lse - top)
    w = w / jnp.sum(w, axis=0, keepdims=True)
    for i in range(req_dev):
        total = jnp.zeros((block, LANES), jnp.float32)
        for s in range(n_src):
            total += w[s, i * block:(i + 1) * block, :] * got_ref[s, i * block:(i + 1) * block, :].astype(jnp.float32)
        out_ref[i] = total.astype(jnp.bfloat16)


def local(query, kv_pool, page_table, context_len, fresh_kv, fresh_bucket):
    n_ctx = lax.axis_size("ctx")
    n_req = lax.axis_size("req")
    ctx_place = lax.axis_index("ctx")
    req_place = lax.axis_index("req")
    req_dev, heads, group, head_dim = query.shape
    pool_slots, page = kv_pool.shape[:2]
    new_dev = fresh_kv.shape[0]
    pages_dev = page_table.shape[1]
    n_reqs = n_req * req_dev
    slots = CAP * n_ctx
    rows = n_ctx * heads * group
    block = heads * group
    n_src = n_req * n_ctx

    gathered = lax.all_gather(query, ("req", "ctx"))
    q_all = gathered.reshape(n_req, n_ctx, req_dev, block, head_dim)
    q_all = q_all.transpose(0, 2, 1, 3, 4).reshape(n_reqs, rows, head_dim)

    left = context_len - ctx_place * (pages_dev * page)
    request = fresh_bucket // n_ctx
    order = jnp.arange(new_dev, dtype=jnp.int32)
    same = (request[:, None] == request[None, :]) & (order[None, :] < order[:, None])
    place = request * slots + jnp.sum(same.astype(jnp.int32), axis=1)
    spots = jnp.arange(n_reqs * slots, dtype=jnp.int32)
    slot_table = jnp.sum(jnp.where(place[None, :] == spots[:, None], order[None, :], 0), axis=1)
    counts = jnp.sum((request[None, :] == jnp.arange(n_reqs)[:, None]).astype(jnp.int32), axis=1)

    split = heads % 4 == 0
    if split:
        pools = (kv_pool, kv_pool, fresh_kv, fresh_kv)
        shape = (page, heads, LANES)
    else:
        pools = tuple(
            a[..., h * LANES:(h + 1) * LANES].reshape(a.shape[0], page * heads, LANES)
            for a in (kv_pool, fresh_kv) for h in (0, 1)
        )
        shape = (page * heads, LANES)
    dims = (n_req, n_ctx, req_dev, heads, group, page, slots, pages_dev, split, 16)
    smem = pl.BlockSpec(memory_space=pltpu.SMEM)
    vmem = pl.BlockSpec(memory_space=pltpu.VMEM)
    hbm = pl.BlockSpec(memory_space=pl.ANY)
    out, lse = pl.pallas_call(
        functools.partial(attend_kernel, dims),
        out_shape=(
            jax.ShapeDtypeStruct((n_reqs, rows, LANES), jnp.bfloat16),
            jax.ShapeDtypeStruct((rows, LANES), jnp.float32),
        ),
        in_specs=[smem] * 5 + [vmem] + [hbm] * 4,
        out_specs=(vmem, vmem),
        scratch_shapes=[
            pltpu.VMEM((pool_slots,) + shape, jnp.bfloat16),
            pltpu.VMEM((pool_slots,) + shape, jnp.bfloat16),
            pltpu.VMEM((new_dev,) + shape, jnp.bfloat16),
            pltpu.VMEM((new_dev,) + shape, jnp.bfloat16),
            pltpu.VMEM((n_reqs, rows, LANES), jnp.float32),
            pltpu.VMEM((n_reqs, rows, LANES), jnp.float32),
            pltpu.VMEM((n_reqs, rows, LANES), jnp.float32),
            pltpu.SemaphoreType.DMA((4,)),
        ],
        compiler_params=pltpu.CompilerParams(vmem_limit_bytes=48 * 2**20),
        name="attend",
    )(
        req_place.astype(jnp.int32).reshape(1), page_table.reshape(-1), left, slot_table, counts,
        q_all, *pools,
    )
    sends = out.reshape(n_req, req_dev, n_ctx, block, LANES).transpose(0, 2, 1, 3, 4)
    sends = sends.reshape(n_src, req_dev * block, LANES)
    lse = lse[:, :n_reqs].T.reshape(n_req, req_dev, n_ctx, block).transpose(0, 2, 1, 3)
    lse = lse.reshape(n_src, req_dev * block)
    got = lax.all_to_all(sends, ("req", "ctx"), split_axis=0, concat_axis=0, tiled=True)
    got_lse = lax.all_to_all(lse, ("req", "ctx"), split_axis=0, concat_axis=0, tiled=True)
    top = jnp.max(got_lse, axis=0)
    w = jnp.exp2(got_lse - top)
    w = w / jnp.sum(w, axis=0)
    merged = jnp.sum(got.astype(jnp.float32) * w[:, :, None], axis=0)
    return merged.astype(jnp.bfloat16).reshape(req_dev, heads, group, head_dim)


def solution(mesh):
    placed = (
        P("req", "kvh", "ctx", None),
        P(("req", "ctx"), None, "kvh", None),
        P("req", "ctx"),
        P("req"),
        P(("req", "ctx"), None, "kvh", None),
        P(("req", "ctx")),
    )
    return jax.shard_map(
        local, mesh=mesh, in_specs=placed, out_specs=P("req", "kvh", "ctx", None), check_vma=False
    )
```

```python
import functools
import math

import jax
import jax.numpy as jnp
from jax import lax
from jax.experimental import pallas as pl
from jax.experimental.pallas import tpu as pltpu
from jax.sharding import PartitionSpec as P

NEG = -1e30
CAP = 2
LANES = 128
SCALE = math.log2(math.e) / math.sqrt(LANES)
WIDE = 1024
VMEM = pl.BlockSpec(memory_space=pltpu.VMEM)
SMEM = pl.BlockSpec(memory_space=pltpu.SMEM)
HBM = pl.BlockSpec(memory_space=pl.ANY)


def shift(value, axis, steps):
    count = lax.axis_size(axis)
    pairs = [(source, (source + steps) % count) for source in range(count)]
    return lax.ppermute(value, axis, pairs)


def stage_kernel(pieces, pool_ref, fresh_ref, kb, vb, kf, vf, sem):
    each = pool_ref.shape[0] // pieces
    copies = []
    for half, (pool_to, fresh_to) in enumerate(((kb, kf), (vb, vf))):
        lanes = pl.ds(half * LANES, LANES)
        copies.append(pltpu.make_async_copy(
            fresh_ref.at[:, :, :, lanes], fresh_to, sem.at[len(copies)]))
        for n in range(pieces):
            some = pl.ds(n * each, each)
            copies.append(pltpu.make_async_copy(
                pool_ref.at[some, :, :, lanes], pool_to.at[some], sem.at[len(copies)]))
    for one in copies:
        one.start()
    for one in copies:
        one.wait()


def tools(heads, page_rows):
    def page_of(ref, index):
        return ref[index].reshape(page_rows, LANES)

    def class_reduce(x, op):
        step = heads
        while step < LANES:
            x = op(x, pltpu.roll(x, step, 1))
            step *= 2
        return x

    def scores(q, keys, sub, lane, limit, first):
        s = lax.dot_general(q, keys, (((1,), (1,)), ((), ())), preferred_element_type=jnp.float32)
        out = []
        for j in range(s.shape[1] // LANES):
            part = s[:, j * LANES:(j + 1) * LANES]
            one = part[:sub]
            for h in range(1, heads):
                one = jnp.where(lane % heads == h, part[h * sub:(h + 1) * sub], one)
            one = jnp.where(lane < limit - (first + j * LANES), one * SCALE, NEG)
            out.append(one)
        return out

    def spread(p, onehots):
        p = p.astype(jnp.bfloat16)
        return jnp.concatenate([p * one for one in onehots], axis=0)

    def rows_of(x, h):
        return jnp.broadcast_to(x[:, h:h + 1], x.shape)

    return page_of, class_reduce, scores, spread, rows_of


def fold_max(parts):
    top = parts[0]
    for part in parts[1:]:
        top = jnp.maximum(top, part)
    return top


def resident_kernel(
    dims, table_ref, left_ref, q_ref, kb, vb, acc_ref, top_ref, tot_ref, t_s,
):
    heads, page_rows, pages_dev, sub = dims
    page_of, class_reduce, scores, spread, rows_of = tools(heads, page_rows)
    columns = pages_dev * page_rows
    wide = min(WIDE, columns)
    per = wide // page_rows
    lane = lax.broadcasted_iota(jnp.int32, (sub, LANES), 1)
    onehots = [(lane % heads == h).astype(jnp.bfloat16) for h in range(heads)]

    def step(i, _):
        q = q_ref[i]
        limit = left_ref[i] * heads
        base = i * pages_dev
        top = jnp.full((sub, LANES), NEG, jnp.float32)
        for c in range(columns // wide):
            keys = jnp.concatenate(
                [page_of(kb, table_ref[base + c * per + n]) for n in range(per)], axis=0)
            parts = scores(q, keys, sub, lane, limit, c * wide)
            for j, part in enumerate(parts):
                t_s[:, c * wide + j * LANES:c * wide + (j + 1) * LANES] = part
            top = jnp.maximum(top, fold_max(parts))
        top = class_reduce(top, jnp.maximum)
        tot = jnp.zeros((sub, LANES), jnp.float32)
        acc = jnp.zeros((heads * sub, LANES), jnp.float32)
        for c in range(columns // wide):
            weights = []
            for j in range(wide // LANES):
                at = c * wide + j * LANES
                p = jnp.exp2(t_s[:, at:at + LANES] - top)
                tot = tot + p
                weights.append(spread(p, onehots))
            values = jnp.concatenate(
                [page_of(vb, table_ref[base + c * per + n]) for n in range(per)], axis=0)
            acc = acc + jnp.dot(
                jnp.concatenate(weights, axis=1), values, preferred_element_type=jnp.float32)
        acc_ref[i] = acc
        top_ref[i] = top
        tot_ref[i] = class_reduce(tot, jnp.add)
        return 0

    lax.fori_loop(0, q_ref.shape[0], step, 0)


def fresh_kernel(
    dims, own_ref, slots_ref, counts_ref, qown_ref, qfar_ref, kf, vf, acc_ref, top_ref, tot_ref,
    out_ref,
):
    heads, page_rows, slots, sub, n_req, req_dev = dims
    page_of, class_reduce, scores, spread, rows_of = tools(heads, page_rows)
    lane = lax.broadcasted_iota(jnp.int32, (sub, LANES), 1)
    onehots = [(lane % heads == h).astype(jnp.bfloat16) for h in range(heads)]
    n_reqs = n_req * req_dev
    unit = 4 * heads
    fill = LANES // unit
    kind = (lane % unit) // heads
    slabs = [jnp.zeros((sub, LANES), jnp.float32) for _ in range(-(-n_reqs // fill))]
    for k in range(n_req):
        place = lax.rem(own_ref[0] + k, n_req)
        for i in range(req_dev):
            n = k * req_dev + i
            request = place * req_dev + i
            q = qown_ref[i] if k == 0 else qfar_ref[n - req_dev]
            spots = [slots_ref[request * slots + m] for m in range(slots)]
            keys = jnp.concatenate([page_of(kf, m) for m in spots], axis=0)
            values = jnp.concatenate([page_of(vf, m) for m in spots], axis=0)
            parts = scores(q, keys, sub, lane, counts_ref[request] * page_rows, 0)
            top = class_reduce(fold_max(parts), jnp.maximum)
            if k == 0:
                top = jnp.maximum(top, top_ref[i])
            weights = []
            tot = jnp.zeros((sub, LANES), jnp.float32)
            for part in parts:
                p = jnp.exp2(part - top)
                tot = tot + p
                weights.append(spread(p, onehots))
            tot = class_reduce(tot, jnp.add)
            acc = jnp.dot(
                jnp.concatenate(weights, axis=1), values, preferred_element_type=jnp.float32)
            if k == 0:
                fade = jnp.exp2(top_ref[i] - top)
                tot = tot + fade * tot_ref[i]
            whole = 1.0 / tot
            for h in range(heads):
                some = acc[h * sub:(h + 1) * sub]
                if k == 0:
                    some = some + acc_ref[i, h * sub:(h + 1) * sub, :] * rows_of(fade, h)
                out_ref[n * heads + h] = (some * rows_of(whole, h)).astype(jnp.bfloat16)
            lse = top + jnp.log2(tot)
            slab = n // fill
            slabs[slab] = jnp.where(lane // unit == n % fill, lse, slabs[slab])
    for n, lse in enumerate(slabs):
        out_ref[n_reqs * heads + n] = pieces_of(lse, kind)


def pieces_of(lse, kind):
    high = lse.astype(jnp.bfloat16)
    rest = lse - high.astype(jnp.float32)
    mid = rest.astype(jnp.bfloat16)
    low = (rest - mid.astype(jnp.float32)).astype(jnp.bfloat16)
    both = jnp.where(kind == 1, mid.astype(jnp.float32), low.astype(jnp.float32))
    return jnp.where(kind == 0, high.astype(jnp.float32), both).astype(jnp.bfloat16)


def whole_of(pieces, heads):
    x = pieces.astype(jnp.float32)
    return x + pltpu.roll(x, LANES - heads, 1) + pltpu.roll(x, LANES - 2 * heads, 1)


def merge_lse(refs, slab, heads):
    lses = [whole_of(ref[slab], heads) for ref in refs]
    top = fold_max(lses)
    shares = [jnp.exp2(lse - top) for lse in lses]
    tot = sum(shares)
    return [share / tot for share in shares], top + jnp.log2(tot)


def ctx_merge_kernel(dims, *refs):
    heads, n_req, req_dev = dims
    refs, out_ref = refs[:-1], refs[-1]
    n_reqs = n_req * req_dev
    unit = 4 * heads
    fill = LANES // unit
    group = out_ref.shape[2]
    lane = lax.broadcasted_iota(jnp.int32, (group, LANES), 1)
    spread_lse = []
    for slab in range(-(-n_reqs // fill)):
        shares, lse = merge_lse(refs, n_reqs * heads + slab, heads)
        kind = (lane % unit) // heads
        same = lse
        for m in (1, 2):
            same = jnp.where(kind == m, pltpu.roll(lse, m * heads, 1), same)
        spread_lse.append(pieces_of(same, kind))
        for n in range(slab * fill, min(n_reqs, (slab + 1) * fill)):
            for h in range(heads):
                at = (n % fill) * unit + h
                total = 0.0
                for ref, share in zip(refs, shares):
                    total = total + ref[n * heads + h].astype(jnp.float32) * jnp.broadcast_to(
                        share[:, at:at + 1], (group, LANES))
                out_ref[n // req_dev, (n % req_dev) * heads + h] = total.astype(jnp.bfloat16)
    for k in range(n_req):
        slab = spread_lse[k * req_dev // fill].astype(jnp.float32)
        at = (k * req_dev) % fill * unit
        if at:
            slab = pltpu.roll(slab, LANES - at, 1)
        out_ref[k, req_dev * heads] = slab.astype(jnp.bfloat16)


def req_merge_kernel(dims, *refs):
    heads, req_dev = dims
    refs, out_ref = refs[:-1], refs[-1]
    group = out_ref.shape[2]
    shares, _ = merge_lse(refs, req_dev * heads, heads)
    for i in range(req_dev):
        for h in range(heads):
            at = i * 4 * heads + h
            total = 0.0
            for ref, share in zip(refs, shares):
                total = total + ref[i * heads + h].astype(jnp.float32) * jnp.broadcast_to(
                    share[:, at:at + 1], (group, LANES))
            out_ref[i, h] = total.astype(jnp.bfloat16)


def params(mib):
    return pltpu.CompilerParams(vmem_limit_bytes=mib * 2**20)


def local(query, kv_pool, page_table, context_len, fresh_kv, fresh_bucket):
    n_ctx = lax.axis_size("ctx")
    n_req = lax.axis_size("req")
    ctx_place = lax.axis_index("ctx")
    req_place = lax.axis_index("req")
    req_dev, heads, group, head_dim = query.shape
    pool_slots, page = kv_pool.shape[:2]
    new_dev = fresh_kv.shape[0]
    pages_dev = page_table.shape[1]
    n_reqs = n_req * req_dev
    slots = CAP * n_ctx
    sub = n_ctx * group
    rows = heads * sub
    page_rows = page * heads

    near = [query] + [shift(query, "ctx", -k) for k in range(1, n_ctx)]
    ahead = jnp.stack([shift(query, "req", -k) for k in range(1, n_req)])

    if heads % 4 == 0:
        pieces = 8
        half = lambda count: jax.ShapeDtypeStruct((count, page, heads, LANES), jnp.bfloat16)
        kb, vb, kf, vf = pl.pallas_call(
            functools.partial(stage_kernel, pieces),
            out_shape=(half(pool_slots), half(pool_slots), half(new_dev), half(new_dev)),
            in_specs=[HBM, HBM],
            out_specs=(VMEM,) * 4,
            scratch_shapes=[pltpu.SemaphoreType.DMA((2 * pieces + 2,))],
            compiler_params=params(2),
            cost_estimate=pl.CostEstimate(
                flops=0, transcendentals=0, bytes_accessed=2 * (kv_pool.size + fresh_kv.size)),
            name="stage",
        )(kv_pool, fresh_kv)
    else:
        kb, vb, kf, vf = (
            a[..., h * LANES:(h + 1) * LANES].reshape(a.shape[0], page_rows, LANES)
            for a in (kv_pool, fresh_kv) for h in (0, 1)
        )

    far = [ahead] + [shift(ahead, "ctx", -k) for k in range(1, n_ctx)]
    q_own = jnp.stack(near).transpose(1, 2, 0, 3, 4).reshape(req_dev, rows, head_dim)
    q_far = jnp.stack(far).transpose(1, 2, 3, 0, 4, 5).reshape(n_reqs - req_dev, rows, head_dim)

    left = context_len - ctx_place * (pages_dev * page)
    request = fresh_bucket // n_ctx
    order = jnp.arange(new_dev, dtype=jnp.int32)
    same = (request[:, None] == request[None, :]) & (order[None, :] < order[:, None])
    place = request * slots + jnp.sum(same.astype(jnp.int32), axis=1)
    spots = jnp.arange(n_reqs * slots, dtype=jnp.int32)
    slot_table = jnp.sum(jnp.where(place[None, :] == spots[:, None], order[None, :], 0), axis=1)
    counts = jnp.sum((request[None, :] == jnp.arange(n_reqs)[:, None]).astype(jnp.int32), axis=1)

    f32 = lambda *shape: jax.ShapeDtypeStruct(shape, jnp.float32)
    bf16 = lambda *shape: jax.ShapeDtypeStruct(shape, jnp.bfloat16)
    columns = pages_dev * page_rows
    acc, top, tot = pl.pallas_call(
        functools.partial(resident_kernel, (heads, page_rows, pages_dev, sub)),
        out_shape=(
            f32(req_dev, rows, LANES), f32(req_dev, sub, LANES), f32(req_dev, sub, LANES)),
        in_specs=[SMEM] * 2 + [VMEM] * 3,
        out_specs=(VMEM,) * 3,
        scratch_shapes=[pltpu.VMEM((sub, columns), jnp.float32)],
        compiler_params=params(8),
        cost_estimate=pl.CostEstimate(
            flops=4 * req_dev * rows * columns * LANES, transcendentals=req_dev * sub * columns,
            bytes_accessed=2 * kv_pool.size),
        name="resident",
    )(page_table.reshape(-1), left, q_own, kb, vb)

    fill = LANES // (4 * heads)
    slabs = n_reqs * heads + -(-n_reqs // fill)
    parts = pl.pallas_call(
        functools.partial(fresh_kernel, (heads, page_rows, slots, sub, n_req, req_dev)),
        out_shape=bf16(slabs, sub, LANES),
        in_specs=[SMEM] * 3 + [VMEM] * 7,
        out_specs=VMEM,
        compiler_params=params(8),
        cost_estimate=pl.CostEstimate(
            flops=4 * n_reqs * rows * slots * page_rows * LANES,
            transcendentals=n_reqs * sub * slots * page_rows, bytes_accessed=2 * fresh_kv.size),
        name="fresh",
    )(
        req_place.astype(jnp.int32).reshape(1), slot_table, counts, q_own, q_far, kf, vf,
        acc, top, tot,
    )
    sends = parts.reshape(slabs, n_ctx, group, LANES).transpose(1, 0, 2, 3)
    got = [sends[0]] + [shift(sends[k], "ctx", k) for k in range(1, n_ctx)]
    merged = pl.pallas_call(
        functools.partial(ctx_merge_kernel, (heads, n_req, req_dev)),
        out_shape=bf16(n_req, req_dev * heads + 1, group, LANES),
        in_specs=[VMEM] * n_ctx,
        out_specs=VMEM,
        compiler_params=params(8),
        name="ctx_merge",
    )(*got)
    got = [merged[0]] + [shift(merged[k], "req", k) for k in range(1, n_req)]
    return pl.pallas_call(
        functools.partial(req_merge_kernel, (heads, req_dev)),
        out_shape=bf16(req_dev, heads, group, LANES),
        in_specs=[VMEM] * n_req,
        out_specs=VMEM,
        compiler_params=params(8),
        name="req_merge",
    )(*got)


def solution(mesh):
    placed = (
        P("req", "kvh", "ctx", None),
        P(("req", "ctx"), None, "kvh", None),
        P("req", "ctx"),
        P("req"),
        P(("req", "ctx"), None, "kvh", None),
        P(("req", "ctx")),
    )
    return jax.shard_map(
        local, mesh=mesh, in_specs=placed, out_specs=P("req", "kvh", "ctx", None), check_vma=False
    )
```

```python
import functools
import math

import jax
import jax.numpy as jnp
from jax import lax
from jax.experimental import pallas as pl
from jax.experimental.pallas import tpu as pltpu
from jax.sharding import PartitionSpec as P

NEG = -1e30
CAP = 2
LANES = 128
SCALE = math.log2(math.e) / math.sqrt(LANES)
WIDE = 1024
VMEM = pl.BlockSpec(memory_space=pltpu.VMEM)
SMEM = pl.BlockSpec(memory_space=pltpu.SMEM)
HBM = pl.BlockSpec(memory_space=pltpu.HBM)


def stage_kernel(
    pieces, n_ctx, slots, bucket_ref, pool_ref, fresh_ref, kb, vb, kf, vf, slots_ref, counts_ref,
    sem,
):
    each = pool_ref.shape[0] // pieces
    copies = []
    for half, (pool_to, fresh_to) in enumerate(((kb, kf), (vb, vf))):
        lanes = pl.ds(half * LANES, LANES)
        copies.append(pltpu.make_async_copy(
            fresh_ref.at[:, :, :, lanes], fresh_to, sem.at[len(copies)]))
        for n in range(pieces):
            some = pl.ds(n * each, each)
            copies.append(pltpu.make_async_copy(
                pool_ref.at[some, :, :, lanes], pool_to.at[some], sem.at[len(copies)]))
    for one in copies:
        one.start()
    list_fresh(n_ctx, slots, bucket_ref, slots_ref, counts_ref)
    for one in copies:
        one.wait()


def list_kernel(n_ctx, slots, bucket_ref, slots_ref, counts_ref):
    list_fresh(n_ctx, slots, bucket_ref, slots_ref, counts_ref)


def list_fresh(n_ctx, slots, bucket_ref, slots_ref, counts_ref):
    for n in range(counts_ref.shape[0]):
        counts_ref[n] = 0
    for n in range(slots_ref.shape[0]):
        slots_ref[n] = 0

    def put(page, _):
        request = bucket_ref[page] // n_ctx
        count = counts_ref[request]
        slots_ref[request * slots + count] = page
        counts_ref[request] = count + 1
        return 0

    lax.fori_loop(0, bucket_ref.shape[0], put, 0)


def class_reduce(x, op, heads):
    step = heads
    while step < LANES:
        x = op(x, pltpu.roll(x, step, 1))
        step *= 2
    return x


def pages_of(ref, table_ref, first, count):
    return jnp.concatenate([ref[table_ref[first + n]] for n in range(count)], axis=0)


def score_parts(q, keys, lane, limit, first, heads, sub):
    s = lax.dot_general(q, keys, (((1,), (1,)), ((), ())), preferred_element_type=jnp.float32)
    out = []
    for j in range(s.shape[1] // LANES):
        part = s[:, j * LANES:(j + 1) * LANES]
        one = part[:sub]
        for h in range(1, heads):
            one = jnp.where(lane % heads == h, part[h * sub:(h + 1) * sub], one)
        out.append(jnp.where(lane < limit - (first + j * LANES), one * SCALE, NEG))
    return out


def spread(p, onehots):
    p = p.astype(jnp.bfloat16)
    return jnp.concatenate([p * one for one in onehots], axis=0)


def rows_of(x, h):
    return jnp.broadcast_to(x[:, h:h + 1], x.shape)


def fold_max(parts):
    top = parts[0]
    for part in parts[1:]:
        top = jnp.maximum(top, part)
    return top


def resident_kernel(
    dims, table_ref, left_ref, q_ref, kb, vb, acc_ref, top_ref, tot_ref, t_s,
):
    heads, page_rows, pages_dev, sub = dims
    columns = pages_dev * page_rows
    wide = min(WIDE, columns)
    per = wide // page_rows
    chunks = columns // wide
    count = q_ref.shape[0]
    lane = lax.broadcasted_iota(jnp.int32, (sub, LANES), 1)
    onehots = [(lane % heads == h).astype(jnp.bfloat16) for h in range(heads)]

    def score_chunk(i, c, top):
        keys = pages_of(kb, table_ref, i * pages_dev + c * per, per)
        parts = score_parts(q_ref[i], keys, lane, left_ref[i] * heads, c * wide, heads, sub)
        for j, part in enumerate(parts):
            t_s[:, c * wide + j * LANES:c * wide + (j + 1) * LANES] = part
        return jnp.maximum(top, fold_max(parts))

    def value_chunk(i, c, top, tot, acc):
        weights = []
        for j in range(wide // LANES):
            at = c * wide + j * LANES
            p = jnp.exp2(t_s[:, at:at + LANES] - top)
            tot = tot + p
            weights.append(spread(p, onehots))
        values = pages_of(vb, table_ref, i * pages_dev + c * per, per)
        return tot, acc + jnp.dot(
            jnp.concatenate(weights, axis=1), values, preferred_element_type=jnp.float32)

    def finish(i, top, tot, acc):
        acc_ref[i] = acc
        top_ref[i] = top
        tot_ref[i] = class_reduce(tot, jnp.add, heads)

    low = jnp.full((sub, LANES), NEG, jnp.float32)
    none = jnp.zeros((sub, LANES), jnp.float32)
    empty = jnp.zeros((heads * sub, LANES), jnp.float32)

    def step(i, top):
        top = class_reduce(top, jnp.maximum, heads)
        later, tot, acc = low, none, empty
        for c in range(chunks):
            tot, acc = value_chunk(i, c, top, tot, acc)
            later = score_chunk(i + 1, c, later)
        finish(i, top, tot, acc)
        return later

    top = low
    for c in range(chunks):
        top = score_chunk(0, c, top)
    top = lax.fori_loop(0, count - 1, step, top)
    top = class_reduce(top, jnp.maximum, heads)
    tot, acc = none, empty
    for c in range(chunks):
        tot, acc = value_chunk(count - 1, c, top, tot, acc)
    finish(count - 1, top, tot, acc)


def fresh_kernel(
    dims, own_ref, slots_ref, counts_ref, q_ref, kf, vf, acc_ref, top_ref, tot_ref,
    out_ref, t_s, p_s,
):
    heads, page_rows, slots, sub, n_req, req_dev = dims
    lane = lax.broadcasted_iota(jnp.int32, (sub, LANES), 1)
    onehots = [(lane % heads == h).astype(jnp.bfloat16) for h in range(heads)]
    n_reqs = n_req * req_dev
    unit = 4 * heads
    fill = LANES // unit
    kind = (lane % unit) // heads
    columns = slots * page_rows
    requests = [
        lax.rem(own_ref[0] + k, n_req) * req_dev + i for k in range(n_req) for i in range(req_dev)
    ]
    tops = []
    for n, request in enumerate(requests):
        keys = pages_of(kf, slots_ref, request * slots, slots)
        parts = score_parts(
            q_ref[request], keys, lane, counts_ref[request] * page_rows, 0, heads, sub)
        for j, part in enumerate(parts):
            t_s[n, :, j * LANES:(j + 1) * LANES] = part
        tops.append(fold_max(parts))
    tops = class_reduce(jnp.concatenate(tops, axis=0), jnp.maximum, heads)
    tops = [tops[n * sub:(n + 1) * sub] for n in range(n_reqs)]
    for i in range(req_dev):
        tops[i] = jnp.maximum(tops[i], top_ref[i])
    tots = []
    for n in range(n_reqs):
        tot = jnp.zeros((sub, LANES), jnp.float32)
        for j in range(columns // LANES):
            p = jnp.exp2(t_s[n, :, j * LANES:(j + 1) * LANES] - tops[n])
            tot = tot + p
            p_s[n, :, j * LANES:(j + 1) * LANES] = spread(p, onehots)
        tots.append(tot)
    tots = class_reduce(jnp.concatenate(tots, axis=0), jnp.add, heads)
    tots = [tots[n * sub:(n + 1) * sub] for n in range(n_reqs)]
    fades = [jnp.exp2(top_ref[i] - tops[i]) for i in range(req_dev)]
    for i in range(req_dev):
        tots[i] = tots[i] + fades[i] * tot_ref[i]
    slabs = [jnp.zeros((sub, LANES), jnp.float32) for _ in range(-(-n_reqs // fill))]
    for n, request in enumerate(requests):
        values = pages_of(vf, slots_ref, request * slots, slots)
        acc = jnp.dot(p_s[n], values, preferred_element_type=jnp.float32)
        whole = 1.0 / tots[n]
        for h in range(heads):
            some = acc[h * sub:(h + 1) * sub]
            if n < req_dev:
                some = some + acc_ref[n, h * sub:(h + 1) * sub, :] * rows_of(fades[n], h)
            out_ref[request * heads + h] = (some * rows_of(whole, h)).astype(jnp.bfloat16)
        lse = tops[n] + jnp.log2(tots[n])
        for m in range(len(slabs)):
            slabs[m] = jnp.where(lane // unit == request - m * fill, lse, slabs[m])
    for n, lse in enumerate(slabs):
        out_ref[n_reqs * heads + n] = pieces_of(lse, kind)


def pieces_of(lse, kind):
    high = lse.astype(jnp.bfloat16)
    rest = lse - high.astype(jnp.float32)
    mid = rest.astype(jnp.bfloat16)
    low = (rest - mid.astype(jnp.float32)).astype(jnp.bfloat16)
    both = jnp.where(kind == 1, mid.astype(jnp.float32), low.astype(jnp.float32))
    return jnp.where(kind == 0, high.astype(jnp.float32), both).astype(jnp.bfloat16)


def whole_of(pieces, heads):
    x = pieces.astype(jnp.float32)
    return x + pltpu.roll(x, LANES - heads, 1) + pltpu.roll(x, LANES - 2 * heads, 1)


def merge_lse(refs, slab, heads):
    lses = [whole_of(ref[slab], heads) for ref in refs]
    top = fold_max(lses)
    shares = [jnp.exp2(lse - top) for lse in lses]
    tot = sum(shares)
    return [share / tot for share in shares], top + jnp.log2(tot)


def ctx_merge_kernel(dims, got_ref, out_ref):
    heads, n_req, req_dev = dims
    refs = [got_ref.at[n] for n in range(got_ref.shape[0])]
    n_reqs = n_req * req_dev
    unit = 4 * heads
    fill = LANES // unit
    group = out_ref.shape[2]
    lane = lax.broadcasted_iota(jnp.int32, (group, LANES), 1)
    spread_lse = []
    for slab in range(-(-n_reqs // fill)):
        shares, lse = merge_lse(refs, n_reqs * heads + slab, heads)
        kind = (lane % unit) // heads
        same = lse
        for m in (1, 2):
            same = jnp.where(kind == m, pltpu.roll(lse, m * heads, 1), same)
        spread_lse.append(pieces_of(same, kind))
        for n in range(slab * fill, min(n_reqs, (slab + 1) * fill)):
            for h in range(heads):
                at = (n % fill) * unit + h
                total = 0.0
                for ref, share in zip(refs, shares):
                    total = total + ref[n * heads + h].astype(jnp.float32) * jnp.broadcast_to(
                        share[:, at:at + 1], (group, LANES))
                out_ref[n // req_dev, (n % req_dev) * heads + h] = total.astype(jnp.bfloat16)
    for k in range(n_req):
        slab = spread_lse[k * req_dev // fill].astype(jnp.float32)
        at = (k * req_dev) % fill * unit
        if at:
            slab = pltpu.roll(slab, LANES - at, 1)
        out_ref[k, req_dev * heads] = slab.astype(jnp.bfloat16)


def req_merge_kernel(dims, got_ref, out_ref):
    heads, req_dev = dims
    refs = [got_ref.at[n] for n in range(got_ref.shape[0])]
    group = out_ref.shape[2]
    shares, _ = merge_lse(refs, req_dev * heads, heads)
    for i in range(req_dev):
        for h in range(heads):
            at = i * 4 * heads + h
            total = 0.0
            for ref, share in zip(refs, shares):
                total = total + ref[i * heads + h].astype(jnp.float32) * jnp.broadcast_to(
                    share[:, at:at + 1], (group, LANES))
            out_ref[i, h] = total.astype(jnp.bfloat16)


def params(mib):
    return pltpu.CompilerParams(vmem_limit_bytes=mib * 2**20)


def local(query, kv_pool, page_table, context_len, fresh_kv, fresh_bucket):
    n_ctx = lax.axis_size("ctx")
    n_req = lax.axis_size("req")
    ctx_place = lax.axis_index("ctx")
    req_place = lax.axis_index("req")
    req_dev, heads, group, head_dim = query.shape
    pool_slots, page = kv_pool.shape[:2]
    new_dev = fresh_kv.shape[0]
    pages_dev = page_table.shape[1]
    n_reqs = n_req * req_dev
    slots = CAP * n_ctx
    sub = n_ctx * group
    rows = heads * sub
    page_rows = page * heads

    smem = lambda count: jax.ShapeDtypeStruct((count,), jnp.int32)
    near = lax.all_to_all(
        jnp.broadcast_to(query, (n_ctx,) + query.shape), "ctx", split_axis=0, concat_axis=0,
        tiled=True)
    if heads % 4 == 0:
        pieces = 8
        half = lambda count: jax.ShapeDtypeStruct((count, page, heads, LANES), jnp.bfloat16)
        kb, vb, kf, vf, slot_table, counts = pl.pallas_call(
            functools.partial(stage_kernel, pieces, n_ctx, slots),
            out_shape=(
                half(pool_slots), half(pool_slots), half(new_dev), half(new_dev),
                smem(n_reqs * slots), smem(n_reqs)),
            in_specs=[SMEM, HBM, HBM],
            out_specs=(VMEM,) * 4 + (SMEM,) * 2,
            scratch_shapes=[pltpu.SemaphoreType.DMA((2 * pieces + 2,))],
            compiler_params=params(2),
            cost_estimate=pl.CostEstimate(
                flops=0, transcendentals=0, bytes_accessed=2 * (kv_pool.size + fresh_kv.size)),
            name="stage",
        )(
            fresh_bucket, pltpu.with_memory_space_constraint(kv_pool, pltpu.HBM),
            pltpu.with_memory_space_constraint(fresh_kv, pltpu.HBM))
        kb, vb, kf, vf = (a.reshape(a.shape[0], page_rows, LANES) for a in (kb, vb, kf, vf))
    else:
        kb, vb, kf, vf = (
            a[..., h * LANES:(h + 1) * LANES].reshape(a.shape[0], page_rows, LANES)
            for a in (kv_pool, fresh_kv) for h in (0, 1)
        )
        slot_table, counts = pl.pallas_call(
            functools.partial(list_kernel, n_ctx, slots),
            out_shape=(smem(n_reqs * slots), smem(n_reqs)),
            in_specs=[SMEM],
            out_specs=(SMEM,) * 2,
            name="list",
        )(fresh_bucket)

    far = lax.all_to_all(
        jnp.broadcast_to(near, (n_req,) + near.shape), "req", split_axis=0, concat_axis=0,
        tiled=True)
    q_own = near.transpose(1, 2, 0, 3, 4).reshape(req_dev, rows, head_dim)
    q_all = far.transpose(0, 2, 3, 1, 4, 5).reshape(n_reqs, rows, head_dim)
    left = context_len - ctx_place * (pages_dev * page)

    f32 = lambda *shape: jax.ShapeDtypeStruct(shape, jnp.float32)
    bf16 = lambda *shape: jax.ShapeDtypeStruct(shape, jnp.bfloat16)
    columns = pages_dev * page_rows
    acc, top, tot = pl.pallas_call(
        functools.partial(resident_kernel, (heads, page_rows, pages_dev, sub)),
        out_shape=(
            f32(req_dev, rows, LANES), f32(req_dev, sub, LANES), f32(req_dev, sub, LANES)),
        in_specs=[SMEM] * 2 + [VMEM] * 3,
        out_specs=(VMEM,) * 3,
        scratch_shapes=[pltpu.VMEM((sub, columns), jnp.float32)],
        compiler_params=params(8),
        cost_estimate=pl.CostEstimate(
            flops=4 * req_dev * rows * columns * LANES, transcendentals=req_dev * sub * columns,
            bytes_accessed=2 * kv_pool.size),
        name="resident",
    )(page_table.reshape(-1), left, q_own, kb, vb)

    fill = LANES // (4 * heads)
    slabs = n_reqs * heads + -(-n_reqs // fill)
    parts = pl.pallas_call(
        functools.partial(fresh_kernel, (heads, page_rows, slots, sub, n_req, req_dev)),
        out_shape=bf16(slabs, sub, LANES),
        in_specs=[SMEM] * 3 + [VMEM] * 6,
        out_specs=VMEM,
        scratch_shapes=[
            pltpu.VMEM((n_reqs, sub, slots * page_rows), jnp.float32),
            pltpu.VMEM((n_reqs, rows, slots * page_rows), jnp.bfloat16),
        ],
        compiler_params=params(8),
        cost_estimate=pl.CostEstimate(
            flops=4 * n_reqs * rows * slots * page_rows * LANES,
            transcendentals=n_reqs * sub * slots * page_rows, bytes_accessed=2 * fresh_kv.size),
        name="fresh",
    )(
        req_place.astype(jnp.int32).reshape(1), slot_table, counts, q_all, kf, vf, acc, top, tot,
    )
    sends = parts.reshape(slabs, n_ctx, group, LANES).transpose(1, 0, 2, 3)
    got = lax.all_to_all(sends, "ctx", split_axis=0, concat_axis=0, tiled=True)
    merged = pl.pallas_call(
        functools.partial(ctx_merge_kernel, (heads, n_req, req_dev)),
        out_shape=bf16(n_req, req_dev * heads + 1, group, LANES),
        in_specs=[VMEM],
        out_specs=VMEM,
        compiler_params=params(8),
        name="ctx_merge",
    )(got)
    got = lax.all_to_all(merged, "req", split_axis=0, concat_axis=0, tiled=True)
    return pl.pallas_call(
        functools.partial(req_merge_kernel, (heads, req_dev)),
        out_shape=bf16(req_dev, heads, group, LANES),
        in_specs=[VMEM],
        out_specs=VMEM,
        compiler_params=params(8),
        name="req_merge",
    )(got)


def solution(mesh):
    placed = (
        P("req", "kvh", "ctx", None),
        P(("req", "ctx"), None, "kvh", None),
        P("req", "ctx"),
        P("req"),
        P(("req", "ctx"), None, "kvh", None),
        P(("req", "ctx")),
    )
    return jax.shard_map(
        local, mesh=mesh, in_specs=placed, out_specs=P("req", "kvh", "ctx", None), check_vma=False
    )
```

```python
import functools
import math

import jax
import jax.numpy as jnp
from jax import lax
from jax.experimental import pallas as pl
from jax.experimental.pallas import tpu as pltpu
from jax.sharding import PartitionSpec as P

NEG = -1e30
CAP = 2
LANES = 128
SCALE = math.log2(math.e) / math.sqrt(LANES)
WIDE = 1024
VMEM = pl.BlockSpec(memory_space=pltpu.VMEM)
SMEM = pl.BlockSpec(memory_space=pltpu.SMEM)
HBM = pl.BlockSpec(memory_space=pltpu.HBM)


def shift(value, axis, steps):
    count = lax.axis_size(axis)
    pairs = [(source, (source + steps) % count) for source in range(count)]
    return lax.ppermute(value, axis, pairs)


def stage_kernel(
    pieces, n_ctx, slots, bucket_ref, pool_ref, fresh_ref, kb, kf, vf, slots_ref, counts_ref, sem,
):
    copies = [
        pltpu.make_async_copy(fresh_ref.at[:, :, :, pl.ds(half * LANES, LANES)], to, sem.at[half])
        for half, to in enumerate((kf, vf))
    ] + half_copies(pool_ref, kb, sem, 2, 0, pieces)
    for one in copies:
        one.start()
    list_fresh(n_ctx, slots, bucket_ref, slots_ref, counts_ref)
    for one in copies:
        one.wait()


def half_copies(pool_ref, target, sem, first, half, pieces):
    each = pool_ref.shape[0] // pieces
    return [
        pltpu.make_async_copy(
            pool_ref.at[pl.ds(n * each, each), :, :, pl.ds(half * LANES, LANES)],
            target.at[pl.ds(n * each, each)], sem.at[first + n])
        for n in range(pieces)
    ]


def list_kernel(n_ctx, slots, bucket_ref, slots_ref, counts_ref):
    list_fresh(n_ctx, slots, bucket_ref, slots_ref, counts_ref)


def list_fresh(n_ctx, slots, bucket_ref, slots_ref, counts_ref):
    for n in range(counts_ref.shape[0]):
        counts_ref[n] = 0
    for n in range(slots_ref.shape[0]):
        slots_ref[n] = 0

    def put(page, _):
        request = bucket_ref[page] // n_ctx
        count = counts_ref[request]
        slots_ref[request * slots + count] = page
        counts_ref[request] = count + 1
        return 0

    lax.fori_loop(0, bucket_ref.shape[0], put, 0)


def class_reduce(x, op, heads):
    step = heads
    while step < LANES:
        x = op(x, pltpu.roll(x, step, 1))
        step *= 2
    return x


def pages_of(ref, table_ref, first, count):
    return jnp.concatenate([ref[table_ref[first + n]] for n in range(count)], axis=0)


def score_parts(q, keys, lane, limit, first, heads, sub):
    s = lax.dot_general(q, keys, (((1,), (1,)), ((), ())), preferred_element_type=jnp.float32)
    out = []
    for j in range(s.shape[1] // LANES):
        part = s[:, j * LANES:(j + 1) * LANES]
        one = part[:sub]
        for h in range(1, heads):
            one = jnp.where(lane % heads == h, part[h * sub:(h + 1) * sub], one)
        out.append(jnp.where(lane < limit - (first + j * LANES), one * SCALE, NEG))
    return out


def spread(p, onehots):
    p = p.astype(jnp.bfloat16)
    return jnp.concatenate([p * one for one in onehots], axis=0)


def rows_of(x, h):
    return jnp.broadcast_to(x[:, h:h + 1], x.shape)


def fold_max(parts):
    top = parts[0]
    for part in parts[1:]:
        top = jnp.maximum(top, part)
    return top


def resident_kernel(
    dims, table_ref, left_ref, q_ref, kb, pool_ref, acc_ref, top_ref, tot_ref, t_s, *held,
):
    heads, page_rows, pages_dev, sub, pieces = dims
    copies = []
    vb = pool_ref
    if held:
        copies = half_copies(pool_ref, held[0], held[1], 0, 1, pieces)
        vb = held[0].reshape(held[0].shape[0], page_rows, LANES)
    for one in copies:
        one.start()
    columns = pages_dev * page_rows
    wide = min(WIDE, columns)
    per = wide // page_rows
    chunks = columns // wide
    lane = lax.broadcasted_iota(jnp.int32, (sub, LANES), 1)
    onehots = [(lane % heads == h).astype(jnp.bfloat16) for h in range(heads)]

    def score_step(i, _):
        top = jnp.full((sub, LANES), NEG, jnp.float32)
        for c in range(chunks):
            keys = pages_of(kb, table_ref, i * pages_dev + c * per, per)
            parts = score_parts(q_ref[i], keys, lane, left_ref[i] * heads, c * wide, heads, sub)
            for j, part in enumerate(parts):
                t_s[i, :, c * wide + j * LANES:c * wide + (j + 1) * LANES] = part
            top = jnp.maximum(top, fold_max(parts))
        top_ref[i] = top
        return 0

    def value_step(i, _):
        tot = jnp.zeros((sub, LANES), jnp.float32)
        acc = jnp.zeros((heads * sub, LANES), jnp.float32)
        top = top_ref[i]
        for c in range(chunks):
            weights = []
            for j in range(wide // LANES):
                at = c * wide + j * LANES
                p = jnp.exp2(t_s[i, :, at:at + LANES] - top)
                tot = tot + p
                weights.append(spread(p, onehots))
            values = pages_of(vb, table_ref, i * pages_dev + c * per, per)
            acc = acc + jnp.dot(
                jnp.concatenate(weights, axis=1), values, preferred_element_type=jnp.float32)
        acc_ref[i] = acc
        tot_ref[i] = tot
        return 0

    shape = top_ref.shape
    flat = (shape[0] * shape[1], LANES)
    lax.fori_loop(0, shape[0], score_step, 0)
    top_ref[...] = class_reduce(top_ref[...].reshape(flat), jnp.maximum, heads).reshape(shape)
    for one in copies:
        one.wait()
    lax.fori_loop(0, shape[0], value_step, 0)
    tot_ref[...] = class_reduce(tot_ref[...].reshape(flat), jnp.add, heads).reshape(shape)


def fresh_kernel(
    dims, own_ref, slots_ref, counts_ref, qown_ref, qfar_ref, kf, vf, acc_ref, top_ref, tot_ref,
    out_ref, t_s, p_s,
):
    heads, page_rows, slots, sub, n_req, req_dev = dims
    lane = lax.broadcasted_iota(jnp.int32, (sub, LANES), 1)
    onehots = [(lane % heads == h).astype(jnp.bfloat16) for h in range(heads)]
    n_reqs = n_req * req_dev
    unit = 4 * heads
    fill = LANES // unit
    kind = (lane % unit) // heads
    columns = slots * page_rows
    requests = [
        lax.rem(own_ref[0] + k, n_req) * req_dev + i for k in range(n_req) for i in range(req_dev)
    ]
    tops = []
    for n, request in enumerate(requests):
        keys = pages_of(kf, slots_ref, request * slots, slots)
        q = qown_ref[n] if n < req_dev else qfar_ref[n - req_dev]
        parts = score_parts(q, keys, lane, counts_ref[request] * page_rows, 0, heads, sub)
        for j, part in enumerate(parts):
            t_s[n, :, j * LANES:(j + 1) * LANES] = part
        tops.append(fold_max(parts))
    tops = class_reduce(jnp.concatenate(tops, axis=0), jnp.maximum, heads)
    tops = [tops[n * sub:(n + 1) * sub] for n in range(n_reqs)]
    for i in range(req_dev):
        tops[i] = jnp.maximum(tops[i], top_ref[i])
    tots = []
    for n in range(n_reqs):
        tot = jnp.zeros((sub, LANES), jnp.float32)
        for j in range(columns // LANES):
            p = jnp.exp2(t_s[n, :, j * LANES:(j + 1) * LANES] - tops[n])
            tot = tot + p
            p_s[n, :, j * LANES:(j + 1) * LANES] = spread(p, onehots)
        tots.append(tot)
    tots = class_reduce(jnp.concatenate(tots, axis=0), jnp.add, heads)
    tots = [tots[n * sub:(n + 1) * sub] for n in range(n_reqs)]
    fades = [jnp.exp2(top_ref[i] - tops[i]) for i in range(req_dev)]
    for i in range(req_dev):
        tots[i] = tots[i] + fades[i] * tot_ref[i]
    slabs = [jnp.zeros((sub, LANES), jnp.float32) for _ in range(-(-n_reqs // fill))]
    for n, request in enumerate(requests):
        values = pages_of(vf, slots_ref, request * slots, slots)
        acc = jnp.dot(p_s[n], values, preferred_element_type=jnp.float32)
        whole = 1.0 / tots[n]
        for h in range(heads):
            some = acc[h * sub:(h + 1) * sub]
            if n < req_dev:
                some = some + acc_ref[n, h * sub:(h + 1) * sub, :] * rows_of(fades[n], h)
            out_ref[n * heads + h] = (some * rows_of(whole, h)).astype(jnp.bfloat16)
        lse = tops[n] + jnp.log2(tots[n])
        slabs[n // fill] = jnp.where(lane // unit == n % fill, lse, slabs[n // fill])
    for n, lse in enumerate(slabs):
        out_ref[n_reqs * heads + n] = pieces_of(lse, kind)


def pieces_of(lse, kind):
    high = lse.astype(jnp.bfloat16)
    rest = lse - high.astype(jnp.float32)
    mid = rest.astype(jnp.bfloat16)
    low = (rest - mid.astype(jnp.float32)).astype(jnp.bfloat16)
    both = jnp.where(kind == 1, mid.astype(jnp.float32), low.astype(jnp.float32))
    return jnp.where(kind == 0, high.astype(jnp.float32), both).astype(jnp.bfloat16)


def whole_of(pieces, heads):
    x = pieces.astype(jnp.float32)
    return x + pltpu.roll(x, LANES - heads, 1) + pltpu.roll(x, LANES - 2 * heads, 1)


def merge_lse(refs, slab, heads):
    lses = [whole_of(ref[slab], heads) for ref in refs]
    top = fold_max(lses)
    shares = [jnp.exp2(lse - top) for lse in lses]
    tot = sum(shares)
    return [share / tot for share in shares], top + jnp.log2(tot)


def ctx_merge_kernel(dims, *refs):
    heads, n_req, req_dev = dims
    refs, out_ref = refs[:-1], refs[-1]
    n_reqs = n_req * req_dev
    unit = 4 * heads
    fill = LANES // unit
    group = out_ref.shape[2]
    lane = lax.broadcasted_iota(jnp.int32, (group, LANES), 1)
    spread_lse = []
    for slab in range(-(-n_reqs // fill)):
        shares, lse = merge_lse(refs, n_reqs * heads + slab, heads)
        kind = (lane % unit) // heads
        same = lse
        for m in (1, 2):
            same = jnp.where(kind == m, pltpu.roll(lse, m * heads, 1), same)
        spread_lse.append(pieces_of(same, kind))
        for n in range(slab * fill, min(n_reqs, (slab + 1) * fill)):
            for h in range(heads):
                at = (n % fill) * unit + h
                total = 0.0
                for ref, share in zip(refs, shares):
                    total = total + ref[n * heads + h].astype(jnp.float32) * jnp.broadcast_to(
                        share[:, at:at + 1], (group, LANES))
                out_ref[n // req_dev, (n % req_dev) * heads + h] = total.astype(jnp.bfloat16)
    for k in range(n_req):
        slab = spread_lse[k * req_dev // fill].astype(jnp.float32)
        at = (k * req_dev) % fill * unit
        if at:
            slab = pltpu.roll(slab, LANES - at, 1)
        out_ref[k, req_dev * heads] = slab.astype(jnp.bfloat16)


def req_merge_kernel(dims, *refs):
    heads, req_dev = dims
    refs, out_ref = refs[:-1], refs[-1]
    group = out_ref.shape[2]
    shares, _ = merge_lse(refs, req_dev * heads, heads)
    for i in range(req_dev):
        for h in range(heads):
            at = i * 4 * heads + h
            total = 0.0
            for ref, share in zip(refs, shares):
                total = total + ref[i * heads + h].astype(jnp.float32) * jnp.broadcast_to(
                    share[:, at:at + 1], (group, LANES))
            out_ref[i, h] = total.astype(jnp.bfloat16)


def params(mib):
    return pltpu.CompilerParams(vmem_limit_bytes=mib * 2**20)


def local(query, kv_pool, page_table, context_len, fresh_kv, fresh_bucket):
    n_ctx = lax.axis_size("ctx")
    n_req = lax.axis_size("req")
    ctx_place = lax.axis_index("ctx")
    req_place = lax.axis_index("req")
    req_dev, heads, group, head_dim = query.shape
    pool_slots, page = kv_pool.shape[:2]
    new_dev = fresh_kv.shape[0]
    pages_dev = page_table.shape[1]
    n_reqs = n_req * req_dev
    slots = CAP * n_ctx
    sub = n_ctx * group
    rows = heads * sub
    page_rows = page * heads

    smem = lambda count: jax.ShapeDtypeStruct((count,), jnp.int32)
    near = jnp.stack([query] + [shift(query, "ctx", -k) for k in range(1, n_ctx)])
    if heads % 4 == 0:
        pieces = 8
        half = lambda count: jax.ShapeDtypeStruct((count, page, heads, LANES), jnp.bfloat16)
        pool = pltpu.with_memory_space_constraint(kv_pool, pltpu.HBM)
        kb, kf, vf, slot_table, counts = pl.pallas_call(
            functools.partial(stage_kernel, pieces, n_ctx, slots),
            out_shape=(
                half(pool_slots), half(new_dev), half(new_dev), smem(n_reqs * slots), smem(n_reqs)),
            in_specs=[SMEM, HBM, HBM],
            out_specs=(VMEM,) * 3 + (SMEM,) * 2,
            scratch_shapes=[pltpu.SemaphoreType.DMA((pieces + 2,))],
            compiler_params=params(2),
            cost_estimate=pl.CostEstimate(
                flops=0, transcendentals=0, bytes_accessed=2 * (kv_pool.size + fresh_kv.size)),
            name="stage",
        )(fresh_bucket, pool, pltpu.with_memory_space_constraint(fresh_kv, pltpu.HBM))
        kb, kf, vf = (a.reshape(a.shape[0], page_rows, LANES) for a in (kb, kf, vf))
        vb, held = pool, [
            pltpu.VMEM((pool_slots, page, heads, LANES), jnp.bfloat16),
            pltpu.SemaphoreType.DMA((pieces,)),
        ]
    else:
        kb, vb, kf, vf = (
            a[..., h * LANES:(h + 1) * LANES].reshape(a.shape[0], page_rows, LANES)
            for a in (kv_pool, fresh_kv) for h in (0, 1)
        )
        held = []
        slot_table, counts = pl.pallas_call(
            functools.partial(list_kernel, n_ctx, slots),
            out_shape=(smem(n_reqs * slots), smem(n_reqs)),
            in_specs=[SMEM],
            out_specs=(SMEM,) * 2,
            name="list",
        )(fresh_bucket)

    far = jnp.stack([shift(near, "req", -k) for k in range(1, n_req)])
    q_own = near.transpose(1, 2, 0, 3, 4).reshape(req_dev, rows, head_dim)
    q_far = far.transpose(0, 2, 3, 1, 4, 5).reshape(n_reqs - req_dev, rows, head_dim)
    left = context_len - ctx_place * (pages_dev * page)

    f32 = lambda *shape: jax.ShapeDtypeStruct(shape, jnp.float32)
    bf16 = lambda *shape: jax.ShapeDtypeStruct(shape, jnp.bfloat16)
    columns = pages_dev * page_rows
    acc, top, tot = pl.pallas_call(
        functools.partial(resident_kernel, (heads, page_rows, pages_dev, sub, 8)),
        out_shape=(
            f32(req_dev, rows, LANES), f32(req_dev, sub, LANES), f32(req_dev, sub, LANES)),
        in_specs=[SMEM] * 2 + [VMEM] * 2 + [HBM if held else VMEM],
        out_specs=(VMEM,) * 3,
        scratch_shapes=[pltpu.VMEM((req_dev, sub, columns), jnp.float32)] + held,
        compiler_params=params(14),
        cost_estimate=pl.CostEstimate(
            flops=4 * req_dev * rows * columns * LANES, transcendentals=req_dev * sub * columns,
            bytes_accessed=2 * kv_pool.size),
        name="resident",
    )(page_table.reshape(-1), left, q_own, kb, vb)

    fill = LANES // (4 * heads)
    slabs = n_reqs * heads + -(-n_reqs // fill)
    parts = pl.pallas_call(
        functools.partial(fresh_kernel, (heads, page_rows, slots, sub, n_req, req_dev)),
        out_shape=bf16(slabs, sub, LANES),
        in_specs=[SMEM] * 3 + [VMEM] * 7,
        out_specs=VMEM,
        scratch_shapes=[
            pltpu.VMEM((n_reqs, sub, slots * page_rows), jnp.float32),
            pltpu.VMEM((n_reqs, rows, slots * page_rows), jnp.bfloat16),
        ],
        compiler_params=params(8),
        cost_estimate=pl.CostEstimate(
            flops=4 * n_reqs * rows * slots * page_rows * LANES,
            transcendentals=n_reqs * sub * slots * page_rows, bytes_accessed=2 * fresh_kv.size),
        name="fresh",
    )(
        req_place.astype(jnp.int32).reshape(1), slot_table, counts, q_own, q_far, kf, vf, acc, top, tot,
    )
    sends = parts.reshape(slabs, n_ctx, group, LANES).transpose(1, 0, 2, 3)
    got = [sends[0]] + [shift(sends[k], "ctx", k) for k in range(1, n_ctx)]
    merged = pl.pallas_call(
        functools.partial(ctx_merge_kernel, (heads, n_req, req_dev)),
        out_shape=bf16(n_req, req_dev * heads + 1, group, LANES),
        in_specs=[VMEM] * n_ctx,
        out_specs=VMEM,
        compiler_params=params(8),
        name="ctx_merge",
    )(*got)
    got = [merged[0]] + [shift(merged[k], "req", k) for k in range(1, n_req)]
    return pl.pallas_call(
        functools.partial(req_merge_kernel, (heads, req_dev)),
        out_shape=bf16(req_dev, heads, group, LANES),
        in_specs=[VMEM] * n_req,
        out_specs=VMEM,
        compiler_params=params(8),
        name="req_merge",
    )(*got)


def solution(mesh):
    placed = (
        P("req", "kvh", "ctx", None),
        P(("req", "ctx"), None, "kvh", None),
        P("req", "ctx"),
        P("req"),
        P(("req", "ctx"), None, "kvh", None),
        P(("req", "ctx")),
    )
    return jax.shard_map(
        local, mesh=mesh, in_specs=placed, out_specs=P("req", "kvh", "ctx", None), check_vma=False
    )
```

```python
import functools
import math

import jax
import jax.numpy as jnp
from jax import lax
from jax.experimental import pallas as pl
from jax.experimental.pallas import tpu as pltpu
from jax.sharding import PartitionSpec as P

NEG = -1e30
CAP = 2
LANES = 128
SCALE = math.log2(math.e) / math.sqrt(LANES)
SCORE_WIDE = 256
VALUE_WIDE = 512
VMEM = pl.BlockSpec(memory_space=pltpu.VMEM)
SMEM = pl.BlockSpec(memory_space=pltpu.SMEM)
HBM = pl.BlockSpec(memory_space=pltpu.HBM)


def swap(value, axis, bit):
    return lax.ppermute(value, axis, [(n, n ^ bit) for n in range(lax.axis_size(axis))])


def bits_of(axis):
    bit = lax.axis_size(axis) // 2
    while bit:
        yield bit
        bit //= 2


def after(value, done):
    return lax.optimization_barrier((value, done))[0]


def half_copies(pool_ref, target, sem, half, pieces):
    each = pool_ref.shape[0] // pieces
    return [
        pltpu.make_async_copy(
            pool_ref.at[pl.ds(n * each, each), :, :, pl.ds(half * LANES, LANES)],
            target.at[pl.ds(n * each, each)], sem.at[n])
        for n in range(pieces)
    ]


def stage_fresh_kernel(
    n_ctx, slots, bucket_hbm, fresh_ref, kf, vf, slots_ref, counts_ref, bucket_ref, sem, bucket_sem,
):
    copies = [
        half_copies(fresh_ref, kf, sem.at[0], 0, 1)[0], half_copies(fresh_ref, vf, sem.at[1], 1, 1)[0],
    ]
    listed = pltpu.make_async_copy(bucket_hbm, bucket_ref, bucket_sem)
    listed.start()
    for one in copies:
        one.start()
    listed.wait()
    list_fresh(n_ctx, slots, bucket_ref, slots_ref, counts_ref)
    for one in copies:
        one.wait()


def stage_keys_kernel(pieces, pool_ref, kb, done_ref, sem):
    copies = half_copies(pool_ref, kb, sem, 0, pieces)
    for one in copies:
        one.start()
    done_ref[0] = 0
    for one in copies:
        one.wait()


def list_kernel(n_ctx, slots, bucket_ref, slots_ref, counts_ref):
    list_fresh(n_ctx, slots, bucket_ref, slots_ref, counts_ref)


def list_fresh(n_ctx, slots, bucket_ref, slots_ref, counts_ref):
    for n in range(counts_ref.shape[0]):
        counts_ref[n] = 0
    for n in range(slots_ref.shape[0]):
        slots_ref[n] = 0

    def put(page, _):
        request = bucket_ref[page] // n_ctx
        count = counts_ref[request]
        slots_ref[request * slots + count] = page
        counts_ref[request] = count + 1
        return 0

    lax.fori_loop(0, bucket_ref.shape[0], put, 0)


def class_reduce(x, op, heads):
    step = heads
    while step < LANES:
        x = op(x, pltpu.roll(x, step, 1))
        step *= 2
    return x


def pages_of(ref, table_ref, first, count):
    return jnp.concatenate([ref[table_ref[first + n]] for n in range(count)], axis=0)


def score_parts(q, keys, lane, limit, first, heads, sub):
    s = lax.dot_general(q, keys, (((1,), (1,)), ((), ())), preferred_element_type=jnp.float32)
    out = []
    for j in range(s.shape[1] // LANES):
        part = s[:, j * LANES:(j + 1) * LANES]
        one = part[:sub]
        for h in range(1, heads):
            one = jnp.where(lane % heads == h, part[h * sub:(h + 1) * sub], one)
        out.append(jnp.where(lane < limit - (first + j * LANES), one * SCALE, NEG))
    return out


def spread(p, onehots):
    p = p.astype(jnp.bfloat16)
    return jnp.concatenate([p * one for one in onehots], axis=0)


def rows_of(x, h):
    return jnp.broadcast_to(x[:, h:h + 1], x.shape)


def fold_max(parts):
    top = parts[0]
    for part in parts[1:]:
        top = jnp.maximum(top, part)
    return top


def score_kernel(dims, table_ref, len_ref, q_ref, kb, *refs):
    heads, page_rows, pages_dev, sub, pieces = dims
    copies = []
    if pieces:
        pool_ref, t_ref, top_ref, vb, sem = refs
        copies = half_copies(pool_ref, vb, sem, 1, pieces)
    else:
        t_ref, top_ref = refs
    for one in copies:
        one.start()
    columns = pages_dev * page_rows
    wide = min(SCORE_WIDE, columns)
    per = wide // page_rows
    lane = lax.broadcasted_iota(jnp.int32, (sub, LANES), 1)
    start = lax.axis_index("ctx") * (pages_dev * page_rows)

    def step(i, _):
        top = jnp.full((sub, LANES), NEG, jnp.float32)
        limit = len_ref[i] * heads - start
        for c in range(columns // wide):
            keys = pages_of(kb, table_ref, i * pages_dev + c * per, per)
            parts = score_parts(q_ref[i], keys, lane, limit, c * wide, heads, sub)
            for j, part in enumerate(parts):
                t_ref[i, :, c * wide + j * LANES:c * wide + (j + 1) * LANES] = part
            top = jnp.maximum(top, fold_max(parts))
        top_ref[i] = top
        return 0

    shape = top_ref.shape
    flat = (shape[0] * shape[1], LANES)
    lax.fori_loop(0, shape[0], step, 0)
    top_ref[...] = class_reduce(top_ref[...].reshape(flat), jnp.maximum, heads).reshape(shape)
    for one in copies:
        one.wait()


def value_kernel(dims, table_ref, t_ref, top_ref, vb, acc_ref, tot_ref):
    heads, page_rows, pages_dev, sub = dims
    columns = pages_dev * page_rows
    wide = min(VALUE_WIDE, columns)
    per = wide // page_rows
    lane = lax.broadcasted_iota(jnp.int32, (sub, LANES), 1)
    onehots = [(lane % heads == h).astype(jnp.bfloat16) for h in range(heads)]

    def step(i, _):
        tot = jnp.zeros((sub, LANES), jnp.float32)
        acc = jnp.zeros((heads * sub, LANES), jnp.float32)
        top = top_ref[i]
        for c in range(columns // wide):
            weights = []
            for j in range(wide // LANES):
                at = c * wide + j * LANES
                p = jnp.exp2(t_ref[i, :, at:at + LANES] - top)
                tot = tot + p
                weights.append(spread(p, onehots))
            values = pages_of(vb, table_ref, i * pages_dev + c * per, per)
            acc = acc + jnp.dot(
                jnp.concatenate(weights, axis=1), values, preferred_element_type=jnp.float32)
        acc_ref[i] = acc
        tot_ref[i] = tot
        return 0

    shape = tot_ref.shape
    flat = (shape[0] * shape[1], LANES)
    lax.fori_loop(0, shape[0], step, 0)
    tot_ref[...] = class_reduce(tot_ref[...].reshape(flat), jnp.add, heads).reshape(shape)


def fresh_kernel(
    dims, slots_ref, counts_ref, q_refs, kf, vf, acc_ref, top_ref, tot_ref, keep_ref, send_ref,
    t_s, p_s,
):
    heads, page_rows, slots, sub, offsets, req_dev = dims
    lane = lax.broadcasted_iota(jnp.int32, (sub, LANES), 1)
    onehots = [(lane % heads == h).astype(jnp.bfloat16) for h in range(heads)]
    unit = 4 * heads
    columns = slots * page_rows
    wide = min(SCORE_WIDE, columns)
    per = wide // page_rows
    own = lax.axis_index("req")
    requests = [(own ^ offset) * req_dev + i for offset in offsets for i in range(req_dev)]
    n_reqs = len(requests)
    tops = []
    for n, request in enumerate(requests):
        limit = counts_ref[request] * page_rows
        top = jnp.full((sub, LANES), NEG, jnp.float32)
        for c in range(columns // wide):
            keys = pages_of(kf, slots_ref, request * slots + c * per, per)
            q = q_refs[n // req_dev][n % req_dev]
            parts = score_parts(q, keys, lane, limit, c * wide, heads, sub)
            for j, part in enumerate(parts):
                t_s[n, :, c * wide + j * LANES:c * wide + (j + 1) * LANES] = part
            top = jnp.maximum(top, fold_max(parts))
        tops.append(top)
    tops = class_reduce(jnp.concatenate(tops, axis=0), jnp.maximum, heads)
    tops = [tops[n * sub:(n + 1) * sub] for n in range(n_reqs)]
    for i in range(req_dev):
        tops[i] = jnp.maximum(tops[i], top_ref[i])
    tots = []
    for n in range(n_reqs):
        tot = jnp.zeros((sub, LANES), jnp.float32)
        for j in range(columns // LANES):
            p = jnp.exp2(t_s[n, :, j * LANES:(j + 1) * LANES] - tops[n])
            tot = tot + p
            p_s[n, :, j * LANES:(j + 1) * LANES] = spread(p, onehots)
        tots.append(tot)
    tots = class_reduce(jnp.concatenate(tots, axis=0), jnp.add, heads)
    tots = [tots[n * sub:(n + 1) * sub] for n in range(n_reqs)]
    fades = [jnp.exp2(top_ref[i] - tops[i]) for i in range(req_dev)]
    for i in range(req_dev):
        tots[i] = tots[i] + fades[i] * tot_ref[i]
    lses = [jnp.zeros((sub, LANES), jnp.float32) for _ in offsets]
    for n, request in enumerate(requests):
        values = pages_of(vf, slots_ref, request * slots, slots)
        acc = jnp.dot(p_s[n], values, preferred_element_type=jnp.float32)
        whole = 1.0 / tots[n]
        block, i = n // req_dev, n % req_dev
        for h in range(heads):
            some = acc[h * sub:(h + 1) * sub]
            if n < req_dev:
                some = some + acc_ref[n, h * sub:(h + 1) * sub, :] * rows_of(fades[n], h)
            some = some * rows_of(whole, h)
            keep_ref[block, i * heads + h] = some[:sub // 2]
            send_ref[block, i * heads + h] = some[sub // 2:].astype(jnp.bfloat16)
        lse = tops[n] + jnp.log2(tots[n])
        lses[block] = jnp.where(lane // unit == i, lse, lses[block])
    for block, lse in enumerate(lses):
        keep_ref[block, req_dev * heads] = lse[:sub // 2]
        send_ref[block, req_dev * heads] = pieces_of(lse[sub // 2:], heads)


def pieces_of(lse, heads):
    lane = lax.broadcasted_iota(jnp.int32, lse.shape, 1)
    kind = lane % (4 * heads) // heads
    high = lse.astype(jnp.bfloat16).astype(jnp.float32)
    rest = lse - high
    mid = rest.astype(jnp.bfloat16).astype(jnp.float32)
    both = jnp.where(kind == 1, mid, rest - mid)
    return jnp.where(kind == 0, high, both).astype(jnp.bfloat16)


def whole_of(pieces, heads):
    x = pieces.astype(jnp.float32)
    lane = lax.broadcasted_iota(jnp.int32, x.shape, 1)
    kind = lane % (4 * heads) // heads
    x = x + pltpu.roll(x, LANES - heads, 1) + pltpu.roll(x, LANES - 2 * heads, 1)
    same = x
    for m in (1, 2):
        same = jnp.where(kind == m, pltpu.roll(x, m * heads, 1), same)
    return same


def merge_kernel(split, heads, keep_ref, got_ref, *outs):
    blocks, slabs, rows, _ = keep_ref.shape
    slabs -= 1
    half = rows // 2

    def put(block, slab, value, coded):
        if split == "rows":
            outs[0][block, slab] = value[:half]
            outs[1][block, slab] = coded(value[half:])
        elif split == "blocks" and block < blocks // 2:
            outs[0][block, slab] = value
        elif split == "blocks":
            outs[1][block - blocks // 2, slab] = coded(value)
        elif slab < slabs:
            outs[0][slab // heads, slab % heads] = coded(value)

    for block in range(blocks):
        own = keep_ref[block, slabs]
        other = whole_of(got_ref[block, slabs], heads)
        top = jnp.maximum(own, other)
        share = jnp.exp2(own - top)
        tot = share + jnp.exp2(other - top)
        share = share / tot
        for slab in range(slabs):
            at = slab // heads * 4 * heads + slab % heads
            part = jnp.broadcast_to(share[:, at:at + 1], (rows, LANES))
            kept, got = keep_ref[block, slab], got_ref[block, slab].astype(jnp.float32)
            put(block, slab, part * kept + (1.0 - part) * got, lambda x: x.astype(jnp.bfloat16))
        put(block, slabs, top + jnp.log2(tot), lambda x: pieces_of(x, heads))


def params(mib):
    return pltpu.CompilerParams(vmem_limit_bytes=mib * 2**20)


def local(query, kv_pool, page_table, context_len, fresh_kv, fresh_bucket):
    n_ctx = lax.axis_size("ctx")
    n_req = lax.axis_size("req")
    req_dev, heads, group, head_dim = query.shape
    pool_slots, page = kv_pool.shape[:2]
    new_dev = fresh_kv.shape[0]
    pages_dev = page_table.shape[1]
    n_reqs = n_req * req_dev
    slots = CAP * n_ctx
    sub = n_ctx * group
    rows = heads * sub
    page_rows = page * heads

    smem = lambda count: jax.ShapeDtypeStruct((count,), jnp.int32)
    bf16 = lambda *shape: jax.ShapeDtypeStruct(shape, jnp.bfloat16)
    f32 = lambda *shape: jax.ShapeDtypeStruct(shape, jnp.float32)
    columns = pages_dev * page_rows
    split = heads % 4 == 0
    pieces = 8 if split else 0

    near = query[None]
    offsets = [0]
    ctx_bits = list(bits_of("ctx"))
    if split:
        keep_hbm = lambda a: pltpu.with_memory_space_constraint(a, pltpu.HBM)
        pool, fresh = keep_hbm(kv_pool), keep_hbm(fresh_kv)
        arrived = swap(near, "ctx", ctx_bits[0])
        kf, vf, slot_table, counts = pl.pallas_call(
            functools.partial(stage_fresh_kernel, n_ctx, slots),
            out_shape=(
                bf16(new_dev, page, heads, LANES), bf16(new_dev, page, heads, LANES),
                smem(n_reqs * slots), smem(n_reqs)),
            in_specs=[HBM, HBM],
            out_specs=(VMEM,) * 2 + (SMEM,) * 2,
            scratch_shapes=[
                pltpu.SMEM((new_dev,), jnp.int32), pltpu.SemaphoreType.DMA((2, 1)),
                pltpu.SemaphoreType.DMA],
            compiler_params=params(2),
            cost_estimate=pl.CostEstimate(
                flops=0, transcendentals=0, bytes_accessed=4 * fresh_kv.size),
            name="stage_fresh",
        )(keep_hbm(fresh_bucket), fresh)
        near = jnp.concatenate([near, after(arrived, counts)])
        for bit in ctx_bits[1:-1]:
            near = jnp.concatenate([near, swap(near, "ctx", bit)])
        arrived = swap(near, "ctx", ctx_bits[-1])
        kb, done = pl.pallas_call(
            functools.partial(stage_keys_kernel, pieces),
            out_shape=(bf16(pool_slots, page, heads, LANES), smem(1)),
            in_specs=[HBM],
            out_specs=(VMEM, SMEM),
            scratch_shapes=[pltpu.SemaphoreType.DMA((pieces,))],
            compiler_params=params(2),
            cost_estimate=pl.CostEstimate(
                flops=0, transcendentals=0, bytes_accessed=2 * kv_pool.size),
            name="stage_keys",
        )(pool)
        near = jnp.concatenate([near, after(arrived, done)])
        kb, kf, vf = (a.reshape(a.shape[0], page_rows, LANES) for a in (kb, kf, vf))
        score_in, score_specs = (pool,), [HBM]
        score_out = (bf16(pool_slots, page, heads, LANES),)
        score_scratch = [pltpu.SemaphoreType.DMA((pieces,))]
    else:
        for bit in ctx_bits:
            near = jnp.concatenate([near, swap(near, "ctx", bit)])
        kb, vb, kf, vf = (
            a[..., h * LANES:(h + 1) * LANES].reshape(a.shape[0], page_rows, LANES)
            for a in (kv_pool, fresh_kv) for h in (0, 1)
        )
        slot_table, counts = pl.pallas_call(
            functools.partial(list_kernel, n_ctx, slots),
            out_shape=(smem(n_reqs * slots), smem(n_reqs)),
            in_specs=[SMEM],
            out_specs=(SMEM,) * 2,
            name="list",
        )(fresh_bucket)
        score_in, score_specs, score_out, score_scratch = (), [], (), []

    rows_first = lambda a: a.transpose(1, 2, 0, 3, 4).reshape(req_dev, rows, head_dim)
    req_bits = list(bits_of("req"))
    far = [rows_first(near)[None]]
    table = page_table.reshape(-1)
    far.append(swap(far[0], "req", req_bits[0]))
    offsets = [0, req_bits[0]]
    t, top, *staged = pl.pallas_call(
        functools.partial(score_kernel, (heads, page_rows, pages_dev, sub, pieces)),
        out_shape=(f32(req_dev, sub, columns), f32(req_dev, sub, LANES)) + score_out,
        in_specs=[SMEM] * 2 + [VMEM] * 2 + score_specs,
        out_specs=(VMEM,) * (2 + len(score_out)),
        scratch_shapes=score_scratch,
        compiler_params=params(4),
        cost_estimate=pl.CostEstimate(
            flops=2 * req_dev * rows * columns * LANES, transcendentals=0,
            bytes_accessed=kv_pool.size),
        name="scores",
    )(table, context_len, far[0][0], kb, *score_in)
    if staged:
        vb = staged[0].reshape(pool_slots, page_rows, LANES)
    far[1] = after(far[1], top)
    for bit in req_bits[1:]:
        far.append(swap(jnp.concatenate(far), "req", bit))
        offsets += [offset ^ bit for offset in offsets]
    acc, tot = pl.pallas_call(
        functools.partial(value_kernel, (heads, page_rows, pages_dev, sub)),
        out_shape=(f32(req_dev, rows, LANES), f32(req_dev, sub, LANES)),
        in_specs=[SMEM] + [VMEM] * 3,
        out_specs=(VMEM,) * 2,
        compiler_params=params(4),
        cost_estimate=pl.CostEstimate(
            flops=2 * req_dev * rows * columns * LANES, transcendentals=req_dev * sub * columns,
            bytes_accessed=kv_pool.size),
        name="values",
    )(table, t, top, vb)

    slabs = req_dev * heads + 1
    blocks = n_req

    def fresh_call(slots_ref, counts_ref, *refs):
        q_refs = [ref.at[n] for ref in refs[:len(far)] for n in range(ref.shape[0])]
        fresh_kernel(
            (heads, page_rows, slots, sub, offsets, req_dev), slots_ref, counts_ref, q_refs,
            *refs[len(far):])

    keep, send = pl.pallas_call(
        fresh_call,
        out_shape=(
            f32(blocks, slabs, sub // 2, LANES), bf16(blocks, slabs, sub // 2, LANES)),
        in_specs=[SMEM] * 2 + [VMEM] * (5 + len(far)),
        out_specs=(VMEM,) * 2,
        scratch_shapes=[
            pltpu.VMEM((n_reqs, sub, slots * page_rows), jnp.float32),
            pltpu.VMEM((n_reqs, rows, slots * page_rows), jnp.bfloat16),
        ],
        compiler_params=params(8),
        cost_estimate=pl.CostEstimate(
            flops=4 * n_reqs * rows * slots * page_rows * LANES,
            transcendentals=n_reqs * sub * slots * page_rows, bytes_accessed=2 * fresh_kv.size),
        name="fresh",
    )(slot_table, counts, *far, kf, vf, acc, top, tot)

    left = sub // 2
    for axis, bit in [("ctx", b) for b in ctx_bits[::-1]] + [("req", b) for b in req_bits[::-1]]:
        got = swap(send, axis, bit)
        if left > group:
            how, left = "rows", left // 2
        elif blocks > 1:
            how, blocks = "blocks", blocks // 2
        else:
            how = "last"
        shape = (blocks, slabs, left, LANES)
        out = pl.pallas_call(
            functools.partial(merge_kernel, how, heads),
            out_shape=[bf16(req_dev, heads, group, LANES)] if how == "last" else [f32(*shape), bf16(*shape)],
            in_specs=[VMEM] * 2,
            out_specs=[VMEM] if how == "last" else [VMEM] * 2,
            compiler_params=params(8),
            name="merge_" + how,
        )(keep, got)
        if how == "last":
            return out[0]
        keep, send = out


def solution(mesh):
    placed = (
        P("req", "kvh", "ctx", None),
        P(("req", "ctx"), None, "kvh", None),
        P("req", "ctx"),
        P("req"),
        P(("req", "ctx"), None, "kvh", None),
        P(("req", "ctx")),
    )
    return jax.shard_map(
        local, mesh=mesh, in_specs=placed, out_specs=P("req", "kvh", "ctx", None), check_vma=False
    )
```

```python
import functools
import math

import jax
import jax.numpy as jnp
from jax import lax
from jax.experimental import pallas as pl
from jax.experimental.pallas import tpu as pltpu
from jax.sharding import PartitionSpec as P

NEG = -1e30
CAP = 2
LANES = 128
SCALE = math.log2(math.e) / math.sqrt(LANES)
SCORE_WIDE = 256
VALUE_WIDE = 512
VMEM = pl.BlockSpec(memory_space=pltpu.VMEM)
SMEM = pl.BlockSpec(memory_space=pltpu.SMEM)
HBM = pl.BlockSpec(memory_space=pltpu.HBM)


def swap(value, axis, bit):
    return lax.ppermute(value, axis, [(n, n ^ bit) for n in range(lax.axis_size(axis))])


def half_copies(pool_ref, target, sem, half, pieces):
    each = pool_ref.shape[0] // pieces
    return [
        pltpu.make_async_copy(
            pool_ref.at[pl.ds(n * each, each), :, :, pl.ds(half * LANES, LANES)],
            target.at[pl.ds(n * each, each)], sem.at[n])
        for n in range(pieces)
    ]


def stage_kernel(
    pieces, n_ctx, slots, bucket_hbm, pool_ref, fresh_ref, kb, vb, kf, vf, slots_ref, counts_ref,
    bucket_ref, sem, fresh_sem, bucket_sem,
):
    listed = pltpu.make_async_copy(bucket_hbm, bucket_ref, bucket_sem)
    copies = []
    for half, (pool_to, fresh_to) in enumerate(((kb, kf), (vb, vf))):
        copies += half_copies(fresh_ref, fresh_to, fresh_sem.at[half], half, 1)
        copies += half_copies(pool_ref, pool_to, sem.at[half], half, pieces)
    listed.start()
    for one in copies:
        one.start()
    listed.wait()
    list_fresh(n_ctx, slots, bucket_ref, slots_ref, counts_ref)
    for one in copies:
        one.wait()


def list_kernel(n_ctx, slots, bucket_ref, slots_ref, counts_ref):
    list_fresh(n_ctx, slots, bucket_ref, slots_ref, counts_ref)


def list_fresh(n_ctx, slots, bucket_ref, slots_ref, counts_ref):
    for n in range(counts_ref.shape[0]):
        counts_ref[n] = 0
    for n in range(slots_ref.shape[0]):
        slots_ref[n] = 0

    def put(page, _):
        request = bucket_ref[page] // n_ctx
        count = counts_ref[request]
        slots_ref[request * slots + count] = page
        counts_ref[request] = count + 1
        return 0

    lax.fori_loop(0, bucket_ref.shape[0], put, 0)


def class_reduce(x, op, heads):
    step = heads
    while step < LANES:
        x = op(x, pltpu.roll(x, step, 1))
        step *= 2
    return x


def pages_of(ref, table_ref, first, count):
    return jnp.concatenate([ref[table_ref[first + n]] for n in range(count)], axis=0)


def score_parts(q, keys, lane, limit, first, heads, sub):
    s = lax.dot_general(q, keys, (((1,), (1,)), ((), ())), preferred_element_type=jnp.float32)
    out = []
    for j in range(s.shape[1] // LANES):
        part = s[:, j * LANES:(j + 1) * LANES]
        one = part[:sub]
        for h in range(1, heads):
            one = jnp.where(lane % heads == h, part[h * sub:(h + 1) * sub], one)
        out.append(jnp.where(lane < limit - (first + j * LANES), one * SCALE, NEG))
    return out


def spread(p, onehots):
    p = p.astype(jnp.bfloat16)
    return jnp.concatenate([p * one for one in onehots], axis=0)


def rows_of(x, h):
    return jnp.broadcast_to(x[:, h:h + 1], x.shape)


def fold_max(parts):
    top = parts[0]
    for part in parts[1:]:
        top = jnp.maximum(top, part)
    return top


def resident_kernel(dims, table_ref, len_ref, q_ref, kb, vb, out_ref, t_s, top_s, tot_s, acc_s):
    heads, page_rows, pages_dev, sub, req_dev, n_ctx = dims
    columns = pages_dev * page_rows
    lane = lax.broadcasted_iota(jnp.int32, (sub, LANES), 1)
    onehots = [(lane % heads == h).astype(jnp.bfloat16) for h in range(heads)]
    ctx = lax.axis_index("ctx")
    first = lax.axis_index("req") * req_dev
    start = ctx * columns

    def score_step(i, _):
        wide = min(SCORE_WIDE, columns)
        per = wide // page_rows
        top = jnp.full((sub, LANES), NEG, jnp.float32)
        limit = len_ref[i] * heads - start
        for c in range(columns // wide):
            keys = pages_of(kb, table_ref, i * pages_dev + c * per, per)
            parts = score_parts(q_ref[first + i], keys, lane, limit, c * wide, heads, sub)
            for j, part in enumerate(parts):
                t_s[i, :, c * wide + j * LANES:c * wide + (j + 1) * LANES] = part
            top = jnp.maximum(top, fold_max(parts))
        top_s[i] = top
        return 0

    def value_step(i, _):
        wide = min(VALUE_WIDE, columns)
        per = wide // page_rows
        tot = jnp.zeros((sub, LANES), jnp.float32)
        acc = jnp.zeros((heads * sub, LANES), jnp.float32)
        top = top_s[i]
        for c in range(columns // wide):
            weights = []
            for j in range(wide // LANES):
                at = c * wide + j * LANES
                p = jnp.exp2(t_s[i, :, at:at + LANES] - top)
                tot = tot + p
                weights.append(spread(p, onehots))
            values = pages_of(vb, table_ref, i * pages_dev + c * per, per)
            acc = acc + jnp.dot(
                jnp.concatenate(weights, axis=1), values, preferred_element_type=jnp.float32)
        acc_s[i] = acc
        tot_s[i] = tot
        return 0

    flat = (req_dev * sub, LANES)
    lax.fori_loop(0, req_dev, score_step, 0)
    top_s[...] = class_reduce(top_s[...].reshape(flat), jnp.maximum, heads).reshape(top_s.shape)
    lax.fori_loop(0, req_dev, value_step, 0)
    tots = class_reduce(tot_s[...].reshape(flat), jnp.add, heads)
    whole = 1.0 / tots
    lses = top_s[...].reshape(flat) + jnp.log2(tots)
    group = sub // n_ctx

    def put(slab, value, coded):
        for place in range(n_ctx):
            out_ref[place ^ ctx, slab] = coded(value[place * group:(place + 1) * group])

    lse = jnp.zeros((sub, LANES), jnp.float32)
    for i in range(req_dev):
        rows = slice(i * sub, (i + 1) * sub)
        for h in range(heads):
            some = acc_s[i, h * sub:(h + 1) * sub, :] * rows_of(whole[rows], h)
            put(i * heads + h, some, lambda x: x.astype(jnp.bfloat16))
        lse = jnp.where(lane // (4 * heads) == i, lses[rows], lse)
    put(req_dev * heads, lse, lambda x: pieces_of(x, heads))


def fresh_kernel(dims, slots_ref, counts_ref, q_ref, kf, vf, out_ref, t_s, p_s):
    heads, page_rows, slots, sub, n_req, req_dev = dims
    lane = lax.broadcasted_iota(jnp.int32, (sub, LANES), 1)
    onehots = [(lane % heads == h).astype(jnp.bfloat16) for h in range(heads)]
    columns = slots * page_rows
    wide = min(SCORE_WIDE, columns)
    per = wide // page_rows
    n_reqs = n_req * req_dev
    tops = []
    for n in range(n_reqs):
        limit = counts_ref[n] * page_rows
        top = jnp.full((sub, LANES), NEG, jnp.float32)
        for c in range(columns // wide):
            keys = pages_of(kf, slots_ref, n * slots + c * per, per)
            parts = score_parts(q_ref[n], keys, lane, limit, c * wide, heads, sub)
            for j, part in enumerate(parts):
                t_s[n, :, c * wide + j * LANES:c * wide + (j + 1) * LANES] = part
            top = jnp.maximum(top, fold_max(parts))
        tops.append(top)
    tops = class_reduce(jnp.concatenate(tops, axis=0), jnp.maximum, heads)
    tots = []
    for n in range(n_reqs):
        tot = jnp.zeros((sub, LANES), jnp.float32)
        for j in range(columns // LANES):
            p = jnp.exp2(
                t_s[n, :, j * LANES:(j + 1) * LANES] - tops[n * sub:(n + 1) * sub])
            tot = tot + p
            p_s[n, :, j * LANES:(j + 1) * LANES] = spread(p, onehots)
        tots.append(tot)
    tots = class_reduce(jnp.concatenate(tots, axis=0), jnp.add, heads)
    whole = 1.0 / tots
    lses = tops + jnp.log2(tots)
    for block in range(n_req):
        lse = jnp.zeros((sub, LANES), jnp.float32)
        for i in range(req_dev):
            n = block * req_dev + i
            values = pages_of(vf, slots_ref, n * slots, slots)
            acc = jnp.dot(p_s[n], values, preferred_element_type=jnp.float32)
            rows = slice(n * sub, (n + 1) * sub)
            for h in range(heads):
                some = acc[h * sub:(h + 1) * sub] * rows_of(whole[rows], h)
                out_ref[block, i * heads + h] = some.astype(jnp.bfloat16)
            lse = jnp.where(lane // (4 * heads) == i, lses[rows], lse)
        out_ref[block, req_dev * heads] = pieces_of(lse, heads)


def pieces_of(lse, heads):
    lane = lax.broadcasted_iota(jnp.int32, lse.shape, 1)
    kind = lane % (4 * heads) // heads
    high = lse.astype(jnp.bfloat16).astype(jnp.float32)
    rest = lse - high
    mid = rest.astype(jnp.bfloat16).astype(jnp.float32)
    both = jnp.where(kind == 1, mid, rest - mid)
    return jnp.where(kind == 0, high, both).astype(jnp.bfloat16)


def whole_of(pieces, heads):
    x = pieces.astype(jnp.float32)
    return x + pltpu.roll(x, LANES - heads, 1) + pltpu.roll(x, LANES - 2 * heads, 1)


def merge_kernel(*refs):
    many, *ones, out_ref = refs
    parts = [many.at[n] for n in range(many.shape[0])] + ones
    req_dev, heads, group, _ = out_ref.shape
    lses = [whole_of(part[req_dev * heads], heads) for part in parts]
    top = fold_max(lses)
    shares = [jnp.exp2(lse - top) for lse in lses]
    tot = shares[0]
    for share in shares[1:]:
        tot = tot + share
    shares = [share / tot for share in shares]
    for i in range(req_dev):
        for h in range(heads):
            at = i * 4 * heads + h
            total = jnp.zeros((group, LANES), jnp.float32)
            for part, share in zip(parts, shares):
                total = total + part[i * heads + h].astype(jnp.float32) * jnp.broadcast_to(
                    share[:, at:at + 1], (group, LANES))
            out_ref[i, h] = total.astype(jnp.bfloat16)


def params(mib):
    return pltpu.CompilerParams(vmem_limit_bytes=mib * 2**20)


def local(query, kv_pool, page_table, context_len, fresh_kv, fresh_bucket):
    n_ctx = lax.axis_size("ctx")
    n_req = lax.axis_size("req")
    req_dev, heads, group, head_dim = query.shape
    pool_slots, page = kv_pool.shape[:2]
    new_dev = fresh_kv.shape[0]
    pages_dev = page_table.shape[1]
    n_reqs = n_req * req_dev
    slots = CAP * n_ctx
    sub = n_ctx * group
    rows = heads * sub
    page_rows = page * heads

    smem = lambda count: jax.ShapeDtypeStruct((count,), jnp.int32)
    bf16 = lambda *shape: jax.ShapeDtypeStruct(shape, jnp.bfloat16)
    f32 = lambda *shape: jax.ShapeDtypeStruct(shape, jnp.float32)
    columns = pages_dev * page_rows
    split = heads % 4 == 0
    pieces = 8 if split else 0

    n_src = n_req * n_ctx
    everyone = ("req", "ctx")
    arrived = lax.all_to_all(
        jnp.broadcast_to(query, (n_src,) + query.shape), everyone, split_axis=0, concat_axis=0,
        tiled=True)
    if split:
        in_hbm = lambda a: pltpu.with_memory_space_constraint(a, pltpu.HBM)
        half = lambda count: bf16(count, page, heads, LANES)
        kb, vb, kf, vf, slot_table, counts = pl.pallas_call(
            functools.partial(stage_kernel, pieces, n_ctx, slots),
            out_shape=(
                half(pool_slots), half(pool_slots), half(new_dev), half(new_dev),
                smem(n_reqs * slots), smem(n_reqs)),
            in_specs=[HBM] * 3,
            out_specs=(VMEM,) * 4 + (SMEM,) * 2,
            scratch_shapes=[
                pltpu.SMEM((new_dev,), jnp.int32), pltpu.SemaphoreType.DMA((2, pieces)),
                pltpu.SemaphoreType.DMA((2, 1)), pltpu.SemaphoreType.DMA],
            compiler_params=params(2),
            cost_estimate=pl.CostEstimate(
                flops=0, transcendentals=0, bytes_accessed=4 * (kv_pool.size + fresh_kv.size)),
            name="stage",
        )(in_hbm(fresh_bucket), in_hbm(kv_pool), in_hbm(fresh_kv))
        kb, vb, kf, vf = (a.reshape(a.shape[0], page_rows, LANES) for a in (kb, vb, kf, vf))
    else:
        kb, vb, kf, vf = (
            a[..., h * LANES:(h + 1) * LANES].reshape(a.shape[0], page_rows, LANES)
            for a in (kv_pool, fresh_kv) for h in (0, 1)
        )
        slot_table, counts = pl.pallas_call(
            functools.partial(list_kernel, n_ctx, slots),
            out_shape=(smem(n_reqs * slots), smem(n_reqs)),
            in_specs=[SMEM],
            out_specs=(SMEM,) * 2,
            name="list",
        )(fresh_bucket)

    queries = arrived.reshape((n_req, n_ctx) + query.shape).transpose(0, 2, 3, 1, 4, 5)
    queries = queries.reshape(n_reqs, rows, head_dim)
    slabs = req_dev * heads + 1
    parts = pl.pallas_call(
        functools.partial(fresh_kernel, (heads, page_rows, slots, sub, n_req, req_dev)),
        out_shape=bf16(n_req, slabs, sub, LANES),
        in_specs=[SMEM] * 2 + [VMEM] * 3,
        out_specs=VMEM,
        scratch_shapes=[
            pltpu.VMEM((n_reqs, sub, slots * page_rows), jnp.float32),
            pltpu.VMEM((n_reqs, rows, slots * page_rows), jnp.bfloat16),
        ],
        compiler_params=params(8),
        cost_estimate=pl.CostEstimate(
            flops=4 * n_reqs * rows * slots * page_rows * LANES,
            transcendentals=n_reqs * sub * slots * page_rows, bytes_accessed=2 * fresh_kv.size),
        name="fresh",
    )(slot_table, counts, queries, kf, vf)
    sends = parts.reshape(n_req, slabs, n_ctx, group, LANES).transpose(0, 2, 1, 3, 4)
    sends = sends.reshape(n_src, slabs, group, LANES)
    sends, queries = lax.optimization_barrier((sends, queries))
    got = lax.all_to_all(sends, everyone, split_axis=0, concat_axis=0, tiled=True)

    mine = pl.pallas_call(
        functools.partial(
            resident_kernel, (heads, page_rows, pages_dev, sub, req_dev, n_ctx)),
        out_shape=bf16(n_ctx, slabs, group, LANES),
        in_specs=[SMEM] * 2 + [VMEM] * 3,
        out_specs=VMEM,
        scratch_shapes=[
            pltpu.VMEM((req_dev, sub, columns), jnp.float32),
            pltpu.VMEM((req_dev, sub, LANES), jnp.float32),
            pltpu.VMEM((req_dev, sub, LANES), jnp.float32),
            pltpu.VMEM((req_dev, rows, LANES), jnp.float32),
        ],
        compiler_params=params(5),
        cost_estimate=pl.CostEstimate(
            flops=4 * req_dev * rows * columns * LANES, transcendentals=req_dev * sub * columns,
            bytes_accessed=2 * kv_pool.size),
        name="resident",
    )(page_table.reshape(-1), context_len, queries, kb, vb)
    ones = [mine[0]] + [swap(mine[bits], "ctx", bits) for bits in range(1, n_ctx)]
    return pl.pallas_call(
        merge_kernel,
        out_shape=bf16(req_dev, heads, group, LANES),
        in_specs=[VMEM] * (1 + n_ctx),
        out_specs=VMEM,
        compiler_params=params(8),
        name="merge",
    )(got, *ones)


def solution(mesh):
    placed = (
        P("req", "kvh", "ctx", None),
        P(("req", "ctx"), None, "kvh", None),
        P("req", "ctx"),
        P("req"),
        P(("req", "ctx"), None, "kvh", None),
        P(("req", "ctx")),
    )
    return jax.shard_map(
        local, mesh=mesh, in_specs=placed, out_specs=P("req", "kvh", "ctx", None), check_vma=False
    )
```

```python
import functools
import math

import jax
import jax.numpy as jnp
from jax import lax
from jax.experimental import pallas as pl
from jax.experimental.pallas import tpu as pltpu
from jax.sharding import PartitionSpec as P

NEG = -1e30
CAP = 2
LANES = 128
SCALE = math.log2(math.e) / math.sqrt(LANES)
SCORE_WIDE = 256
VALUE_WIDE = 512
VMEM = pl.BlockSpec(memory_space=pltpu.VMEM)
SMEM = pl.BlockSpec(memory_space=pltpu.SMEM)
HBM = pl.BlockSpec(memory_space=pltpu.HBM)


def swap(value, axis, bit):
    return lax.ppermute(value, axis, [(n, n ^ bit) for n in range(lax.axis_size(axis))])


def bits_of(axis):
    bit = lax.axis_size(axis) // 2
    while bit:
        yield bit
        bit //= 2


def half_copies(pool_ref, target, sem, half, pieces):
    each = pool_ref.shape[0] // pieces
    return [
        pltpu.make_async_copy(
            pool_ref.at[pl.ds(n * each, each), :, :, pl.ds(half * LANES, LANES)],
            target.at[pl.ds(n * each, each)], sem.at[n])
        for n in range(pieces)
    ]


def stage_fresh_kernel(fresh_ref, kf, vf, sem):
    copies = []
    for half, to in enumerate((kf, vf)):
        copies += half_copies(fresh_ref, to, sem.at[half], half, sem.shape[1])
    for one in copies:
        one.start()
    for one in copies:
        one.wait()


def stage_keys_kernel(
    n_ctx, slots, bucket_hbm, pool_ref, kb, slots_ref, counts_ref, bucket_ref, sem, bucket_sem,
):
    listed = pltpu.make_async_copy(bucket_hbm, bucket_ref, bucket_sem)
    copies = half_copies(pool_ref, kb, sem, 0, sem.shape[0])
    listed.start()
    for one in copies:
        one.start()
    listed.wait()
    list_fresh(n_ctx, slots, bucket_ref, slots_ref, counts_ref)
    for one in copies:
        one.wait()


def list_kernel(n_ctx, slots, bucket_ref, slots_ref, counts_ref):
    list_fresh(n_ctx, slots, bucket_ref, slots_ref, counts_ref)


def list_fresh(n_ctx, slots, bucket_ref, slots_ref, counts_ref):
    for n in range(counts_ref.shape[0]):
        counts_ref[n] = 0
    for n in range(slots_ref.shape[0]):
        slots_ref[n] = 0

    def put(page, _):
        request = bucket_ref[page] // n_ctx
        count = counts_ref[request]
        slots_ref[request * slots + count] = page
        counts_ref[request] = count + 1
        return 0

    lax.fori_loop(0, bucket_ref.shape[0], put, 0)


def class_reduce(x, op, heads):
    step = heads
    while step < LANES:
        x = op(x, pltpu.roll(x, step, 1))
        step *= 2
    return x


def pages_of(ref, table_ref, first, count):
    return jnp.concatenate([ref[table_ref[first + n]] for n in range(count)], axis=0)


def score_parts(q, keys, lane, limit, first, heads, sub):
    s = lax.dot_general(q, keys, (((1,), (1,)), ((), ())), preferred_element_type=jnp.float32)
    out = []
    for j in range(s.shape[1] // LANES):
        part = s[:, j * LANES:(j + 1) * LANES]
        one = part[:sub]
        for h in range(1, heads):
            one = jnp.where(lane % heads == h, part[h * sub:(h + 1) * sub], one)
        out.append(jnp.where(lane < limit - (first + j * LANES), one * SCALE, NEG))
    return out


def spread(p, onehots):
    p = p.astype(jnp.bfloat16)
    return jnp.concatenate([p * one for one in onehots], axis=0)


def rows_of(x, h):
    return jnp.broadcast_to(x[:, h:h + 1], x.shape)


def fold_max(parts):
    top = parts[0]
    for part in parts[1:]:
        top = jnp.maximum(top, part)
    return top


def score_kernel(dims, table_ref, len_ref, q_ref, kb, *refs):
    heads, page_rows, pages_dev, sub, pieces = dims
    copies = []
    if pieces:
        pool_ref, t_ref, top_ref, vb, sem = refs
        copies = half_copies(pool_ref, vb, sem, 1, pieces)
    else:
        t_ref, top_ref = refs
    for one in copies:
        one.start()
    columns = pages_dev * page_rows
    wide = min(SCORE_WIDE, columns)
    per = wide // page_rows
    lane = lax.broadcasted_iota(jnp.int32, (sub, LANES), 1)
    start = lax.axis_index("ctx") * (pages_dev * page_rows)

    def step(i, _):
        top = jnp.full((sub, LANES), NEG, jnp.float32)
        limit = len_ref[i] * heads - start
        for c in range(columns // wide):
            keys = pages_of(kb, table_ref, i * pages_dev + c * per, per)
            parts = score_parts(q_ref[i], keys, lane, limit, c * wide, heads, sub)
            for j, part in enumerate(parts):
                t_ref[i, :, c * wide + j * LANES:c * wide + (j + 1) * LANES] = part
            top = jnp.maximum(top, fold_max(parts))
        top_ref[i] = top
        return 0

    shape = top_ref.shape
    flat = (shape[0] * shape[1], LANES)
    lax.fori_loop(0, shape[0], step, 0)
    top_ref[...] = class_reduce(top_ref[...].reshape(flat), jnp.maximum, heads).reshape(shape)
    for one in copies:
        one.wait()


def value_kernel(
    dims, table_ref, t_ref, top_ref, vb, acc_ref, ftop_ref, ftot_ref, keep_ref, send_ref,
    acc_s, tot_s,
):
    heads, page_rows, pages_dev, sub = dims
    req_dev = t_ref.shape[0]
    columns = pages_dev * page_rows
    wide = min(VALUE_WIDE, columns)
    per = wide // page_rows
    lane = lax.broadcasted_iota(jnp.int32, (sub, LANES), 1)
    onehots = [(lane % heads == h).astype(jnp.bfloat16) for h in range(heads)]

    def step(i, _):
        tot = jnp.zeros((sub, LANES), jnp.float32)
        acc = jnp.zeros((heads * sub, LANES), jnp.float32)
        top = top_ref[i]
        for c in range(columns // wide):
            weights = []
            for j in range(wide // LANES):
                at = c * wide + j * LANES
                p = jnp.exp2(t_ref[i, :, at:at + LANES] - top)
                tot = tot + p
                weights.append(spread(p, onehots))
            values = pages_of(vb, table_ref, i * pages_dev + c * per, per)
            acc = acc + jnp.dot(
                jnp.concatenate(weights, axis=1), values, preferred_element_type=jnp.float32)
        acc_s[i] = acc
        tot_s[i] = tot
        return 0

    lax.fori_loop(0, req_dev, step, 0)
    flat = (req_dev * sub, LANES)
    tots = class_reduce(tot_s[...].reshape(flat), jnp.add, heads)
    top, ftop = top_ref[...].reshape(flat), ftop_ref[...].reshape(flat)
    both = jnp.maximum(top, ftop)
    fade, ffade = jnp.exp2(top - both), jnp.exp2(ftop - both)
    tots = tots * fade + ftot_ref[...].reshape(flat) * ffade
    fade, ffade = fade / tots, ffade / tots
    lses = both + jnp.log2(tots)
    for i in range(req_dev):
        rows = slice(i * sub, (i + 1) * sub)
        for h in range(heads):
            part = slice(h * sub, (h + 1) * sub)
            some = acc_s[i, part, :] * rows_of(fade[rows], h)
            some = some + acc_ref[i, part, :] * rows_of(ffade[rows], h)
            put_rows(keep_ref, send_ref, (0, i * heads + h), some)
    lse = by_request(lses, heads, sub, range(req_dev))
    put_rows(keep_ref, send_ref, (0, req_dev * heads), lse, heads)


def put_rows(keep_ref, send_ref, place, value, heads=0):
    half = value.shape[0] // 2
    send = value[half:]
    keep_ref[place] = value[:half]
    send_ref[place] = pieces_of(send, heads) if heads else send.astype(jnp.bfloat16)


def by_request(lses, heads, sub, requests):
    lane = lax.broadcasted_iota(jnp.int32, (sub, LANES), 1)
    out = jnp.zeros((sub, LANES), jnp.float32)
    for i, n in enumerate(requests):
        out = jnp.where(lane // (4 * heads) == i, lses[n * sub:(n + 1) * sub], out)
    return out


def fresh_kernel(
    dims, slots_ref, counts_ref, *refs,
):
    heads, page_rows, slots, sub, req_dev = dims
    *q_refs, kf, vf, keep_ref, send_ref, acc_ref, top_ref, tot_ref, t_s, p_s = refs
    lane = lax.broadcasted_iota(jnp.int32, (sub, LANES), 1)
    onehots = [(lane % heads == h).astype(jnp.bfloat16) for h in range(heads)]
    columns = slots * page_rows
    wide = min(SCORE_WIDE, columns)
    per = wide // page_rows
    own = lax.axis_index("req")
    requests = [(own ^ k) * req_dev + i for k in range(len(q_refs)) for i in range(req_dev)]
    n_reqs = len(requests)
    tops = []
    for n, request in enumerate(requests):
        limit = counts_ref[request] * page_rows
        top = jnp.full((sub, LANES), NEG, jnp.float32)
        for c in range(columns // wide):
            keys = pages_of(kf, slots_ref, request * slots + c * per, per)
            q = q_refs[n // req_dev][n % req_dev]
            parts = score_parts(q, keys, lane, limit, c * wide, heads, sub)
            for j, part in enumerate(parts):
                t_s[n, :, c * wide + j * LANES:c * wide + (j + 1) * LANES] = part
            top = jnp.maximum(top, fold_max(parts))
        tops.append(top)
    tops = class_reduce(jnp.concatenate(tops, axis=0), jnp.maximum, heads)
    tots = []
    for n in range(n_reqs):
        tot = jnp.zeros((sub, LANES), jnp.float32)
        for j in range(columns // LANES):
            p = jnp.exp2(
                t_s[n, :, j * LANES:(j + 1) * LANES] - tops[n * sub:(n + 1) * sub])
            tot = tot + p
            p_s[n, :, j * LANES:(j + 1) * LANES] = spread(p, onehots)
        tots.append(tot)
    tots = class_reduce(jnp.concatenate(tots, axis=0), jnp.add, heads)
    whole = 1.0 / tots
    lses = tops + jnp.log2(tots)
    for n, request in enumerate(requests):
        values = pages_of(vf, slots_ref, request * slots, slots)
        acc = jnp.dot(p_s[n], values, preferred_element_type=jnp.float32)
        rows = slice(n * sub, (n + 1) * sub)
        block, i = n // req_dev - 1, n % req_dev
        if block < 0:
            acc_ref[i] = acc
            top_ref[i] = tops[rows]
            tot_ref[i] = tots[rows]
            continue
        for h in range(heads):
            some = acc[h * sub:(h + 1) * sub] * rows_of(whole[rows], h)
            put_rows(keep_ref, send_ref, (block, i * heads + h), some)
    for block in range(len(q_refs) - 1):
        first = (block + 1) * req_dev
        lse = by_request(lses, heads, sub, range(first, first + req_dev))
        put_rows(keep_ref, send_ref, (block, req_dev * heads), lse, heads)


def pieces_of(lse, heads):
    lane = lax.broadcasted_iota(jnp.int32, lse.shape, 1)
    kind = lane % (4 * heads) // heads
    high = lse.astype(jnp.bfloat16).astype(jnp.float32)
    rest = lse - high
    mid = rest.astype(jnp.bfloat16).astype(jnp.float32)
    both = jnp.where(kind == 1, mid, rest - mid)
    return jnp.where(kind == 0, high, both).astype(jnp.bfloat16)


def whole_of(pieces, heads):
    x = pieces.astype(jnp.float32)
    lane = lax.broadcasted_iota(jnp.int32, x.shape, 1)
    kind = lane % (4 * heads) // heads
    x = x + pltpu.roll(x, LANES - heads, 1) + pltpu.roll(x, LANES - 2 * heads, 1)
    same = x
    for m in (1, 2):
        same = jnp.where(kind == m, pltpu.roll(x, m * heads, 1), same)
    return same


def merge_kernel(heads, skip, goals, keep_ref, got_ref, *outs):
    blocks, slabs, rows, _ = keep_ref.shape
    slabs -= 1

    def put(block, slab, value, coded=0):
        if goals[block] is None:
            put_rows(outs[0], outs[1], (block, slab), value, coded)
        else:
            which, place = goals[block]
            if outs[which].dtype == jnp.bfloat16:
                value = pieces_of(value, coded) if coded else value.astype(jnp.bfloat16)
            outs[which][place, slab] = value

    for block in range(blocks):
        own = keep_ref[block, slabs]
        other = whole_of(got_ref[block + skip, slabs], heads)
        top = jnp.maximum(own, other)
        share = jnp.exp2(own - top)
        tot = share + jnp.exp2(other - top)
        share = share / tot
        for slab in range(slabs):
            at = slab // heads * 4 * heads + slab % heads
            part = jnp.broadcast_to(share[:, at:at + 1], (rows, LANES))
            kept = keep_ref[block, slab]
            got = got_ref[block + skip, slab].astype(jnp.float32)
            put(block, slab, part * kept + (1.0 - part) * got)
        put(block, slabs, top + jnp.log2(tot), heads)


def last_kernel(keep_ref, *refs):
    *got_refs, out_ref = refs
    req_dev, heads, group, _ = out_ref.shape
    slabs = req_dev * heads
    parts = [keep_ref.at[0]] + [ref.at[0] for ref in got_refs]
    lses = [keep_ref[0, slabs]] + [whole_of(ref[0, slabs], heads) for ref in got_refs]
    top = fold_max(lses)
    shares = [jnp.exp2(lse - top) for lse in lses]
    tot = shares[0]
    for share in shares[1:]:
        tot = tot + share
    shares = [share / tot for share in shares]
    for slab in range(slabs):
        at = slab // heads * 4 * heads + slab % heads
        total = jnp.zeros((group, LANES), jnp.float32)
        for part, share in zip(parts, shares):
            total = total + part[slab].astype(jnp.float32) * jnp.broadcast_to(
                share[:, at:at + 1], (group, LANES))
        out_ref[slab // heads, slab % heads] = total.astype(jnp.bfloat16)


def params(mib):
    return pltpu.CompilerParams(vmem_limit_bytes=mib * 2**20)


def local(query, kv_pool, page_table, context_len, fresh_kv, fresh_bucket):
    n_ctx = lax.axis_size("ctx")
    n_req = lax.axis_size("req")
    req_dev, heads, group, head_dim = query.shape
    pool_slots, page = kv_pool.shape[:2]
    new_dev = fresh_kv.shape[0]
    pages_dev = page_table.shape[1]
    n_reqs = n_req * req_dev
    slots = CAP * n_ctx
    sub = n_ctx * group
    rows = heads * sub
    page_rows = page * heads

    smem = lambda count: jax.ShapeDtypeStruct((count,), jnp.int32)
    bf16 = lambda *shape: jax.ShapeDtypeStruct(shape, jnp.bfloat16)
    f32 = lambda *shape: jax.ShapeDtypeStruct(shape, jnp.float32)
    columns = pages_dev * page_rows
    split = heads % 4 == 0
    pieces = 8 if split else 0

    near = query[None]
    first, *others = bits_of("ctx")
    arrived = swap(near, "ctx", first)
    if split:
        in_hbm = lambda a: pltpu.with_memory_space_constraint(a, pltpu.HBM)
        pool = in_hbm(kv_pool)
        half = lambda count: bf16(count, page, heads, LANES)
        kf, vf = pl.pallas_call(
            stage_fresh_kernel,
            out_shape=(half(new_dev), half(new_dev)),
            in_specs=[HBM],
            out_specs=(VMEM,) * 2,
            scratch_shapes=[pltpu.SemaphoreType.DMA((2, 4))],
            compiler_params=params(2),
            cost_estimate=pl.CostEstimate(
                flops=0, transcendentals=0, bytes_accessed=4 * fresh_kv.size),
            name="stage_fresh",
        )(in_hbm(fresh_kv))
        arrived, kf = lax.optimization_barrier((arrived, kf))
        kb, slot_table, counts = pl.pallas_call(
            functools.partial(stage_keys_kernel, n_ctx, slots),
            out_shape=(half(pool_slots), smem(n_reqs * slots), smem(n_reqs)),
            in_specs=[HBM] * 2,
            out_specs=(VMEM, SMEM, SMEM),
            scratch_shapes=[
                pltpu.SMEM((new_dev,), jnp.int32), pltpu.SemaphoreType.DMA((pieces,)),
                pltpu.SemaphoreType.DMA],
            compiler_params=params(2),
            cost_estimate=pl.CostEstimate(
                flops=0, transcendentals=0, bytes_accessed=2 * kv_pool.size),
            name="stage_keys",
        )(in_hbm(fresh_bucket), pool)
        kb, kf, vf = (a.reshape(a.shape[0], page_rows, LANES) for a in (kb, kf, vf))
        score_in, score_specs, score_out = (pool,), [HBM], (half(pool_slots),)
        score_scratch = [pltpu.SemaphoreType.DMA((pieces,))]
    else:
        kb, vb, kf, vf = (
            a[..., h * LANES:(h + 1) * LANES].reshape(a.shape[0], page_rows, LANES)
            for a in (kv_pool, fresh_kv) for h in (0, 1)
        )
        slot_table, counts = pl.pallas_call(
            functools.partial(list_kernel, n_ctx, slots),
            out_shape=(smem(n_reqs * slots), smem(n_reqs)),
            in_specs=[SMEM],
            out_specs=(SMEM,) * 2,
            name="list",
        )(fresh_bucket)
        score_in, score_specs, score_out, score_scratch = (), [], (), []

    near = jnp.concatenate([near, arrived])
    for bit in others:
        near = jnp.concatenate([near, swap(near, "ctx", bit)])
    q_own = near.transpose(1, 2, 0, 3, 4).reshape(req_dev, rows, head_dim)
    far = [q_own] + [swap(q_own, "req", k) for k in range(n_req - 1, 0, -1)][::-1]

    slabs = req_dev * heads + 1
    left = sub // 2
    keep, send, acc, ftop, ftot = pl.pallas_call(
        functools.partial(fresh_kernel, (heads, page_rows, slots, sub, req_dev)),
        out_shape=(
            f32(n_req - 1, slabs, left, LANES), bf16(n_req - 1, slabs, left, LANES),
            f32(req_dev, rows, LANES), f32(req_dev, sub, LANES), f32(req_dev, sub, LANES)),
        in_specs=[SMEM] * 2 + [VMEM] * (2 + n_req),
        out_specs=(VMEM,) * 5,
        scratch_shapes=[
            pltpu.VMEM((n_reqs, sub, slots * page_rows), jnp.float32),
            pltpu.VMEM((n_reqs, rows, slots * page_rows), jnp.bfloat16),
        ],
        compiler_params=params(8),
        cost_estimate=pl.CostEstimate(
            flops=4 * n_reqs * rows * slots * page_rows * LANES,
            transcendentals=n_reqs * sub * slots * page_rows, bytes_accessed=2 * fresh_kv.size),
        name="fresh",
    )(slot_table, counts, *far, kf, vf)

    def merge(keep, got, skip, goals, shapes):
        return pl.pallas_call(
            functools.partial(merge_kernel, heads, skip, goals),
            out_shape=shapes,
            in_specs=[VMEM] * 2,
            out_specs=[VMEM] * len(shapes),
            compiler_params=params(8),
            name="merge",
        )(keep, got)

    def halved(keep, got):
        shape = (keep.shape[0], slabs, keep.shape[2] // 2, LANES)
        return merge(keep, got, 0, [None] * keep.shape[0], [f32(*shape), bf16(*shape)])

    def sorted_by(keep, got, skip, offsets, bit):
        sends = [offset for offset in offsets if offset & bit]
        keeps = [offset for offset in offsets if not offset & bit]
        goals = [
            (0, sends.index(o)) if o in sends else (1, keeps.index(o)) for o in offsets]
        shape = lambda count: (count, slabs, group, LANES)
        shapes = [bf16(*shape(len(sends)))] + ([f32(*shape(len(keeps)))] if keeps else [])
        return merge(keep, got, skip, goals, shapes), keeps

    ctx_bits = list(bits_of("ctx"))[::-1]
    req_bits = list(bits_of("req"))[::-1]
    table = page_table.reshape(-1)
    send, q_own = lax.optimization_barrier((send, q_own))
    got = swap(send, "ctx", ctx_bits[0])
    t, top, *staged = pl.pallas_call(
        functools.partial(score_kernel, (heads, page_rows, pages_dev, sub, pieces)),
        out_shape=(f32(req_dev, sub, columns), f32(req_dev, sub, LANES)) + score_out,
        in_specs=[SMEM] * 2 + [VMEM] * 2 + score_specs,
        out_specs=(VMEM,) * (2 + len(score_out)),
        scratch_shapes=score_scratch,
        compiler_params=params(4),
        cost_estimate=pl.CostEstimate(
            flops=2 * req_dev * rows * columns * LANES, transcendentals=0,
            bytes_accessed=kv_pool.size),
        name="scores",
    )(table, context_len, q_own, kb, *score_in)
    if staged:
        vb = staged[0].reshape(pool_slots, page_rows, LANES)
    got, top = lax.optimization_barrier((got, top))
    for bit in ctx_bits[1:]:
        keep, send = halved(keep, got)
        send, top = lax.optimization_barrier((send, top))
        got = swap(send, "ctx", bit)
    own_keep, own_send = pl.pallas_call(
        functools.partial(value_kernel, (heads, page_rows, pages_dev, sub)),
        out_shape=(f32(1, slabs, left, LANES), bf16(1, slabs, left, LANES)),
        in_specs=[SMEM] + [VMEM] * 6,
        out_specs=(VMEM,) * 2,
        scratch_shapes=[
            pltpu.VMEM((req_dev, rows, LANES), jnp.float32),
            pltpu.VMEM((req_dev, sub, LANES), jnp.float32)],
        compiler_params=params(4),
        cost_estimate=pl.CostEstimate(
            flops=2 * req_dev * rows * columns * LANES, transcendentals=req_dev * sub * columns,
            bytes_accessed=kv_pool.size),
        name="values",
    )(table, t, top, vb, acc, ftop, ftot)
    own_got = swap(own_send, "ctx", ctx_bits[0])
    got, own_keep = lax.optimization_barrier((got, own_keep))
    offsets, skip, arrived = list(range(1, n_req)), 0, []
    for bit in req_bits:
        if offsets:
            (send, *kept), offsets = sorted_by(keep, got, skip, offsets, bit)
        keep = kept[0] if kept else None
        if bit == req_bits[0]:
            for ctx_bit in ctx_bits[1:]:
                own_keep, own_send = halved(own_keep, own_got)
                own_got = swap(own_send, "ctx", ctx_bit)
        got = swap(send, "req", bit)
        arrived.append(got)
        skip = 1
    return pl.pallas_call(
        last_kernel,
        out_shape=bf16(req_dev, heads, group, LANES),
        in_specs=[VMEM] * (2 + len(arrived)),
        out_specs=VMEM,
        compiler_params=params(8),
        name="last",
    )(own_keep, own_got, *arrived)


def solution(mesh):
    placed = (
        P("req", "kvh", "ctx", None),
        P(("req", "ctx"), None, "kvh", None),
        P("req", "ctx"),
        P("req"),
        P(("req", "ctx"), None, "kvh", None),
        P(("req", "ctx")),
    )
    return jax.shard_map(
        local, mesh=mesh, in_specs=placed, out_specs=P("req", "kvh", "ctx", None), check_vma=False
    )
```

```python
import functools
import math

import jax
import jax.numpy as jnp
from jax import lax
from jax.experimental import pallas as pl
from jax.experimental.pallas import tpu as pltpu
from jax.sharding import PartitionSpec as P

NEG = -1e30
CAP = 2
LANES = 128
SCALE = math.log2(math.e) / math.sqrt(LANES)
SCORE_WIDE = 256
VALUE_WIDE = 512
VMEM = pl.BlockSpec(memory_space=pltpu.VMEM)
SMEM = pl.BlockSpec(memory_space=pltpu.SMEM)
HBM = pl.BlockSpec(memory_space=pltpu.HBM)


def swap(value, axis, bit):
    return lax.ppermute(value, axis, [(n, n ^ bit) for n in range(lax.axis_size(axis))])


def bits_of(axis):
    bit = lax.axis_size(axis) // 2
    while bit:
        yield bit
        bit //= 2


def half_copies(pool_ref, target, sem, half, pieces, tokens=None):
    each = pool_ref.shape[0] // pieces
    tokens = tokens or pl.ds(0, pool_ref.shape[1])
    return [
        pltpu.make_async_copy(
            pool_ref.at[pl.ds(n * each, each), tokens, :, pl.ds(half * LANES, LANES)],
            target.at[pl.ds(n * each, each)], sem.at[n])
        for n in range(pieces)
    ]


class ValueCopies:
    def __init__(self, refs, part, pieces):
        self.copies = []
        if pieces:
            pool_ref, target, sem = refs
            count = pool_ref.shape[1] // 2
            self.copies = half_copies(
                pool_ref, target, sem, 1, pieces, pl.ds(part * count, count))

    def start(self):
        for one in self.copies:
            one.start()

    def wait(self):
        for one in self.copies:
            one.wait()


def stage_fresh_kernel(fresh_ref, kf, vf, sem):
    copies = []
    for half, to in enumerate((kf, vf)):
        copies += half_copies(fresh_ref, to, sem.at[half], half, sem.shape[1])
    for one in copies:
        one.start()
    for one in copies:
        one.wait()


def stage_keys_kernel(
    n_ctx, slots, bucket_hbm, pool_ref, kb, slots_ref, counts_ref, bucket_ref, sem, bucket_sem,
):
    listed = pltpu.make_async_copy(bucket_hbm, bucket_ref, bucket_sem)
    copies = half_copies(pool_ref, kb, sem, 0, sem.shape[0])
    listed.start()
    for one in copies:
        one.start()
    listed.wait()
    list_fresh(n_ctx, slots, bucket_ref, slots_ref, counts_ref)
    for one in copies:
        one.wait()


def list_kernel(n_ctx, slots, bucket_ref, slots_ref, counts_ref):
    list_fresh(n_ctx, slots, bucket_ref, slots_ref, counts_ref)


def list_fresh(n_ctx, slots, bucket_ref, slots_ref, counts_ref):
    for n in range(counts_ref.shape[0]):
        counts_ref[n] = 0
    for n in range(slots_ref.shape[0]):
        slots_ref[n] = 0

    def put(page, _):
        request = bucket_ref[page] >> (n_ctx.bit_length() - 1)
        count = counts_ref[request]
        slots_ref[request * slots + count] = page
        counts_ref[request] = count + 1
        return 0

    lax.fori_loop(0, bucket_ref.shape[0], put, 0, unroll=16)


def class_reduce(x, op, heads):
    step = heads
    while step < LANES:
        x = op(x, pltpu.roll(x, step, 1))
        step *= 2
    return x


def pages_of(refs, table_ref, first, count):
    pages = [table_ref[first + n] for n in range(count)]
    return jnp.concatenate([ref[page] for page in pages for ref in refs], axis=0)


def score_parts(q, keys, lane, limit, first, heads, sub):
    s = lax.dot_general(q, keys, (((1,), (1,)), ((), ())), preferred_element_type=jnp.float32)
    out = []
    for j in range(s.shape[1] // LANES):
        part = s[:, j * LANES:(j + 1) * LANES]
        one = part[:sub]
        for h in range(1, heads):
            one = jnp.where(lane % heads == h, part[h * sub:(h + 1) * sub], one)
        out.append(jnp.where(lane < limit - (first + j * LANES), one * SCALE, NEG))
    return out


def spread(p, onehots):
    p = p.astype(jnp.bfloat16)
    return jnp.concatenate([p * one for one in onehots], axis=0)


def rows_of(x, h):
    return jnp.broadcast_to(x[:, h:h + 1], x.shape)


def fold_max(parts):
    top = parts[0]
    for part in parts[1:]:
        top = jnp.maximum(top, part)
    return top


def score_request(dims, i, table_ref, len_ref, q_ref, kb, t_ref, top_ref, at):
    heads, page_rows, pages_dev, sub = dims
    columns = pages_dev * page_rows
    wide = min(SCORE_WIDE, columns)
    per = wide // page_rows
    lane = lax.broadcasted_iota(jnp.int32, (sub, LANES), 1)
    top = jnp.full((sub, LANES), NEG, jnp.float32)
    limit = len_ref[i] * heads - lax.axis_index("ctx") * columns
    for c in range(columns // wide):
        keys = pages_of([kb], table_ref, i * pages_dev + c * per, per)
        parts = score_parts(q_ref[0, i], keys, lane, limit, c * wide, heads, sub)
        for j, part in enumerate(parts):
            t_ref[at, :, c * wide + j * LANES:c * wide + (j + 1) * LANES] = part
        top = jnp.maximum(top, fold_max(parts))
    top_ref[at] = top


def value_request(dims, i, table_ref, t_ref, top_ref, at, vbs, acc_ref, tot_ref):
    heads, page_rows, pages_dev, sub = dims
    columns = pages_dev * page_rows
    wide = min(VALUE_WIDE, columns)
    per = wide // page_rows
    lane = lax.broadcasted_iota(jnp.int32, (sub, LANES), 1)
    onehots = [(lane % heads == h).astype(jnp.bfloat16) for h in range(heads)]
    tot = jnp.zeros((sub, LANES), jnp.float32)
    acc = jnp.zeros((heads * sub, LANES), jnp.float32)
    top = top_ref[at]
    for c in range(columns // wide):
        weights = []
        for j in range(wide // LANES):
            where = c * wide + j * LANES
            p = jnp.exp2(t_ref[at, :, where:where + LANES] - top)
            tot = tot + p
            weights.append(spread(p, onehots))
        values = pages_of(vbs, table_ref, i * pages_dev + c * per, per)
        acc = acc + jnp.dot(
            jnp.concatenate(weights, axis=1), values, preferred_element_type=jnp.float32)
    acc_ref[at] = acc
    tot_ref[at] = tot


def reduce_rows(ref, op, heads):
    flat = ref[...].reshape(ref.shape[0] * ref.shape[1], LANES)
    return class_reduce(flat, op, heads)


def first_kernel(dims, pieces, table_ref, len_ref, q_ref, kb, *refs):
    refs = list(refs)
    pool = [refs.pop(0)] if pieces else []
    t_ref, top_ref, *refs = refs
    copies = ValueCopies(pool + refs, 1, pieces)
    copies.start()

    def step(i, _):
        score_request(dims, i, table_ref, len_ref, q_ref, kb, t_ref, top_ref, i)
        return 0

    lax.fori_loop(0, t_ref.shape[0], step, 0)
    top_ref[...] = reduce_rows(top_ref, jnp.maximum, dims[0]).reshape(top_ref.shape)
    copies.wait()


def middle_kernel(dims, table_ref, len_ref, q_ref, kb, t_ref, top_ref, *refs):
    *vbs, later_ref, later_top_ref, acc_ref, tot_ref = refs
    half = t_ref.shape[0]

    def step(i, _):
        score_request(
            dims, half + i, table_ref, len_ref, q_ref, kb, later_ref, later_top_ref, i)
        value_request(dims, i, table_ref, t_ref, top_ref, i, vbs, acc_ref, tot_ref)
        return 0

    lax.fori_loop(0, half, step, 0)
    later_top_ref[...] = reduce_rows(
        later_top_ref, jnp.maximum, dims[0]).reshape(later_top_ref.shape)


def second_kernel(
    dims, table_ref, t_ref, top_ref, first_top_ref, first_acc_ref, first_tot_ref, facc_ref,
    ftop_ref, ftot_ref, *refs,
):
    *vbs, keep_ref, send_ref, acc_s, tot_s = refs
    heads, page_rows, pages_dev, sub = dims
    half = t_ref.shape[0]
    req_dev = ftop_ref.shape[0]

    def step(i, _):
        value_request(dims, half + i, table_ref, t_ref, top_ref, i, vbs, acc_s, tot_s)
        return 0

    lax.fori_loop(0, half, step, 0)
    flat = (req_dev * sub, LANES)
    tots = jnp.concatenate(
        [reduce_rows(ref, jnp.add, heads) for ref in (first_tot_ref, tot_s)], axis=0)
    top = jnp.concatenate(
        [ref[...].reshape(half * sub, LANES) for ref in (first_top_ref, top_ref)], axis=0)
    ftop = ftop_ref[...].reshape(flat)
    both = jnp.maximum(top, ftop)
    fade, ffade = jnp.exp2(top - both), jnp.exp2(ftop - both)
    tots = tots * fade + ftot_ref[...].reshape(flat) * ffade
    fade, ffade = fade / tots, ffade / tots
    lses = both + jnp.log2(tots)
    for i in range(req_dev):
        acc_ref = first_acc_ref if i < half else acc_s
        rows = slice(i * sub, (i + 1) * sub)
        for h in range(heads):
            part = slice(h * sub, (h + 1) * sub)
            some = acc_ref[i % half, part, :] * rows_of(fade[rows], h)
            some = some + facc_ref[i, part, :] * rows_of(ffade[rows], h)
            put_rows(keep_ref, send_ref, (0, i * heads + h), some)
    lse = by_request(lses, heads, sub, range(req_dev))
    put_rows(keep_ref, send_ref, (0, req_dev * heads), lse, heads)


def put_rows(keep_ref, send_ref, place, value, heads=0):
    half = value.shape[0] // 2
    send = value[half:]
    keep_ref[place] = value[:half]
    send_ref[place] = pieces_of(send, heads) if heads else send.astype(jnp.bfloat16)


def by_request(lses, heads, sub, requests):
    lane = lax.broadcasted_iota(jnp.int32, (sub, LANES), 1)
    out = jnp.zeros((sub, LANES), jnp.float32)
    for i, n in enumerate(requests):
        out = jnp.where(lane // (4 * heads) == i, lses[n * sub:(n + 1) * sub], out)
    return out


def fresh_kernel(dims, pieces, slots_ref, counts_ref, q_ref, kf, vf, *refs):
    heads, page_rows, slots, sub = dims
    n_req, req_dev = q_ref.shape[:2]
    refs = list(refs)
    pool = [refs.pop(0)] if pieces else []
    keep_ref, send_ref, acc_ref, top_ref, tot_ref, *refs = refs
    target = [refs.pop(0)] if pieces else []
    t_s, p_s, *sem = refs
    copies = ValueCopies(pool + target + sem, 0, pieces)
    copies.start()
    lane = lax.broadcasted_iota(jnp.int32, (sub, LANES), 1)
    onehots = [(lane % heads == h).astype(jnp.bfloat16) for h in range(heads)]
    columns = slots * page_rows
    wide = min(SCORE_WIDE, columns)
    per = wide // page_rows
    own = lax.axis_index("req")
    requests = [(own ^ k) * req_dev + i for k in range(n_req) for i in range(req_dev)]
    n_reqs = len(requests)
    tops = []
    for n, request in enumerate(requests):
        limit = counts_ref[request] * page_rows
        top = jnp.full((sub, LANES), NEG, jnp.float32)
        for c in range(columns // wide):
            keys = pages_of([kf], slots_ref, request * slots + c * per, per)
            parts = score_parts(q_ref[n // req_dev, n % req_dev], keys, lane, limit, c * wide, heads, sub)
            for j, part in enumerate(parts):
                t_s[n, :, c * wide + j * LANES:c * wide + (j + 1) * LANES] = part
            top = jnp.maximum(top, fold_max(parts))
        tops.append(top)
    tops = class_reduce(jnp.concatenate(tops, axis=0), jnp.maximum, heads)
    tots = []
    for n in range(n_reqs):
        tot = jnp.zeros((sub, LANES), jnp.float32)
        for j in range(columns // LANES):
            p = jnp.exp2(
                t_s[n, :, j * LANES:(j + 1) * LANES] - tops[n * sub:(n + 1) * sub])
            tot = tot + p
            p_s[n, :, j * LANES:(j + 1) * LANES] = spread(p, onehots)
        tots.append(tot)
    tots = class_reduce(jnp.concatenate(tots, axis=0), jnp.add, heads)
    whole = 1.0 / tots
    lses = tops + jnp.log2(tots)
    for n, request in enumerate(requests):
        values = pages_of([vf], slots_ref, request * slots, slots)
        acc = jnp.dot(p_s[n], values, preferred_element_type=jnp.float32)
        rows = slice(n * sub, (n + 1) * sub)
        block, i = n // req_dev - 1, n % req_dev
        if block < 0:
            acc_ref[i] = acc
            top_ref[i] = tops[rows]
            tot_ref[i] = tots[rows]
            continue
        for h in range(heads):
            some = acc[h * sub:(h + 1) * sub] * rows_of(whole[rows], h)
            put_rows(keep_ref, send_ref, (block, i * heads + h), some)
    for block in range(n_req - 1):
        first = (block + 1) * req_dev
        lse = by_request(lses, heads, sub, range(first, first + req_dev))
        put_rows(keep_ref, send_ref, (block, req_dev * heads), lse, heads)
    copies.wait()


def pieces_of(lse, heads):
    lane = lax.broadcasted_iota(jnp.int32, lse.shape, 1)
    kind = lane % (4 * heads) // heads
    high = lse.astype(jnp.bfloat16).astype(jnp.float32)
    rest = lse - high
    mid = rest.astype(jnp.bfloat16).astype(jnp.float32)
    both = jnp.where(kind == 1, mid, rest - mid)
    return jnp.where(kind == 0, high, both).astype(jnp.bfloat16)


def whole_of(pieces, heads):
    x = pieces.astype(jnp.float32)
    lane = lax.broadcasted_iota(jnp.int32, x.shape, 1)
    kind = lane % (4 * heads) // heads
    x = x + pltpu.roll(x, LANES - heads, 1) + pltpu.roll(x, LANES - 2 * heads, 1)
    same = x
    for m in (1, 2):
        same = jnp.where(kind == m, pltpu.roll(x, m * heads, 1), same)
    return same


def merge_kernel(heads, skip, goals, keep_ref, got_ref, *outs):
    blocks, slabs, rows, _ = keep_ref.shape
    slabs -= 1

    def put(block, slab, value, coded=0):
        if goals[block] is None:
            put_rows(outs[0], outs[1], (block, slab), value, coded)
        else:
            which, place = goals[block]
            if outs[which].dtype == jnp.bfloat16:
                value = pieces_of(value, coded) if coded else value.astype(jnp.bfloat16)
            outs[which][place, slab] = value

    for block in range(blocks):
        own = keep_ref[block, slabs]
        other = whole_of(got_ref[block + skip, slabs], heads)
        top = jnp.maximum(own, other)
        share = jnp.exp2(own - top)
        tot = share + jnp.exp2(other - top)
        share = share / tot
        for slab in range(slabs):
            at = slab // heads * 4 * heads + slab % heads
            part = jnp.broadcast_to(share[:, at:at + 1], (rows, LANES))
            kept = keep_ref[block, slab]
            got = got_ref[block + skip, slab].astype(jnp.float32)
            put(block, slab, part * kept + (1.0 - part) * got)
        put(block, slabs, top + jnp.log2(tot), heads)


def last_kernel(keep_ref, *refs):
    *got_refs, out_ref = refs
    req_dev, heads, group, _ = out_ref.shape
    slabs = req_dev * heads
    parts = [keep_ref.at[0]] + [ref.at[0] for ref in got_refs]
    lses = [keep_ref[0, slabs]] + [whole_of(ref[0, slabs], heads) for ref in got_refs]
    top = fold_max(lses)
    shares = [jnp.exp2(lse - top) for lse in lses]
    tot = shares[0]
    for share in shares[1:]:
        tot = tot + share
    shares = [share / tot for share in shares]
    for slab in range(slabs):
        at = slab // heads * 4 * heads + slab % heads
        total = jnp.zeros((group, LANES), jnp.float32)
        for part, share in zip(parts, shares):
            total = total + part[slab].astype(jnp.float32) * jnp.broadcast_to(
                share[:, at:at + 1], (group, LANES))
        out_ref[slab // heads, slab % heads] = total.astype(jnp.bfloat16)


def params(mib):
    return pltpu.CompilerParams(vmem_limit_bytes=mib * 2**20)


def local(query, kv_pool, page_table, context_len, fresh_kv, fresh_bucket):
    n_ctx = lax.axis_size("ctx")
    n_req = lax.axis_size("req")
    req_dev, heads, group, head_dim = query.shape
    pool_slots, page = kv_pool.shape[:2]
    new_dev = fresh_kv.shape[0]
    pages_dev = page_table.shape[1]
    n_reqs = n_req * req_dev
    slots = CAP * n_ctx
    sub = n_ctx * group
    rows = heads * sub
    page_rows = page * heads

    smem = lambda count: jax.ShapeDtypeStruct((count,), jnp.int32)
    bf16 = lambda *shape: jax.ShapeDtypeStruct(shape, jnp.bfloat16)
    f32 = lambda *shape: jax.ShapeDtypeStruct(shape, jnp.float32)
    columns = pages_dev * page_rows
    split = heads % 4 == 0
    pieces = 8 if split else 0

    reqs = [swap(query, "req", k) for k in range(n_req - 1, 0, -1)][::-1]
    first, *others = bits_of("ctx")
    if split:
        in_hbm = lambda a: pltpu.with_memory_space_constraint(a, pltpu.HBM)
        pool = in_hbm(kv_pool)
        half = lambda count: bf16(count, page, heads, LANES)
        kf, vf = pl.pallas_call(
            stage_fresh_kernel,
            out_shape=(half(new_dev), half(new_dev)),
            in_specs=[HBM],
            out_specs=(VMEM,) * 2,
            scratch_shapes=[pltpu.SemaphoreType.DMA((2, 4))],
            compiler_params=params(2),
            cost_estimate=pl.CostEstimate(
                flops=0, transcendentals=0, bytes_accessed=4 * fresh_kv.size),
            name="stage_fresh",
        )(in_hbm(fresh_kv))
        bucket, kf, *reqs = lax.optimization_barrier((in_hbm(fresh_bucket), kf, *reqs))
        near = jnp.stack([query] + reqs)[None]
        arrived = swap(near, "ctx", first)
        kb, slot_table, counts = pl.pallas_call(
            functools.partial(stage_keys_kernel, n_ctx, slots),
            out_shape=(half(pool_slots), smem(n_reqs * slots), smem(n_reqs)),
            in_specs=[HBM] * 2,
            out_specs=(VMEM, SMEM, SMEM),
            scratch_shapes=[
                pltpu.SMEM((new_dev,), jnp.int32), pltpu.SemaphoreType.DMA((pieces,)),
                pltpu.SemaphoreType.DMA],
            compiler_params=params(2),
            cost_estimate=pl.CostEstimate(
                flops=0, transcendentals=0, bytes_accessed=2 * kv_pool.size),
            name="stage_keys",
        )(in_hbm(bucket), pool)
        arrived, counts = lax.optimization_barrier((arrived, counts))
        kb, kf, vf = (a.reshape(a.shape[0], page_rows, LANES) for a in (kb, kf, vf))
        value_in, value_specs = (pool,), [HBM]
        value_out = (bf16(pool_slots, page // 2, heads, LANES),)
        value_scratch = [pltpu.SemaphoreType.DMA((pieces,))]
    else:
        kb, vb, kf, vf = (
            a[..., h * LANES:(h + 1) * LANES].reshape(a.shape[0], page_rows, LANES)
            for a in (kv_pool, fresh_kv) for h in (0, 1)
        )
        slot_table, counts = pl.pallas_call(
            functools.partial(list_kernel, n_ctx, slots),
            out_shape=(smem(n_reqs * slots), smem(n_reqs)),
            in_specs=[SMEM],
            out_specs=(SMEM,) * 2,
            name="list",
        )(fresh_bucket)
        value_in, value_specs, value_out, value_scratch = (), [], (), []
        near = jnp.stack([query] + reqs)[None]
        arrived = swap(near, "ctx", first)

    near = jnp.concatenate([near, arrived])
    for bit in others:
        near = jnp.concatenate([near, swap(near, "ctx", bit)])
    queries = near.transpose(1, 2, 3, 0, 4, 5).reshape(n_req, req_dev, rows, head_dim)

    slabs = req_dev * heads + 1
    left = sub // 2
    keep, send, facc, ftop, ftot, *vbs = pl.pallas_call(
        functools.partial(fresh_kernel, (heads, page_rows, slots, sub), pieces),
        out_shape=(
            f32(n_req - 1, slabs, left, LANES), bf16(n_req - 1, slabs, left, LANES),
            f32(req_dev, rows, LANES), f32(req_dev, sub, LANES), f32(req_dev, sub, LANES),
        ) + value_out,
        in_specs=[SMEM] * 2 + [VMEM] * 3 + value_specs,
        out_specs=(VMEM,) * (5 + len(value_out)),
        scratch_shapes=[
            pltpu.VMEM((n_reqs, sub, slots * page_rows), jnp.float32),
            pltpu.VMEM((n_reqs, rows, slots * page_rows), jnp.bfloat16),
        ] + value_scratch,
        compiler_params=params(8),
        cost_estimate=pl.CostEstimate(
            flops=4 * n_reqs * rows * slots * page_rows * LANES,
            transcendentals=n_reqs * sub * slots * page_rows, bytes_accessed=2 * fresh_kv.size),
        name="fresh",
    )(slot_table, counts, queries, kf, vf, *value_in)

    def merge(keep, got, skip, goals, shapes):
        return pl.pallas_call(
            functools.partial(merge_kernel, heads, skip, goals),
            out_shape=shapes,
            in_specs=[VMEM] * 2,
            out_specs=[VMEM] * len(shapes),
            compiler_params=params(8),
            name="merge",
        )(keep, got)

    def halved(keep, got):
        shape = (keep.shape[0], slabs, keep.shape[2] // 2, LANES)
        return merge(keep, got, 0, [None] * keep.shape[0], [f32(*shape), bf16(*shape)])

    def sorted_by(keep, got, skip, offsets, bit):
        sends = [offset for offset in offsets if offset & bit]
        keeps = [offset for offset in offsets if not offset & bit]
        goals = [
            (0, sends.index(o)) if o in sends else (1, keeps.index(o)) for o in offsets]
        shape = lambda count: (count, slabs, group, LANES)
        shapes = [bf16(*shape(len(sends)))] + ([f32(*shape(len(keeps)))] if keeps else [])
        return merge(keep, got, skip, goals, shapes), keeps

    ctx_bits = list(bits_of("ctx"))[::-1]
    req_bits = list(bits_of("req"))[::-1]
    dims = (heads, page_rows, pages_dev, sub)
    table = page_table.reshape(-1)
    part = req_dev // 2
    cost = lambda scores, values: pl.CostEstimate(
        flops=2 * (scores + values) * rows * columns * LANES,
        transcendentals=values * sub * columns,
        bytes_accessed=(scores + values) * columns * LANES * 2)
    send, queries = lax.optimization_barrier((send, queries))
    got = swap(send, "ctx", ctx_bits[0])
    t, top, *more = pl.pallas_call(
        functools.partial(first_kernel, dims, pieces),
        out_shape=(f32(part, sub, columns), f32(part, sub, LANES)) + value_out,
        in_specs=[SMEM] * 2 + [VMEM] * 2 + value_specs,
        out_specs=(VMEM,) * (2 + len(value_out)),
        scratch_shapes=value_scratch,
        compiler_params=params(4),
        cost_estimate=cost(part, 0),
        name="first",
    )(table, context_len, queries, kb, *value_in)
    vbs = [a.reshape(a.shape[0], -1, LANES) for a in vbs + more] if split else [vb]
    got, top = lax.optimization_barrier((got, top))
    for bit in ctx_bits[1:]:
        keep, send = halved(keep, got)
        send, top = lax.optimization_barrier((send, top))
        got = swap(send, "ctx", bit)
    later, later_top, acc, tot = pl.pallas_call(
        functools.partial(middle_kernel, dims),
        out_shape=(
            f32(part, sub, columns), f32(part, sub, LANES), f32(part, rows, LANES),
            f32(part, sub, LANES)),
        in_specs=[SMEM] * 2 + [VMEM] * (4 + len(vbs)),
        out_specs=(VMEM,) * 4,
        compiler_params=params(4),
        cost_estimate=cost(part, part),
        name="middle",
    )(table, context_len, queries, kb, t, top, *vbs)
    got, later_top = lax.optimization_barrier((got, later_top))
    offsets = list(range(1, n_req))
    (send, *kept), offsets = sorted_by(keep, got, 0, offsets, req_bits[0])
    send, later_top = lax.optimization_barrier((send, later_top))
    got = swap(send, "req", req_bits[0])
    arrived = [got]
    own_keep, own_send = pl.pallas_call(
        functools.partial(second_kernel, dims),
        out_shape=(f32(1, slabs, left, LANES), bf16(1, slabs, left, LANES)),
        in_specs=[SMEM] + [VMEM] * (8 + len(vbs)),
        out_specs=(VMEM,) * 2,
        scratch_shapes=[
            pltpu.VMEM((part, rows, LANES), jnp.float32),
            pltpu.VMEM((part, sub, LANES), jnp.float32)],
        compiler_params=params(4),
        cost_estimate=cost(0, part),
        name="second",
    )(table, later, later_top, top, acc, tot, facc, ftop, ftot, *vbs)
    got, own_send = lax.optimization_barrier((got, own_send))
    own_got = swap(own_send, "ctx", ctx_bits[0])
    for bit in req_bits[1:]:
        (send, *kept), offsets = sorted_by(kept[0], got, 1, offsets, bit)
        got = swap(send, "req", bit)
        arrived.append(got)
    for bit in ctx_bits[1:]:
        own_keep, own_send = halved(own_keep, own_got)
        own_got = swap(own_send, "ctx", bit)
    return pl.pallas_call(
        last_kernel,
        out_shape=bf16(req_dev, heads, group, LANES),
        in_specs=[VMEM] * (2 + len(arrived)),
        out_specs=VMEM,
        compiler_params=params(8),
        name="last",
    )(own_keep, own_got, *arrived)


def solution(mesh):
    placed = (
        P("req", "kvh", "ctx", None),
        P(("req", "ctx"), None, "kvh", None),
        P("req", "ctx"),
        P("req"),
        P(("req", "ctx"), None, "kvh", None),
        P(("req", "ctx")),
    )
    return jax.shard_map(
        local, mesh=mesh, in_specs=placed, out_specs=P("req", "kvh", "ctx", None), check_vma=False
    )
```

```python
import functools
import math

import jax
import jax.numpy as jnp
from jax import lax
from jax.experimental import pallas as pl
from jax.experimental.pallas import tpu as pltpu
from jax.sharding import PartitionSpec as P

NEG = -1e30
CAP = 2
LANES = 128
SCALE = math.log2(math.e) / math.sqrt(LANES)
SCORE_WIDE = 256
VALUE_WIDE = 512
VMEM = pl.BlockSpec(memory_space=pltpu.VMEM)
SMEM = pl.BlockSpec(memory_space=pltpu.SMEM)
HBM = pl.BlockSpec(memory_space=pltpu.HBM)


def swap(value, axis, bit):
    return lax.ppermute(value, axis, [(n, n ^ bit) for n in range(lax.axis_size(axis))])


def bits_of(axis):
    bit = lax.axis_size(axis) // 2
    while bit:
        yield bit
        bit //= 2


def half_copies(pool_ref, target, sem, half, pieces, tokens=None):
    each = pool_ref.shape[0] // pieces
    tokens = tokens or pl.ds(0, pool_ref.shape[1])
    return [
        pltpu.make_async_copy(
            pool_ref.at[pl.ds(n * each, each), tokens, :, pl.ds(half * LANES, LANES)],
            target.at[pl.ds(n * each, each)], sem.at[n])
        for n in range(pieces)
    ]


class ValueCopies:
    def __init__(self, refs, part, pieces):
        self.copies = []
        if pieces:
            pool_ref, target, sem = refs
            count = pool_ref.shape[1] // 2
            self.copies = half_copies(
                pool_ref, target, sem, 1, pieces, pl.ds(part * count, count))

    def start(self):
        for one in self.copies:
            one.start()

    def wait(self):
        for one in self.copies:
            one.wait()


def stage_fresh_kernel(fresh_ref, kf, vf, sem):
    copies = []
    for half, to in enumerate((kf, vf)):
        copies += half_copies(fresh_ref, to, sem.at[half], half, sem.shape[1])
    for one in copies:
        one.start()
    for one in copies:
        one.wait()


def stage_keys_kernel(
    n_ctx, slots, bucket_hbm, pool_ref, kb, slots_ref, counts_ref, bucket_ref, sem, bucket_sem,
):
    listed = pltpu.make_async_copy(bucket_hbm, bucket_ref, bucket_sem)
    copies = half_copies(pool_ref, kb, sem, 0, sem.shape[0])
    listed.start()
    for one in copies:
        one.start()
    listed.wait()
    list_fresh(n_ctx, slots, bucket_ref, slots_ref, counts_ref)
    for one in copies:
        one.wait()


def list_kernel(n_ctx, slots, bucket_ref, slots_ref, counts_ref):
    list_fresh(n_ctx, slots, bucket_ref, slots_ref, counts_ref)


def list_fresh(n_ctx, slots, bucket_ref, slots_ref, counts_ref):
    for n in range(counts_ref.shape[0]):
        counts_ref[n] = 0
    for n in range(slots_ref.shape[0]):
        slots_ref[n] = 0

    def put(page, _):
        request = bucket_ref[page] >> (n_ctx.bit_length() - 1)
        count = counts_ref[request]
        slots_ref[request * slots + count] = page
        counts_ref[request] = count + 1
        return 0

    lax.fori_loop(0, bucket_ref.shape[0], put, 0, unroll=16)


def class_reduce(x, op, heads):
    step = heads
    while step < LANES:
        x = op(x, pltpu.roll(x, step, 1))
        step *= 2
    return x


def pages_of(refs, table_ref, first, count):
    pages = [table_ref[first + n] for n in range(count)]
    return jnp.concatenate([ref[page] for page in pages for ref in refs], axis=0)


def score_parts(q, keys, lane, limit, first, heads, sub):
    s = lax.dot_general(q, keys, (((1,), (1,)), ((), ())), preferred_element_type=jnp.float32)
    out = []
    for j in range(s.shape[1] // LANES):
        part = s[:, j * LANES:(j + 1) * LANES]
        one = part[:sub]
        for h in range(1, heads):
            one = jnp.where(lane % heads == h, part[h * sub:(h + 1) * sub], one)
        out.append(jnp.where(lane < limit - (first + j * LANES), one * SCALE, NEG))
    return out


def spread(p, onehots):
    p = p.astype(jnp.bfloat16)
    return jnp.concatenate([p * one for one in onehots], axis=0)


def rows_of(x, h):
    return jnp.broadcast_to(x[:, h:h + 1], x.shape)


def fold_max(parts):
    top = parts[0]
    for part in parts[1:]:
        top = jnp.maximum(top, part)
    return top


def score_request(dims, i, table_ref, len_ref, q_ref, kb, t_ref, top_ref, at):
    heads, page_rows, pages_dev, sub = dims
    columns = pages_dev * page_rows
    wide = min(SCORE_WIDE, columns)
    per = wide // page_rows
    lane = lax.broadcasted_iota(jnp.int32, (sub, LANES), 1)
    top = jnp.full((sub, LANES), NEG, jnp.float32)
    limit = len_ref[i] * heads - lax.axis_index("ctx") * columns
    for c in range(columns // wide):
        keys = pages_of([kb], table_ref, i * pages_dev + c * per, per)
        parts = score_parts(q_ref[i], keys, lane, limit, c * wide, heads, sub)
        for j, part in enumerate(parts):
            t_ref[at, :, c * wide + j * LANES:c * wide + (j + 1) * LANES] = part
        top = jnp.maximum(top, fold_max(parts))
    top_ref[at] = top


def value_request(dims, i, table_ref, t_ref, top_ref, at, vbs, acc_ref, tot_ref):
    heads, page_rows, pages_dev, sub = dims
    columns = pages_dev * page_rows
    wide = min(VALUE_WIDE, columns)
    per = wide // page_rows
    lane = lax.broadcasted_iota(jnp.int32, (sub, LANES), 1)
    onehots = [(lane % heads == h).astype(jnp.bfloat16) for h in range(heads)]
    tot = jnp.zeros((sub, LANES), jnp.float32)
    acc = jnp.zeros((heads * sub, LANES), jnp.float32)
    top = top_ref[at]
    for c in range(columns // wide):
        weights = []
        for j in range(wide // LANES):
            where = c * wide + j * LANES
            p = jnp.exp2(t_ref[at, :, where:where + LANES] - top)
            tot = tot + p
            weights.append(spread(p, onehots))
        values = pages_of(vbs, table_ref, i * pages_dev + c * per, per)
        acc = acc + jnp.dot(
            jnp.concatenate(weights, axis=1), values, preferred_element_type=jnp.float32)
    acc_ref[at] = acc
    tot_ref[at] = tot


def reduce_rows(ref, op, heads):
    flat = ref[...].reshape(ref.shape[0] * ref.shape[1], LANES)
    return class_reduce(flat, op, heads)


def first_kernel(dims, pieces, table_ref, len_ref, q_ref, kb, *refs):
    refs = list(refs)
    pool = [refs.pop(0)] if pieces else []
    t_ref, top_ref, *refs = refs
    copies = ValueCopies(pool + refs, 1, pieces)
    copies.start()

    def step(i, _):
        score_request(dims, i, table_ref, len_ref, q_ref, kb, t_ref, top_ref, i)
        return 0

    lax.fori_loop(0, t_ref.shape[0], step, 0)
    top_ref[...] = reduce_rows(top_ref, jnp.maximum, dims[0]).reshape(top_ref.shape)
    copies.wait()


def middle_kernel(dims, table_ref, len_ref, q_ref, kb, t_ref, top_ref, *refs):
    *vbs, later_ref, later_top_ref, acc_ref, tot_ref = refs
    half = t_ref.shape[0]

    def step(i, _):
        score_request(
            dims, half + i, table_ref, len_ref, q_ref, kb, later_ref, later_top_ref, i)
        value_request(dims, i, table_ref, t_ref, top_ref, i, vbs, acc_ref, tot_ref)
        return 0

    lax.fori_loop(0, half, step, 0)
    later_top_ref[...] = reduce_rows(
        later_top_ref, jnp.maximum, dims[0]).reshape(later_top_ref.shape)


def second_kernel(
    dims, table_ref, t_ref, top_ref, first_top_ref, first_acc_ref, first_tot_ref, facc_ref,
    ftop_ref, ftot_ref, *refs,
):
    *vbs, keep_ref, send_ref, acc_s, tot_s = refs
    heads, page_rows, pages_dev, sub = dims
    half = t_ref.shape[0]
    req_dev = ftop_ref.shape[0]

    def step(i, _):
        value_request(dims, half + i, table_ref, t_ref, top_ref, i, vbs, acc_s, tot_s)
        return 0

    lax.fori_loop(0, half, step, 0)
    flat = (req_dev * sub, LANES)
    tots = jnp.concatenate(
        [reduce_rows(ref, jnp.add, heads) for ref in (first_tot_ref, tot_s)], axis=0)
    top = jnp.concatenate(
        [ref[...].reshape(half * sub, LANES) for ref in (first_top_ref, top_ref)], axis=0)
    ftop = ftop_ref[...].reshape(flat)
    both = jnp.maximum(top, ftop)
    fade, ffade = jnp.exp2(top - both), jnp.exp2(ftop - both)
    tots = tots * fade + ftot_ref[...].reshape(flat) * ffade
    fade, ffade = fade / tots, ffade / tots
    lses = both + jnp.log2(tots)
    for i in range(req_dev):
        acc_ref = first_acc_ref if i < half else acc_s
        rows = slice(i * sub, (i + 1) * sub)
        for h in range(heads):
            part = slice(h * sub, (h + 1) * sub)
            some = acc_ref[i % half, part, :] * rows_of(fade[rows], h)
            some = some + facc_ref[i, part, :] * rows_of(ffade[rows], h)
            put_rows(keep_ref, send_ref, (0, i * heads + h), some)
    lse = by_request(lses, heads, sub, range(req_dev))
    put_rows(keep_ref, send_ref, (0, req_dev * heads), lse, heads)


def put_rows(keep_ref, send_ref, place, value, heads=0):
    half = value.shape[0] // 2
    send = value[half:]
    keep_ref[place] = value[:half]
    send_ref[place] = pieces_of(send, heads) if heads else send.astype(jnp.bfloat16)


def by_request(lses, heads, sub, requests):
    lane = lax.broadcasted_iota(jnp.int32, (sub, LANES), 1)
    out = jnp.zeros((sub, LANES), jnp.float32)
    for i, n in enumerate(requests):
        out = jnp.where(lane // (4 * heads) == i, lses[n * sub:(n + 1) * sub], out)
    return out


def fresh_kernel(dims, pieces, n_req, slots_ref, counts_ref, kf, vf, *refs):
    heads, page_rows, slots, sub = dims
    q_refs, refs = refs[:n_req], list(refs[n_req:])
    req_dev = q_refs[0].shape[0]
    pool = [refs.pop(0)] if pieces else []
    keep_ref, send_ref, acc_ref, top_ref, tot_ref, *refs = refs
    target = [refs.pop(0)] if pieces else []
    t_s, p_s, *sem = refs
    copies = ValueCopies(pool + target + sem, 0, pieces)
    copies.start()
    lane = lax.broadcasted_iota(jnp.int32, (sub, LANES), 1)
    onehots = [(lane % heads == h).astype(jnp.bfloat16) for h in range(heads)]
    columns = slots * page_rows
    wide = min(SCORE_WIDE, columns)
    per = wide // page_rows
    own = lax.axis_index("req")
    requests = [(own ^ k) * req_dev + i for k in range(n_req) for i in range(req_dev)]
    n_reqs = len(requests)
    tops = []
    for n, request in enumerate(requests):
        limit = counts_ref[request] * page_rows
        top = jnp.full((sub, LANES), NEG, jnp.float32)
        for c in range(columns // wide):
            keys = pages_of([kf], slots_ref, request * slots + c * per, per)
            parts = score_parts(
                q_refs[n // req_dev][n % req_dev], keys, lane, limit, c * wide, heads, sub)
            for j, part in enumerate(parts):
                t_s[n, :, c * wide + j * LANES:c * wide + (j + 1) * LANES] = part
            top = jnp.maximum(top, fold_max(parts))
        tops.append(top)
    tops = class_reduce(jnp.concatenate(tops, axis=0), jnp.maximum, heads)
    tots = []
    for n in range(n_reqs):
        tot = jnp.zeros((sub, LANES), jnp.float32)
        for j in range(columns // LANES):
            p = jnp.exp2(
                t_s[n, :, j * LANES:(j + 1) * LANES] - tops[n * sub:(n + 1) * sub])
            tot = tot + p
            p_s[n, :, j * LANES:(j + 1) * LANES] = spread(p, onehots)
        tots.append(tot)
    tots = class_reduce(jnp.concatenate(tots, axis=0), jnp.add, heads)
    whole = 1.0 / tots
    lses = tops + jnp.log2(tots)
    for n, request in enumerate(requests):
        values = pages_of([vf], slots_ref, request * slots, slots)
        acc = jnp.dot(p_s[n], values, preferred_element_type=jnp.float32)
        rows = slice(n * sub, (n + 1) * sub)
        block, i = n // req_dev - 1, n % req_dev
        if block < 0:
            acc_ref[i] = acc
            top_ref[i] = tops[rows]
            tot_ref[i] = tots[rows]
            continue
        for h in range(heads):
            some = acc[h * sub:(h + 1) * sub] * rows_of(whole[rows], h)
            put_rows(keep_ref, send_ref, (block, i * heads + h), some)
    for block in range(n_req - 1):
        first = (block + 1) * req_dev
        lse = by_request(lses, heads, sub, range(first, first + req_dev))
        put_rows(keep_ref, send_ref, (block, req_dev * heads), lse, heads)
    copies.wait()


def pieces_of(lse, heads):
    lane = lax.broadcasted_iota(jnp.int32, lse.shape, 1)
    kind = lane % (4 * heads) // heads
    high = lse.astype(jnp.bfloat16).astype(jnp.float32)
    rest = lse - high
    mid = rest.astype(jnp.bfloat16).astype(jnp.float32)
    both = jnp.where(kind == 1, mid, rest - mid)
    return jnp.where(kind == 0, high, both).astype(jnp.bfloat16)


def whole_of(pieces, heads):
    x = pieces.astype(jnp.float32)
    lane = lax.broadcasted_iota(jnp.int32, x.shape, 1)
    kind = lane % (4 * heads) // heads
    x = x + pltpu.roll(x, LANES - heads, 1) + pltpu.roll(x, LANES - 2 * heads, 1)
    same = x
    for m in (1, 2):
        same = jnp.where(kind == m, pltpu.roll(x, m * heads, 1), same)
    return same


def merge_kernel(heads, skip, goals, keep_ref, got_ref, *outs):
    blocks, slabs, rows, _ = keep_ref.shape
    slabs -= 1

    def put(block, slab, value, coded=0):
        if goals[block] is None:
            put_rows(outs[0], outs[1], (block, slab), value, coded)
        else:
            which, place = goals[block]
            if outs[which].dtype == jnp.bfloat16:
                value = pieces_of(value, coded) if coded else value.astype(jnp.bfloat16)
            outs[which][place, slab] = value

    for block in range(blocks):
        own = keep_ref[block, slabs]
        other = whole_of(got_ref[block + skip, slabs], heads)
        top = jnp.maximum(own, other)
        share = jnp.exp2(own - top)
        tot = share + jnp.exp2(other - top)
        share = share / tot
        for slab in range(slabs):
            at = slab // heads * 4 * heads + slab % heads
            part = jnp.broadcast_to(share[:, at:at + 1], (rows, LANES))
            kept = keep_ref[block, slab]
            got = got_ref[block + skip, slab].astype(jnp.float32)
            put(block, slab, part * kept + (1.0 - part) * got)
        put(block, slabs, top + jnp.log2(tot), heads)


def last_kernel(keep_ref, *refs):
    *got_refs, out_ref = refs
    req_dev, heads, group, _ = out_ref.shape
    slabs = req_dev * heads
    parts = [keep_ref.at[0]] + [ref.at[0] for ref in got_refs]
    lses = [keep_ref[0, slabs]] + [whole_of(ref[0, slabs], heads) for ref in got_refs]
    top = fold_max(lses)
    shares = [jnp.exp2(lse - top) for lse in lses]
    tot = shares[0]
    for share in shares[1:]:
        tot = tot + share
    shares = [share / tot for share in shares]
    for slab in range(slabs):
        at = slab // heads * 4 * heads + slab % heads
        total = jnp.zeros((group, LANES), jnp.float32)
        for part, share in zip(parts, shares):
            total = total + part[slab].astype(jnp.float32) * jnp.broadcast_to(
                share[:, at:at + 1], (group, LANES))
        out_ref[slab // heads, slab % heads] = total.astype(jnp.bfloat16)


def params(mib):
    return pltpu.CompilerParams(vmem_limit_bytes=mib * 2**20)


def local(query, kv_pool, page_table, context_len, fresh_kv, fresh_bucket):
    n_ctx = lax.axis_size("ctx")
    n_req = lax.axis_size("req")
    req_dev, heads, group, head_dim = query.shape
    pool_slots, page = kv_pool.shape[:2]
    new_dev = fresh_kv.shape[0]
    pages_dev = page_table.shape[1]
    n_reqs = n_req * req_dev
    slots = CAP * n_ctx
    sub = n_ctx * group
    rows = heads * sub
    page_rows = page * heads

    smem = lambda count: jax.ShapeDtypeStruct((count,), jnp.int32)
    bf16 = lambda *shape: jax.ShapeDtypeStruct(shape, jnp.bfloat16)
    f32 = lambda *shape: jax.ShapeDtypeStruct(shape, jnp.float32)
    columns = pages_dev * page_rows
    split = heads % 4 == 0
    pieces = 8 if split else 0

    near = query[None]
    first, *others = bits_of("ctx")
    arrived = swap(near, "ctx", first)
    if split:
        in_hbm = lambda a: pltpu.with_memory_space_constraint(a, pltpu.HBM)
        pool = in_hbm(kv_pool)
        half = lambda count: bf16(count, page, heads, LANES)
        kf, vf = pl.pallas_call(
            stage_fresh_kernel,
            out_shape=(half(new_dev), half(new_dev)),
            in_specs=[HBM],
            out_specs=(VMEM,) * 2,
            scratch_shapes=[pltpu.SemaphoreType.DMA((2, 4))],
            compiler_params=params(2),
            cost_estimate=pl.CostEstimate(
                flops=0, transcendentals=0, bytes_accessed=4 * fresh_kv.size),
            name="stage_fresh",
        )(in_hbm(fresh_kv))
        arrived, kf = lax.optimization_barrier((arrived, kf))
        kb, slot_table, counts = pl.pallas_call(
            functools.partial(stage_keys_kernel, n_ctx, slots),
            out_shape=(half(pool_slots), smem(n_reqs * slots), smem(n_reqs)),
            in_specs=[HBM] * 2,
            out_specs=(VMEM, SMEM, SMEM),
            scratch_shapes=[
                pltpu.SMEM((new_dev,), jnp.int32), pltpu.SemaphoreType.DMA((pieces,)),
                pltpu.SemaphoreType.DMA],
            compiler_params=params(2),
            cost_estimate=pl.CostEstimate(
                flops=0, transcendentals=0, bytes_accessed=2 * kv_pool.size),
            name="stage_keys",
        )(in_hbm(fresh_bucket), pool)
        kb, kf, vf = (a.reshape(a.shape[0], page_rows, LANES) for a in (kb, kf, vf))
        value_in, value_specs = (pool,), [HBM]
        value_out = (bf16(pool_slots, page // 2, heads, LANES),)
        value_scratch = [pltpu.SemaphoreType.DMA((pieces,))]
    else:
        kb, vb, kf, vf = (
            a[..., h * LANES:(h + 1) * LANES].reshape(a.shape[0], page_rows, LANES)
            for a in (kv_pool, fresh_kv) for h in (0, 1)
        )
        slot_table, counts = pl.pallas_call(
            functools.partial(list_kernel, n_ctx, slots),
            out_shape=(smem(n_reqs * slots), smem(n_reqs)),
            in_specs=[SMEM],
            out_specs=(SMEM,) * 2,
            name="list",
        )(fresh_bucket)
        value_in, value_specs, value_out, value_scratch = (), [], (), []

    near = jnp.concatenate([near, arrived])
    for bit in others:
        near = jnp.concatenate([near, swap(near, "ctx", bit)])
    queries = near.transpose(1, 2, 0, 3, 4).reshape(req_dev, rows, head_dim)
    far = [swap(queries, "req", k) for k in range(n_req - 1, 0, -1)][::-1]

    slabs = req_dev * heads + 1
    left = sub // 2
    keep, send, facc, ftop, ftot, *vbs = pl.pallas_call(
        functools.partial(fresh_kernel, (heads, page_rows, slots, sub), pieces, n_req),
        out_shape=(
            f32(n_req - 1, slabs, left, LANES), bf16(n_req - 1, slabs, left, LANES),
            f32(req_dev, rows, LANES), f32(req_dev, sub, LANES), f32(req_dev, sub, LANES),
        ) + value_out,
        in_specs=[SMEM] * 2 + [VMEM] * (2 + n_req) + value_specs,
        out_specs=(VMEM,) * (5 + len(value_out)),
        scratch_shapes=[
            pltpu.VMEM((n_reqs, sub, slots * page_rows), jnp.float32),
            pltpu.VMEM((n_reqs, rows, slots * page_rows), jnp.bfloat16),
        ] + value_scratch,
        compiler_params=params(8),
        cost_estimate=pl.CostEstimate(
            flops=4 * n_reqs * rows * slots * page_rows * LANES,
            transcendentals=n_reqs * sub * slots * page_rows, bytes_accessed=2 * fresh_kv.size),
        name="fresh",
    )(slot_table, counts, kf, vf, queries, *far, *value_in)

    def merge(keep, got, skip, goals, shapes):
        return pl.pallas_call(
            functools.partial(merge_kernel, heads, skip, goals),
            out_shape=shapes,
            in_specs=[VMEM] * 2,
            out_specs=[VMEM] * len(shapes),
            compiler_params=params(8),
            name="merge",
        )(keep, got)

    def halved(keep, got):
        shape = (keep.shape[0], slabs, keep.shape[2] // 2, LANES)
        return merge(keep, got, 0, [None] * keep.shape[0], [f32(*shape), bf16(*shape)])

    def sorted_by(keep, got, skip, offsets, bit):
        sends = [offset for offset in offsets if offset & bit]
        keeps = [offset for offset in offsets if not offset & bit]
        goals = [
            (0, sends.index(o)) if o in sends else (1, keeps.index(o)) for o in offsets]
        shape = lambda count: (count, slabs, group, LANES)
        shapes = [bf16(*shape(len(sends)))] + ([f32(*shape(len(keeps)))] if keeps else [])
        return merge(keep, got, skip, goals, shapes), keeps

    ctx_bits = list(bits_of("ctx"))[::-1]
    req_bits = list(bits_of("req"))[::-1]
    dims = (heads, page_rows, pages_dev, sub)
    table = page_table.reshape(-1)
    part = req_dev // 2
    cost = lambda scores, values: pl.CostEstimate(
        flops=2 * (scores + values) * rows * columns * LANES,
        transcendentals=values * sub * columns,
        bytes_accessed=(scores + values) * columns * LANES * 2)
    send, queries = lax.optimization_barrier((send, queries))
    got = swap(send, "ctx", ctx_bits[0])
    t, top, *more = pl.pallas_call(
        functools.partial(first_kernel, dims, pieces),
        out_shape=(f32(part, sub, columns), f32(part, sub, LANES)) + value_out,
        in_specs=[SMEM] * 2 + [VMEM] * 2 + value_specs,
        out_specs=(VMEM,) * (2 + len(value_out)),
        scratch_shapes=value_scratch,
        compiler_params=params(4),
        cost_estimate=cost(part, 0),
        name="first",
    )(table, context_len, queries, kb, *value_in)
    vbs = [a.reshape(a.shape[0], -1, LANES) for a in vbs + more] if split else [vb]
    got, top = lax.optimization_barrier((got, top))
    for bit in ctx_bits[1:]:
        keep, send = halved(keep, got)
        send, top = lax.optimization_barrier((send, top))
        got = swap(send, "ctx", bit)
    later, later_top, acc, tot = pl.pallas_call(
        functools.partial(middle_kernel, dims),
        out_shape=(
            f32(part, sub, columns), f32(part, sub, LANES), f32(part, rows, LANES),
            f32(part, sub, LANES)),
        in_specs=[SMEM] * 2 + [VMEM] * (4 + len(vbs)),
        out_specs=(VMEM,) * 4,
        compiler_params=params(4),
        cost_estimate=cost(part, part),
        name="middle",
    )(table, context_len, queries, kb, t, top, *vbs)
    got, later_top = lax.optimization_barrier((got, later_top))
    offsets = list(range(1, n_req))
    (send, *kept), offsets = sorted_by(keep, got, 0, offsets, req_bits[0])
    send, later_top = lax.optimization_barrier((send, later_top))
    got = swap(send, "req", req_bits[0])
    arrived = [got]
    own_keep, own_send = pl.pallas_call(
        functools.partial(second_kernel, dims),
        out_shape=(f32(1, slabs, left, LANES), bf16(1, slabs, left, LANES)),
        in_specs=[SMEM] + [VMEM] * (8 + len(vbs)),
        out_specs=(VMEM,) * 2,
        scratch_shapes=[
            pltpu.VMEM((part, rows, LANES), jnp.float32),
            pltpu.VMEM((part, sub, LANES), jnp.float32)],
        compiler_params=params(4),
        cost_estimate=cost(0, part),
        name="second",
    )(table, later, later_top, top, acc, tot, facc, ftop, ftot, *vbs)
    got, own_keep = lax.optimization_barrier((got, own_keep))
    own_got = swap(own_send, "ctx", ctx_bits[0])
    for bit in req_bits[1:]:
        (send, *kept), offsets = sorted_by(kept[0], got, 1, offsets, bit)
        send, own_got = lax.optimization_barrier((send, own_got))
        got = swap(send, "req", bit)
        arrived.append(got)
    for bit in ctx_bits[1:]:
        own_keep, own_send = halved(own_keep, own_got)
        own_got = swap(own_send, "ctx", bit)
    return pl.pallas_call(
        last_kernel,
        out_shape=bf16(req_dev, heads, group, LANES),
        in_specs=[VMEM] * (2 + len(arrived)),
        out_specs=VMEM,
        compiler_params=params(8),
        name="last",
    )(own_keep, own_got, *arrived)


def solution(mesh):
    placed = (
        P("req", "kvh", "ctx", None),
        P(("req", "ctx"), None, "kvh", None),
        P("req", "ctx"),
        P("req"),
        P(("req", "ctx"), None, "kvh", None),
        P(("req", "ctx")),
    )
    return jax.shard_map(
        local, mesh=mesh, in_specs=placed, out_specs=P("req", "kvh", "ctx", None), check_vma=False
    )
```

```python
import functools
import math

import jax
import jax.numpy as jnp
from jax import lax
from jax.experimental import pallas as pl
from jax.experimental.pallas import tpu as pltpu
from jax.sharding import PartitionSpec as P

NEG = -1e30
CAP = 2
LANES = 128
SCALE = math.log2(math.e) / math.sqrt(LANES)
SCORE_WIDE = 256
VALUE_WIDE = 512
VMEM = pl.BlockSpec(memory_space=pltpu.VMEM)
SMEM = pl.BlockSpec(memory_space=pltpu.SMEM)
HBM = pl.BlockSpec(memory_space=pltpu.HBM)


def swap(value, axis, bit):
    return lax.ppermute(value, axis, [(n, n ^ bit) for n in range(lax.axis_size(axis))])


def bits_of(axis):
    bit = lax.axis_size(axis) // 2
    while bit:
        yield bit
        bit //= 2


def half_copies(pool_ref, target, sem, half, pieces, tokens=None):
    each = pool_ref.shape[0] // pieces
    tokens = tokens or pl.ds(0, pool_ref.shape[1])
    return [
        pltpu.make_async_copy(
            pool_ref.at[pl.ds(n * each, each), tokens, :, pl.ds(half * LANES, LANES)],
            target.at[pl.ds(n * each, each)], sem.at[n])
        for n in range(pieces)
    ]


class ValueCopies:
    def __init__(self, refs, part, pieces):
        self.copies = []
        if pieces:
            pool_ref, target, sem = refs
            count = pool_ref.shape[1] // 2
            self.copies = half_copies(
                pool_ref, target, sem, 1, pieces, pl.ds(part * count, count))

    def start(self):
        for one in self.copies:
            one.start()

    def wait(self):
        for one in self.copies:
            one.wait()


def stage_fresh_kernel(query_hbm, fresh_ref, query_ref, kf, vf, sem, query_sem):
    copies = [pltpu.make_async_copy(query_hbm, query_ref, query_sem)]
    for half, to in enumerate((kf, vf)):
        copies += half_copies(fresh_ref, to, sem.at[half], half, sem.shape[1])
    for one in copies:
        one.start()
    for one in copies:
        one.wait()


def stage_keys_kernel(
    n_ctx, slots, bucket_hbm, pool_ref, kb, slots_ref, counts_ref, bucket_ref, sem, bucket_sem,
):
    listed = pltpu.make_async_copy(bucket_hbm, bucket_ref, bucket_sem)
    copies = half_copies(pool_ref, kb, sem, 0, sem.shape[0])
    listed.start()
    for one in copies:
        one.start()
    listed.wait()
    list_fresh(n_ctx, slots, bucket_ref, slots_ref, counts_ref)
    for one in copies:
        one.wait()


def list_kernel(n_ctx, slots, bucket_ref, slots_ref, counts_ref):
    list_fresh(n_ctx, slots, bucket_ref, slots_ref, counts_ref)


def list_fresh(n_ctx, slots, bucket_ref, slots_ref, counts_ref):
    for n in range(counts_ref.shape[0]):
        counts_ref[n] = 0
    for n in range(slots_ref.shape[0]):
        slots_ref[n] = 0

    def put(page, _):
        request = bucket_ref[page] >> (n_ctx.bit_length() - 1)
        count = counts_ref[request]
        slots_ref[request * slots + count] = page
        counts_ref[request] = count + 1
        return 0

    lax.fori_loop(0, bucket_ref.shape[0], put, 0, unroll=16)


def class_reduce(x, op, heads):
    step = heads
    while step < LANES:
        x = op(x, pltpu.roll(x, step, 1))
        step *= 2
    return x


def pages_of(refs, table_ref, first, count):
    pages = [table_ref[first + n] for n in range(count)]
    return jnp.concatenate([ref[page] for page in pages for ref in refs], axis=0)


def score_parts(q, keys, lane, limit, first, heads, sub):
    s = lax.dot_general(q, keys, (((1,), (1,)), ((), ())), preferred_element_type=jnp.float32)
    out = []
    for j in range(s.shape[1] // LANES):
        part = s[:, j * LANES:(j + 1) * LANES]
        one = part[:sub]
        for h in range(1, heads):
            one = jnp.where(lane % heads == h, part[h * sub:(h + 1) * sub], one)
        out.append(jnp.where(lane < limit - (first + j * LANES), one * SCALE, NEG))
    return out


def spread(p, onehots):
    p = p.astype(jnp.bfloat16)
    return jnp.concatenate([p * one for one in onehots], axis=0)


def rows_of(x, h):
    return jnp.broadcast_to(x[:, h:h + 1], x.shape)


def fold_max(parts):
    top = parts[0]
    for part in parts[1:]:
        top = jnp.maximum(top, part)
    return top


def score_request(dims, i, table_ref, len_ref, q_ref, kb, t_ref, top_ref, at):
    heads, page_rows, pages_dev, sub = dims
    columns = pages_dev * page_rows
    wide = min(SCORE_WIDE, columns)
    per = wide // page_rows
    lane = lax.broadcasted_iota(jnp.int32, (sub, LANES), 1)
    top = jnp.full((sub, LANES), NEG, jnp.float32)
    limit = len_ref[i] * heads - lax.axis_index("ctx") * columns
    for c in range(columns // wide):
        keys = pages_of([kb], table_ref, i * pages_dev + c * per, per)
        parts = score_parts(q_ref[i], keys, lane, limit, c * wide, heads, sub)
        for j, part in enumerate(parts):
            t_ref[at, :, c * wide + j * LANES:c * wide + (j + 1) * LANES] = part
        top = jnp.maximum(top, fold_max(parts))
    top_ref[at] = top


def value_request(dims, i, table_ref, t_ref, top_ref, at, vbs, acc_ref, tot_ref):
    heads, page_rows, pages_dev, sub = dims
    columns = pages_dev * page_rows
    wide = min(VALUE_WIDE, columns)
    per = wide // page_rows
    lane = lax.broadcasted_iota(jnp.int32, (sub, LANES), 1)
    onehots = [(lane % heads == h).astype(jnp.bfloat16) for h in range(heads)]
    tot = jnp.zeros((sub, LANES), jnp.float32)
    acc = jnp.zeros((heads * sub, LANES), jnp.float32)
    top = top_ref[at]
    for c in range(columns // wide):
        weights = []
        for j in range(wide // LANES):
            where = c * wide + j * LANES
            p = jnp.exp2(t_ref[at, :, where:where + LANES] - top)
            tot = tot + p
            weights.append(spread(p, onehots))
        values = pages_of(vbs, table_ref, i * pages_dev + c * per, per)
        acc = acc + jnp.dot(
            jnp.concatenate(weights, axis=1), values, preferred_element_type=jnp.float32)
    acc_ref[at] = acc
    tot_ref[at] = tot


def reduce_rows(ref, op, heads):
    flat = ref[...].reshape(ref.shape[0] * ref.shape[1], LANES)
    return class_reduce(flat, op, heads)


def first_kernel(dims, pieces, table_ref, len_ref, q_ref, kb, *refs):
    refs = list(refs)
    pool = [refs.pop(0)] if pieces else []
    t_ref, top_ref, *refs = refs
    copies = ValueCopies(pool + refs, 1, pieces)
    copies.start()

    def step(i, _):
        score_request(dims, i, table_ref, len_ref, q_ref, kb, t_ref, top_ref, i)
        return 0

    lax.fori_loop(0, t_ref.shape[0], step, 0)
    top_ref[...] = reduce_rows(top_ref, jnp.maximum, dims[0]).reshape(top_ref.shape)
    copies.wait()


def middle_kernel(dims, table_ref, len_ref, q_ref, kb, t_ref, top_ref, *refs):
    *vbs, later_ref, later_top_ref, acc_ref, tot_ref = refs
    half = t_ref.shape[0]

    def step(i, _):
        score_request(
            dims, half + i, table_ref, len_ref, q_ref, kb, later_ref, later_top_ref, i)
        value_request(dims, i, table_ref, t_ref, top_ref, i, vbs, acc_ref, tot_ref)
        return 0

    lax.fori_loop(0, half, step, 0)
    later_top_ref[...] = reduce_rows(
        later_top_ref, jnp.maximum, dims[0]).reshape(later_top_ref.shape)


def second_kernel(
    dims, n_vbs, table_ref, t_ref, top_ref, first_top_ref, first_acc_ref, first_tot_ref, facc_ref,
    ftop_ref, ftot_ref, *refs,
):
    heads, page_rows, pages_dev, sub = dims
    half = t_ref.shape[0]
    req_dev = ftop_ref.shape[0]
    vbs, (keep_ref, *send_refs, acc_s, tot_s) = refs[:n_vbs], refs[n_vbs:]
    group = keep_ref.shape[2]

    def put(slab, value, coded=0):
        keep_ref[0, slab] = value[:group]
        for place, ref in enumerate(send_refs):
            send = value[(place + 1) * group:(place + 2) * group]
            ref[0, slab] = pieces_of(send, coded) if coded else send.astype(jnp.bfloat16)

    def step(i, _):
        value_request(dims, half + i, table_ref, t_ref, top_ref, i, vbs, acc_s, tot_s)
        return 0

    lax.fori_loop(0, half, step, 0)
    flat = (req_dev * sub, LANES)
    tots = jnp.concatenate(
        [reduce_rows(ref, jnp.add, heads) for ref in (first_tot_ref, tot_s)], axis=0)
    top = jnp.concatenate(
        [ref[...].reshape(half * sub, LANES) for ref in (first_top_ref, top_ref)], axis=0)
    ftop = ftop_ref[...].reshape(flat)
    both = jnp.maximum(top, ftop)
    fade, ffade = jnp.exp2(top - both), jnp.exp2(ftop - both)
    tots = tots * fade + ftot_ref[...].reshape(flat) * ffade
    fade, ffade = fade / tots, ffade / tots
    lses = both + jnp.log2(tots)
    for i in range(req_dev):
        acc_ref = first_acc_ref if i < half else acc_s
        rows = slice(i * sub, (i + 1) * sub)
        for h in range(heads):
            part = slice(h * sub, (h + 1) * sub)
            some = acc_ref[i % half, part, :] * rows_of(fade[rows], h)
            some = some + facc_ref[i, part, :] * rows_of(ffade[rows], h)
            put(i * heads + h, some)
    put(req_dev * heads, by_request(lses, heads, sub, range(req_dev)), heads)


def put_rows(keep_ref, send_ref, place, value, heads=0):
    half = value.shape[0] // 2
    send = value[half:]
    keep_ref[place] = value[:half]
    send_ref[place] = pieces_of(send, heads) if heads else send.astype(jnp.bfloat16)


def by_request(lses, heads, sub, requests):
    lane = lax.broadcasted_iota(jnp.int32, (sub, LANES), 1)
    out = jnp.zeros((sub, LANES), jnp.float32)
    for i, n in enumerate(requests):
        out = jnp.where(lane // (4 * heads) == i, lses[n * sub:(n + 1) * sub], out)
    return out


def fresh_kernel(dims, pieces, n_req, slots_ref, counts_ref, kf, vf, *refs):
    heads, page_rows, slots, sub = dims
    q_refs, refs = refs[:n_req], list(refs[n_req:])
    req_dev = q_refs[0].shape[0]
    pool = [refs.pop(0)] if pieces else []
    keep_ref, send_ref, acc_ref, top_ref, tot_ref, *refs = refs
    target = [refs.pop(0)] if pieces else []
    t_s, p_s, *sem = refs
    copies = ValueCopies(pool + target + sem, 0, pieces)
    copies.start()
    lane = lax.broadcasted_iota(jnp.int32, (sub, LANES), 1)
    onehots = [(lane % heads == h).astype(jnp.bfloat16) for h in range(heads)]
    columns = slots * page_rows
    wide = min(SCORE_WIDE, columns)
    per = wide // page_rows
    own = lax.axis_index("req")
    requests = [(own ^ k) * req_dev + i for k in range(n_req) for i in range(req_dev)]
    n_reqs = len(requests)
    tops = []
    for n, request in enumerate(requests):
        limit = counts_ref[request] * page_rows
        top = jnp.full((sub, LANES), NEG, jnp.float32)
        for c in range(columns // wide):
            keys = pages_of([kf], slots_ref, request * slots + c * per, per)
            parts = score_parts(
                q_refs[n // req_dev][n % req_dev], keys, lane, limit, c * wide, heads, sub)
            for j, part in enumerate(parts):
                t_s[n, :, c * wide + j * LANES:c * wide + (j + 1) * LANES] = part
            top = jnp.maximum(top, fold_max(parts))
        tops.append(top)
    tops = class_reduce(jnp.concatenate(tops, axis=0), jnp.maximum, heads)
    tots = []
    for n in range(n_reqs):
        tot = jnp.zeros((sub, LANES), jnp.float32)
        for j in range(columns // LANES):
            p = jnp.exp2(
                t_s[n, :, j * LANES:(j + 1) * LANES] - tops[n * sub:(n + 1) * sub])
            tot = tot + p
            p_s[n, :, j * LANES:(j + 1) * LANES] = spread(p, onehots)
        tots.append(tot)
    tots = class_reduce(jnp.concatenate(tots, axis=0), jnp.add, heads)
    whole = 1.0 / tots
    lses = tops + jnp.log2(tots)
    for n, request in enumerate(requests):
        values = pages_of([vf], slots_ref, request * slots, slots)
        acc = jnp.dot(p_s[n], values, preferred_element_type=jnp.float32)
        rows = slice(n * sub, (n + 1) * sub)
        block, i = n // req_dev - 1, n % req_dev
        if block < 0:
            acc_ref[i] = acc
            top_ref[i] = tops[rows]
            tot_ref[i] = tots[rows]
            continue
        for h in range(heads):
            some = acc[h * sub:(h + 1) * sub] * rows_of(whole[rows], h)
            put_rows(keep_ref, send_ref, (block, i * heads + h), some)
    for block in range(n_req - 1):
        first = (block + 1) * req_dev
        lse = by_request(lses, heads, sub, range(first, first + req_dev))
        put_rows(keep_ref, send_ref, (block, req_dev * heads), lse, heads)
    copies.wait()


def pieces_of(lse, heads):
    lane = lax.broadcasted_iota(jnp.int32, lse.shape, 1)
    kind = lane % (4 * heads) // heads
    high = lse.astype(jnp.bfloat16).astype(jnp.float32)
    rest = lse - high
    mid = rest.astype(jnp.bfloat16).astype(jnp.float32)
    both = jnp.where(kind == 1, mid, rest - mid)
    return jnp.where(kind == 0, high, both).astype(jnp.bfloat16)


def whole_of(pieces, heads):
    x = pieces.astype(jnp.float32)
    lane = lax.broadcasted_iota(jnp.int32, x.shape, 1)
    kind = lane % (4 * heads) // heads
    x = x + pltpu.roll(x, LANES - heads, 1) + pltpu.roll(x, LANES - 2 * heads, 1)
    same = x
    for m in (1, 2):
        same = jnp.where(kind == m, pltpu.roll(x, m * heads, 1), same)
    return same


def merge_kernel(heads, skip, goals, keep_ref, got_ref, *outs):
    blocks, slabs, rows, _ = keep_ref.shape
    slabs -= 1

    def put(block, slab, value, coded=0):
        if goals[block] is None:
            put_rows(outs[0], outs[1], (block, slab), value, coded)
        else:
            which, place = goals[block]
            if outs[which].dtype == jnp.bfloat16:
                value = pieces_of(value, coded) if coded else value.astype(jnp.bfloat16)
            outs[which][place, slab] = value

    for block in range(blocks):
        own = keep_ref[block, slabs]
        other = whole_of(got_ref[block + skip, slabs], heads)
        top = jnp.maximum(own, other)
        share = jnp.exp2(own - top)
        tot = share + jnp.exp2(other - top)
        share = share / tot
        for slab in range(slabs):
            at = slab // heads * 4 * heads + slab % heads
            part = jnp.broadcast_to(share[:, at:at + 1], (rows, LANES))
            kept = keep_ref[block, slab]
            got = got_ref[block + skip, slab].astype(jnp.float32)
            put(block, slab, part * kept + (1.0 - part) * got)
        put(block, slabs, top + jnp.log2(tot), heads)


def last_kernel(keep_ref, *refs):
    *got_refs, out_ref = refs
    req_dev, heads, group, _ = out_ref.shape
    slabs = req_dev * heads
    parts = [keep_ref.at[0]] + [ref.at[0] for ref in got_refs]
    lses = [keep_ref[0, slabs]] + [whole_of(ref[0, slabs], heads) for ref in got_refs]
    top = fold_max(lses)
    shares = [jnp.exp2(lse - top) for lse in lses]
    tot = shares[0]
    for share in shares[1:]:
        tot = tot + share
    shares = [share / tot for share in shares]
    for slab in range(slabs):
        at = slab // heads * 4 * heads + slab % heads
        total = jnp.zeros((group, LANES), jnp.float32)
        for part, share in zip(parts, shares):
            total = total + part[slab].astype(jnp.float32) * jnp.broadcast_to(
                share[:, at:at + 1], (group, LANES))
        out_ref[slab // heads, slab % heads] = total.astype(jnp.bfloat16)


def params(mib):
    return pltpu.CompilerParams(vmem_limit_bytes=mib * 2**20)


def local(query, kv_pool, page_table, context_len, fresh_kv, fresh_bucket):
    n_ctx = lax.axis_size("ctx")
    n_req = lax.axis_size("req")
    req_dev, heads, group, head_dim = query.shape
    pool_slots, page = kv_pool.shape[:2]
    new_dev = fresh_kv.shape[0]
    pages_dev = page_table.shape[1]
    n_reqs = n_req * req_dev
    slots = CAP * n_ctx
    sub = n_ctx * group
    rows = heads * sub
    page_rows = page * heads

    smem = lambda count: jax.ShapeDtypeStruct((count,), jnp.int32)
    bf16 = lambda *shape: jax.ShapeDtypeStruct(shape, jnp.bfloat16)
    f32 = lambda *shape: jax.ShapeDtypeStruct(shape, jnp.float32)
    columns = pages_dev * page_rows
    split = heads % 4 == 0
    pieces = 8 if split else 0

    ctx_offsets = [0]
    for bit in bits_of("ctx"):
        ctx_offsets += [offset ^ bit for offset in ctx_offsets]
    near = [swap(query, "ctx", offset) for offset in ctx_offsets[1:]]
    if split:
        in_hbm = lambda a: pltpu.with_memory_space_constraint(a, pltpu.HBM)
        pool = in_hbm(kv_pool)
        half = lambda count: bf16(count, page, heads, LANES)
        query, kf, vf = pl.pallas_call(
            stage_fresh_kernel,
            out_shape=(bf16(*query.shape), half(new_dev), half(new_dev)),
            in_specs=[HBM] * 2,
            out_specs=(VMEM,) * 3,
            scratch_shapes=[pltpu.SemaphoreType.DMA((2, 4)), pltpu.SemaphoreType.DMA],
            compiler_params=params(2),
            cost_estimate=pl.CostEstimate(
                flops=0, transcendentals=0, bytes_accessed=4 * fresh_kv.size),
            name="stage_fresh",
        )(in_hbm(query), in_hbm(fresh_kv))
        kf, *near = lax.optimization_barrier((kf, *near))
        kb, slot_table, counts = pl.pallas_call(
            functools.partial(stage_keys_kernel, n_ctx, slots),
            out_shape=(half(pool_slots), smem(n_reqs * slots), smem(n_reqs)),
            in_specs=[HBM] * 2,
            out_specs=(VMEM, SMEM, SMEM),
            scratch_shapes=[
                pltpu.SMEM((new_dev,), jnp.int32), pltpu.SemaphoreType.DMA((pieces,)),
                pltpu.SemaphoreType.DMA],
            compiler_params=params(2),
            cost_estimate=pl.CostEstimate(
                flops=0, transcendentals=0, bytes_accessed=2 * kv_pool.size),
            name="stage_keys",
        )(in_hbm(fresh_bucket), pool)
        kb, kf, vf = (a.reshape(a.shape[0], page_rows, LANES) for a in (kb, kf, vf))
        value_in, value_specs = (pool,), [HBM]
        value_out = (bf16(pool_slots, page // 2, heads, LANES),)
        value_scratch = [pltpu.SemaphoreType.DMA((pieces,))]
    else:
        kb, vb, kf, vf = (
            a[..., h * LANES:(h + 1) * LANES].reshape(a.shape[0], page_rows, LANES)
            for a in (kv_pool, fresh_kv) for h in (0, 1)
        )
        slot_table, counts = pl.pallas_call(
            functools.partial(list_kernel, n_ctx, slots),
            out_shape=(smem(n_reqs * slots), smem(n_reqs)),
            in_specs=[SMEM],
            out_specs=(SMEM,) * 2,
            name="list",
        )(fresh_bucket)
        value_in, value_specs, value_out, value_scratch = (), [], (), []

    queries = jnp.stack([query] + near).transpose(1, 2, 0, 3, 4).reshape(req_dev, rows, head_dim)
    far = [swap(queries, "req", k) for k in range(n_req - 1, 0, -1)][::-1]

    slabs = req_dev * heads + 1
    left = sub // 2
    keep, send, facc, ftop, ftot, *vbs = pl.pallas_call(
        functools.partial(fresh_kernel, (heads, page_rows, slots, sub), pieces, n_req),
        out_shape=(
            f32(n_req - 1, slabs, left, LANES), bf16(n_req - 1, slabs, left, LANES),
            f32(req_dev, rows, LANES), f32(req_dev, sub, LANES), f32(req_dev, sub, LANES),
        ) + value_out,
        in_specs=[SMEM] * 2 + [VMEM] * (2 + n_req) + value_specs,
        out_specs=(VMEM,) * (5 + len(value_out)),
        scratch_shapes=[
            pltpu.VMEM((n_reqs, sub, slots * page_rows), jnp.float32),
            pltpu.VMEM((n_reqs, rows, slots * page_rows), jnp.bfloat16),
        ] + value_scratch,
        compiler_params=params(8),
        cost_estimate=pl.CostEstimate(
            flops=4 * n_reqs * rows * slots * page_rows * LANES,
            transcendentals=n_reqs * sub * slots * page_rows, bytes_accessed=2 * fresh_kv.size),
        name="fresh",
    )(slot_table, counts, kf, vf, queries, *far, *value_in)

    def merge(keep, got, skip, goals, shapes):
        return pl.pallas_call(
            functools.partial(merge_kernel, heads, skip, goals),
            out_shape=shapes,
            in_specs=[VMEM] * 2,
            out_specs=[VMEM] * len(shapes),
            compiler_params=params(8),
            name="merge",
        )(keep, got)

    def halved(keep, got):
        shape = (keep.shape[0], slabs, keep.shape[2] // 2, LANES)
        return merge(keep, got, 0, [None] * keep.shape[0], [f32(*shape), bf16(*shape)])

    def sorted_by(keep, got, skip, offsets, bit):
        sends = [offset for offset in offsets if offset & bit]
        keeps = [offset for offset in offsets if not offset & bit]
        goals = [
            (0, sends.index(o)) if o in sends else (1, keeps.index(o)) for o in offsets]
        shape = lambda count: (count, slabs, group, LANES)
        shapes = [bf16(*shape(len(sends)))] + ([f32(*shape(len(keeps)))] if keeps else [])
        return merge(keep, got, skip, goals, shapes), keeps

    ctx_bits = list(bits_of("ctx"))[::-1]
    req_bits = list(bits_of("req"))[::-1]
    dims = (heads, page_rows, pages_dev, sub)
    table = page_table.reshape(-1)
    part = req_dev // 2
    cost = lambda scores, values: pl.CostEstimate(
        flops=2 * (scores + values) * rows * columns * LANES,
        transcendentals=values * sub * columns,
        bytes_accessed=(scores + values) * columns * LANES * 2)
    send, queries = lax.optimization_barrier((send, queries))
    got = swap(send, "ctx", ctx_bits[0])
    t, top, *more = pl.pallas_call(
        functools.partial(first_kernel, dims, pieces),
        out_shape=(f32(part, sub, columns), f32(part, sub, LANES)) + value_out,
        in_specs=[SMEM] * 2 + [VMEM] * 2 + value_specs,
        out_specs=(VMEM,) * (2 + len(value_out)),
        scratch_shapes=value_scratch,
        compiler_params=params(4),
        cost_estimate=cost(part, 0),
        name="first",
    )(table, context_len, queries, kb, *value_in)
    vbs = [a.reshape(a.shape[0], -1, LANES) for a in vbs + more] if split else [vb]
    got, top = lax.optimization_barrier((got, top))
    for bit in ctx_bits[1:]:
        keep, send = halved(keep, got)
        send, top = lax.optimization_barrier((send, top))
        got = swap(send, "ctx", bit)
    later, later_top, acc, tot = pl.pallas_call(
        functools.partial(middle_kernel, dims),
        out_shape=(
            f32(part, sub, columns), f32(part, sub, LANES), f32(part, rows, LANES),
            f32(part, sub, LANES)),
        in_specs=[SMEM] * 2 + [VMEM] * (4 + len(vbs)),
        out_specs=(VMEM,) * 4,
        compiler_params=params(4),
        cost_estimate=cost(part, part),
        name="middle",
    )(table, context_len, queries, kb, t, top, *vbs)
    got, later_top = lax.optimization_barrier((got, later_top))
    offsets = list(range(1, n_req))
    (send, *kept), offsets = sorted_by(keep, got, 0, offsets, req_bits[0])
    send, later_top = lax.optimization_barrier((send, later_top))
    got = swap(send, "req", req_bits[0])
    arrived = [got]
    own_keep, *own_sends = pl.pallas_call(
        functools.partial(second_kernel, dims, len(vbs)),
        out_shape=(f32(1, slabs, group, LANES),)
        + (bf16(1, slabs, group, LANES),) * (n_ctx - 1),
        in_specs=[SMEM] + [VMEM] * (8 + len(vbs)),
        out_specs=(VMEM,) * n_ctx,
        scratch_shapes=[
            pltpu.VMEM((part, rows, LANES), jnp.float32),
            pltpu.VMEM((part, sub, LANES), jnp.float32)],
        compiler_params=params(4),
        cost_estimate=cost(0, part),
        name="second",
    )(table, later, later_top, top, acc, tot, facc, ftop, ftot, *vbs)
    got, own_keep = lax.optimization_barrier((got, own_keep))
    arrived += [
        swap(one, "ctx", offset) for one, offset in zip(own_sends, ctx_offsets[1:])]
    for bit in req_bits[1:]:
        (send, *kept), offsets = sorted_by(kept[0], got, 1, offsets, bit)
        got = swap(send, "req", bit)
        arrived.append(got)
    return pl.pallas_call(
        last_kernel,
        out_shape=bf16(req_dev, heads, group, LANES),
        in_specs=[VMEM] * (1 + len(arrived)),
        out_specs=VMEM,
        compiler_params=params(8),
        name="last",
    )(own_keep, *arrived)


def solution(mesh):
    placed = (
        P("req", "kvh", "ctx", None),
        P(("req", "ctx"), None, "kvh", None),
        P("req", "ctx"),
        P("req"),
        P(("req", "ctx"), None, "kvh", None),
        P(("req", "ctx")),
    )
    return jax.shard_map(
        local, mesh=mesh, in_specs=placed, out_specs=P("req", "kvh", "ctx", None), check_vma=False
    )
```

```python
import functools
import math

import jax
import jax.numpy as jnp
from jax import lax
from jax.experimental import pallas as pl
from jax.experimental.pallas import tpu as pltpu
from jax.sharding import PartitionSpec as P

NEG = -1e30
CAP = 2
LANES = 128
SCALE = math.log2(math.e) / math.sqrt(LANES)
SCORE_WIDE = 256
VALUE_WIDE = 512
VMEM = pl.BlockSpec(memory_space=pltpu.VMEM)
SMEM = pl.BlockSpec(memory_space=pltpu.SMEM)
HBM = pl.BlockSpec(memory_space=pltpu.HBM)


def swap(value, axis, bit):
    return lax.ppermute(value, axis, [(n, n ^ bit) for n in range(lax.axis_size(axis))])


def bits_of(axis):
    bit = lax.axis_size(axis) // 2
    while bit:
        yield bit
        bit //= 2


def half_copies(pool_ref, target, sem, half, pieces, tokens=None):
    each = pool_ref.shape[0] // pieces
    tokens = tokens or pl.ds(0, pool_ref.shape[1])
    return [
        pltpu.make_async_copy(
            pool_ref.at[pl.ds(n * each, each), tokens, :, pl.ds(half * LANES, LANES)],
            target.at[pl.ds(n * each, each)], sem.at[n])
        for n in range(pieces)
    ]


class ValueCopies:
    def __init__(self, refs, part, pieces):
        self.copies = []
        if pieces:
            pool_ref, target, sem = refs
            count = pool_ref.shape[1] // 2
            self.copies = half_copies(
                pool_ref, target, sem, 1, pieces, pl.ds(part * count, count))

    def start(self):
        for one in self.copies:
            one.start()

    def wait(self):
        for one in self.copies:
            one.wait()


def stage_fresh_kernel(query_hbm, fresh_ref, query_ref, kf, vf, sem, query_sem):
    copies = [pltpu.make_async_copy(query_hbm, query_ref, query_sem)]
    for half, to in enumerate((kf, vf)):
        copies += half_copies(fresh_ref, to, sem.at[half], half, sem.shape[1])
    for one in copies:
        one.start()
    for one in copies:
        one.wait()


def stage_keys_kernel(
    n_ctx, slots, bucket_hbm, pool_ref, kb, slots_ref, counts_ref, bucket_ref, sem, bucket_sem,
):
    listed = pltpu.make_async_copy(bucket_hbm, bucket_ref, bucket_sem)
    copies = half_copies(pool_ref, kb, sem, 0, sem.shape[0])
    listed.start()
    for one in copies:
        one.start()
    listed.wait()
    list_fresh(n_ctx, slots, bucket_ref, slots_ref, counts_ref)
    for one in copies:
        one.wait()


def list_kernel(n_ctx, slots, bucket_ref, slots_ref, counts_ref):
    list_fresh(n_ctx, slots, bucket_ref, slots_ref, counts_ref)


def list_fresh(n_ctx, slots, bucket_ref, slots_ref, counts_ref):
    for n in range(counts_ref.shape[0]):
        counts_ref[n] = 0
    for n in range(slots_ref.shape[0]):
        slots_ref[n] = 0

    def put(page, _):
        request = bucket_ref[page] >> (n_ctx.bit_length() - 1)
        count = counts_ref[request]
        slots_ref[request * slots + count] = page
        counts_ref[request] = count + 1
        return 0

    lax.fori_loop(0, bucket_ref.shape[0], put, 0, unroll=16)


def class_reduce(x, op, heads):
    step = heads
    while step < LANES:
        x = op(x, pltpu.roll(x, step, 1))
        step *= 2
    return x


def pages_of(refs, table_ref, first, count):
    pages = [table_ref[first + n] for n in range(count)]
    return jnp.concatenate([ref[page] for page in pages for ref in refs], axis=0)


def score_parts(q, keys, lane, limit, first, heads, sub):
    s = lax.dot_general(q, keys, (((1,), (1,)), ((), ())), preferred_element_type=jnp.float32)
    out = []
    for j in range(s.shape[1] // LANES):
        part = s[:, j * LANES:(j + 1) * LANES]
        one = part[:sub]
        for h in range(1, heads):
            one = jnp.where(lane % heads == h, part[h * sub:(h + 1) * sub], one)
        out.append(jnp.where(lane < limit - (first + j * LANES), one * SCALE, NEG))
    return out


def spread(p, onehots):
    p = p.astype(jnp.bfloat16)
    return jnp.concatenate([p * one for one in onehots], axis=0)


def rows_of(x, h):
    return jnp.broadcast_to(x[:, h:h + 1], x.shape)


def fold_max(parts):
    top = parts[0]
    for part in parts[1:]:
        top = jnp.maximum(top, part)
    return top


def score_request(dims, i, table_ref, len_ref, q_ref, kb, t_ref, top_ref, at):
    heads, page_rows, pages_dev, sub = dims
    columns = pages_dev * page_rows
    wide = min(SCORE_WIDE, columns)
    per = wide // page_rows
    lane = lax.broadcasted_iota(jnp.int32, (sub, LANES), 1)
    top = jnp.full((sub, LANES), NEG, jnp.float32)
    limit = len_ref[i] * heads - lax.axis_index("ctx") * columns
    for c in range(columns // wide):
        keys = pages_of([kb], table_ref, i * pages_dev + c * per, per)
        parts = score_parts(q_ref[i], keys, lane, limit, c * wide, heads, sub)
        for j, part in enumerate(parts):
            t_ref[at, :, c * wide + j * LANES:c * wide + (j + 1) * LANES] = part
        top = jnp.maximum(top, fold_max(parts))
    top_ref[at] = top


def value_request(dims, i, table_ref, t_ref, top_ref, at, vbs, acc_ref, tot_ref):
    heads, page_rows, pages_dev, sub = dims
    columns = pages_dev * page_rows
    wide = min(VALUE_WIDE, columns)
    per = wide // page_rows
    lane = lax.broadcasted_iota(jnp.int32, (sub, LANES), 1)
    onehots = [(lane % heads == h).astype(jnp.bfloat16) for h in range(heads)]
    tot = jnp.zeros((sub, LANES), jnp.float32)
    acc = jnp.zeros((heads * sub, LANES), jnp.float32)
    top = top_ref[at]
    for c in range(columns // wide):
        weights = []
        for j in range(wide // LANES):
            where = c * wide + j * LANES
            p = jnp.exp2(t_ref[at, :, where:where + LANES] - top)
            tot = tot + p
            weights.append(spread(p, onehots))
        values = pages_of(vbs, table_ref, i * pages_dev + c * per, per)
        acc = acc + jnp.dot(
            jnp.concatenate(weights, axis=1), values, preferred_element_type=jnp.float32)
    acc_ref[at] = acc
    tot_ref[at] = tot


def reduce_rows(ref, op, heads):
    flat = ref[...].reshape(ref.shape[0] * ref.shape[1], LANES)
    return class_reduce(flat, op, heads)


def score_kernel(dims, first, pieces, table_ref, len_ref, q_ref, kb, *refs):
    refs = list(refs)
    pool = [refs.pop(0)] if pieces else []
    t_ref, top_ref, *refs = refs
    copies = ValueCopies(pool + refs, 1, pieces)
    copies.start()

    def step(i, _):
        score_request(dims, first + i, table_ref, len_ref, q_ref, kb, t_ref, top_ref, i)
        return 0

    lax.fori_loop(0, t_ref.shape[0], step, 0)
    top_ref[...] = reduce_rows(top_ref, jnp.maximum, dims[0]).reshape(top_ref.shape)
    copies.wait()


def value_kernel(
    dims, n_vbs, table_ref, first_t_ref, first_top_ref, t_ref, top_ref, facc_ref, ftop_ref,
    ftot_ref, *refs,
):
    heads, page_rows, pages_dev, sub = dims
    half = t_ref.shape[0]
    req_dev = ftop_ref.shape[0]
    vbs, (keep_ref, *send_refs, first_acc, first_tot, acc_s, tot_s) = refs[:n_vbs], refs[n_vbs:]
    group = keep_ref.shape[2]

    def put(slab, value, coded=0):
        keep_ref[0, slab] = value[:group]
        for place, ref in enumerate(send_refs):
            send = value[(place + 1) * group:(place + 2) * group]
            ref[0, slab] = pieces_of(send, coded) if coded else send.astype(jnp.bfloat16)

    def step(i, _):
        value_request(
            dims, i, table_ref, first_t_ref, first_top_ref, i, vbs, first_acc, first_tot)
        value_request(dims, half + i, table_ref, t_ref, top_ref, i, vbs, acc_s, tot_s)
        return 0

    lax.fori_loop(0, half, step, 0)
    flat = (req_dev * sub, LANES)
    tots = jnp.concatenate(
        [reduce_rows(ref, jnp.add, heads) for ref in (first_tot, tot_s)], axis=0)
    top = jnp.concatenate(
        [ref[...].reshape(half * sub, LANES) for ref in (first_top_ref, top_ref)], axis=0)
    ftop = ftop_ref[...].reshape(flat)
    both = jnp.maximum(top, ftop)
    fade, ffade = jnp.exp2(top - both), jnp.exp2(ftop - both)
    tots = tots * fade + ftot_ref[...].reshape(flat) * ffade
    fade, ffade = fade / tots, ffade / tots
    lses = both + jnp.log2(tots)
    for i in range(req_dev):
        acc_ref = first_acc if i < half else acc_s
        rows = slice(i * sub, (i + 1) * sub)
        for h in range(heads):
            part = slice(h * sub, (h + 1) * sub)
            some = acc_ref[i % half, part, :] * rows_of(fade[rows], h)
            some = some + facc_ref[i, part, :] * rows_of(ffade[rows], h)
            put(i * heads + h, some)
    put(req_dev * heads, by_request(lses, heads, sub, range(req_dev)), heads)


def put_rows(keep_ref, send_ref, place, value, heads=0):
    half = value.shape[0] // 2
    send = value[half:]
    keep_ref[place] = value[:half]
    send_ref[place] = pieces_of(send, heads) if heads else send.astype(jnp.bfloat16)


def by_request(lses, heads, sub, requests):
    lane = lax.broadcasted_iota(jnp.int32, (sub, LANES), 1)
    out = jnp.zeros((sub, LANES), jnp.float32)
    for i, n in enumerate(requests):
        out = jnp.where(lane // (4 * heads) == i, lses[n * sub:(n + 1) * sub], out)
    return out


def fresh_kernel(dims, pieces, n_req, slots_ref, counts_ref, kf, vf, *refs):
    heads, page_rows, slots, sub = dims
    q_refs, refs = refs[:n_req], list(refs[n_req:])
    req_dev = q_refs[0].shape[0]
    pool = [refs.pop(0)] if pieces else []
    keep_ref, send_ref, acc_ref, top_ref, tot_ref, *refs = refs
    target = [refs.pop(0)] if pieces else []
    t_s, p_s, *sem = refs
    copies = ValueCopies(pool + target + sem, 0, pieces)
    copies.start()
    lane = lax.broadcasted_iota(jnp.int32, (sub, LANES), 1)
    onehots = [(lane % heads == h).astype(jnp.bfloat16) for h in range(heads)]
    columns = slots * page_rows
    wide = min(SCORE_WIDE, columns)
    per = wide // page_rows
    own = lax.axis_index("req")
    requests = [(own ^ k) * req_dev + i for k in range(n_req) for i in range(req_dev)]
    n_reqs = len(requests)
    tops = []
    for n, request in enumerate(requests):
        limit = counts_ref[request] * page_rows
        top = jnp.full((sub, LANES), NEG, jnp.float32)
        for c in range(columns // wide):
            keys = pages_of([kf], slots_ref, request * slots + c * per, per)
            parts = score_parts(
                q_refs[n // req_dev][n % req_dev], keys, lane, limit, c * wide, heads, sub)
            for j, part in enumerate(parts):
                t_s[n, :, c * wide + j * LANES:c * wide + (j + 1) * LANES] = part
            top = jnp.maximum(top, fold_max(parts))
        tops.append(top)
    tops = class_reduce(jnp.concatenate(tops, axis=0), jnp.maximum, heads)
    tots = []
    for n in range(n_reqs):
        tot = jnp.zeros((sub, LANES), jnp.float32)
        for j in range(columns // LANES):
            p = jnp.exp2(
                t_s[n, :, j * LANES:(j + 1) * LANES] - tops[n * sub:(n + 1) * sub])
            tot = tot + p
            p_s[n, :, j * LANES:(j + 1) * LANES] = spread(p, onehots)
        tots.append(tot)
    tots = class_reduce(jnp.concatenate(tots, axis=0), jnp.add, heads)
    whole = 1.0 / tots
    lses = tops + jnp.log2(tots)
    for n, request in enumerate(requests):
        values = pages_of([vf], slots_ref, request * slots, slots)
        acc = jnp.dot(p_s[n], values, preferred_element_type=jnp.float32)
        rows = slice(n * sub, (n + 1) * sub)
        block, i = n // req_dev - 1, n % req_dev
        if block < 0:
            acc_ref[i] = acc
            top_ref[i] = tops[rows]
            tot_ref[i] = tots[rows]
            continue
        for h in range(heads):
            some = acc[h * sub:(h + 1) * sub] * rows_of(whole[rows], h)
            put_rows(keep_ref, send_ref, (block, i * heads + h), some)
    for block in range(n_req - 1):
        first = (block + 1) * req_dev
        lse = by_request(lses, heads, sub, range(first, first + req_dev))
        put_rows(keep_ref, send_ref, (block, req_dev * heads), lse, heads)
    copies.wait()


def pieces_of(lse, heads):
    lane = lax.broadcasted_iota(jnp.int32, lse.shape, 1)
    kind = lane % (4 * heads) // heads
    high = lse.astype(jnp.bfloat16).astype(jnp.float32)
    rest = lse - high
    mid = rest.astype(jnp.bfloat16).astype(jnp.float32)
    both = jnp.where(kind == 1, mid, rest - mid)
    return jnp.where(kind == 0, high, both).astype(jnp.bfloat16)


def whole_of(pieces, heads):
    x = pieces.astype(jnp.float32)
    lane = lax.broadcasted_iota(jnp.int32, x.shape, 1)
    kind = lane % (4 * heads) // heads
    x = x + pltpu.roll(x, LANES - heads, 1) + pltpu.roll(x, LANES - 2 * heads, 1)
    same = x
    for m in (1, 2):
        same = jnp.where(kind == m, pltpu.roll(x, m * heads, 1), same)
    return same


def merge_kernel(heads, skip, goals, keep_ref, got_ref, *outs):
    blocks, slabs, rows, _ = keep_ref.shape
    slabs -= 1

    def put(block, slab, value, coded=0):
        if goals[block] is None:
            put_rows(outs[0], outs[1], (block, slab), value, coded)
        else:
            which, place = goals[block]
            if outs[which].dtype == jnp.bfloat16:
                value = pieces_of(value, coded) if coded else value.astype(jnp.bfloat16)
            outs[which][place, slab] = value

    for block in range(blocks):
        own = keep_ref[block, slabs]
        other = whole_of(got_ref[block + skip, slabs], heads)
        top = jnp.maximum(own, other)
        share = jnp.exp2(own - top)
        tot = share + jnp.exp2(other - top)
        share = share / tot
        for slab in range(slabs):
            at = slab // heads * 4 * heads + slab % heads
            part = jnp.broadcast_to(share[:, at:at + 1], (rows, LANES))
            kept = keep_ref[block, slab]
            got = got_ref[block + skip, slab].astype(jnp.float32)
            put(block, slab, part * kept + (1.0 - part) * got)
        put(block, slabs, top + jnp.log2(tot), heads)


def last_kernel(keep_ref, *refs):
    *got_refs, out_ref = refs
    req_dev, heads, group, _ = out_ref.shape
    slabs = req_dev * heads
    parts = [keep_ref.at[0]] + [ref.at[0] for ref in got_refs]
    lses = [keep_ref[0, slabs]] + [whole_of(ref[0, slabs], heads) for ref in got_refs]
    top = fold_max(lses)
    shares = [jnp.exp2(lse - top) for lse in lses]
    tot = shares[0]
    for share in shares[1:]:
        tot = tot + share
    shares = [share / tot for share in shares]
    for slab in range(slabs):
        at = slab // heads * 4 * heads + slab % heads
        total = jnp.zeros((group, LANES), jnp.float32)
        for part, share in zip(parts, shares):
            total = total + part[slab].astype(jnp.float32) * jnp.broadcast_to(
                share[:, at:at + 1], (group, LANES))
        out_ref[slab // heads, slab % heads] = total.astype(jnp.bfloat16)


def params(mib):
    return pltpu.CompilerParams(vmem_limit_bytes=mib * 2**20)


def local(query, kv_pool, page_table, context_len, fresh_kv, fresh_bucket):
    n_ctx = lax.axis_size("ctx")
    n_req = lax.axis_size("req")
    req_dev, heads, group, head_dim = query.shape
    pool_slots, page = kv_pool.shape[:2]
    new_dev = fresh_kv.shape[0]
    pages_dev = page_table.shape[1]
    n_reqs = n_req * req_dev
    slots = CAP * n_ctx
    sub = n_ctx * group
    rows = heads * sub
    page_rows = page * heads

    smem = lambda count: jax.ShapeDtypeStruct((count,), jnp.int32)
    bf16 = lambda *shape: jax.ShapeDtypeStruct(shape, jnp.bfloat16)
    f32 = lambda *shape: jax.ShapeDtypeStruct(shape, jnp.float32)
    columns = pages_dev * page_rows
    split = heads % 4 == 0
    pieces = 16 if split else 0

    ctx_offsets = [0]
    for bit in bits_of("ctx"):
        ctx_offsets += [offset ^ bit for offset in ctx_offsets]
    near = [swap(query, "ctx", offset) for offset in ctx_offsets[1:]]
    if split:
        in_hbm = lambda a: pltpu.with_memory_space_constraint(a, pltpu.HBM)
        pool = in_hbm(kv_pool)
        half = lambda count: bf16(count, page, heads, LANES)
        query, kf, vf = pl.pallas_call(
            stage_fresh_kernel,
            out_shape=(bf16(*query.shape), half(new_dev), half(new_dev)),
            in_specs=[HBM] * 2,
            out_specs=(VMEM,) * 3,
            scratch_shapes=[pltpu.SemaphoreType.DMA((2, 4)), pltpu.SemaphoreType.DMA],
            compiler_params=params(2),
            cost_estimate=pl.CostEstimate(
                flops=0, transcendentals=0, bytes_accessed=4 * fresh_kv.size),
            name="stage_fresh",
        )(in_hbm(query), in_hbm(fresh_kv))
        kf, *near = lax.optimization_barrier((kf, *near))
        kb, slot_table, counts = pl.pallas_call(
            functools.partial(stage_keys_kernel, n_ctx, slots),
            out_shape=(half(pool_slots), smem(n_reqs * slots), smem(n_reqs)),
            in_specs=[HBM] * 2,
            out_specs=(VMEM, SMEM, SMEM),
            scratch_shapes=[
                pltpu.SMEM((new_dev,), jnp.int32), pltpu.SemaphoreType.DMA((pieces,)),
                pltpu.SemaphoreType.DMA],
            compiler_params=params(2),
            cost_estimate=pl.CostEstimate(
                flops=0, transcendentals=0, bytes_accessed=2 * kv_pool.size),
            name="stage_keys",
        )(in_hbm(fresh_bucket), pool)
        kb, kf, vf = (a.reshape(a.shape[0], page_rows, LANES) for a in (kb, kf, vf))
        value_in, value_specs = (pool,), [HBM]
        value_out = (bf16(pool_slots, page // 2, heads, LANES),)
        value_scratch = [pltpu.SemaphoreType.DMA((pieces,))]
    else:
        kb, vb, kf, vf = (
            a[..., h * LANES:(h + 1) * LANES].reshape(a.shape[0], page_rows, LANES)
            for a in (kv_pool, fresh_kv) for h in (0, 1)
        )
        slot_table, counts = pl.pallas_call(
            functools.partial(list_kernel, n_ctx, slots),
            out_shape=(smem(n_reqs * slots), smem(n_reqs)),
            in_specs=[SMEM],
            out_specs=(SMEM,) * 2,
            name="list",
        )(fresh_bucket)
        value_in, value_specs, value_out, value_scratch = (), [], (), []

    queries = jnp.stack([query] + near).transpose(1, 2, 0, 3, 4).reshape(req_dev, rows, head_dim)
    far = [swap(queries, "req", k) for k in range(n_req - 1, 0, -1)][::-1]

    slabs = req_dev * heads + 1
    left = sub // 2
    keep, send, facc, ftop, ftot, *vbs = pl.pallas_call(
        functools.partial(fresh_kernel, (heads, page_rows, slots, sub), pieces, n_req),
        out_shape=(
            f32(n_req - 1, slabs, left, LANES), bf16(n_req - 1, slabs, left, LANES),
            f32(req_dev, rows, LANES), f32(req_dev, sub, LANES), f32(req_dev, sub, LANES),
        ) + value_out,
        in_specs=[SMEM] * 2 + [VMEM] * (2 + n_req) + value_specs,
        out_specs=(VMEM,) * (5 + len(value_out)),
        scratch_shapes=[
            pltpu.VMEM((n_reqs, sub, slots * page_rows), jnp.float32),
            pltpu.VMEM((n_reqs, rows, slots * page_rows), jnp.bfloat16),
        ] + value_scratch,
        compiler_params=params(8),
        cost_estimate=pl.CostEstimate(
            flops=4 * n_reqs * rows * slots * page_rows * LANES,
            transcendentals=n_reqs * sub * slots * page_rows, bytes_accessed=2 * fresh_kv.size),
        name="fresh",
    )(slot_table, counts, kf, vf, queries, *far, *value_in)

    def merge(keep, got, skip, goals, shapes):
        return pl.pallas_call(
            functools.partial(merge_kernel, heads, skip, goals),
            out_shape=shapes,
            in_specs=[VMEM] * 2,
            out_specs=[VMEM] * len(shapes),
            compiler_params=params(8),
            name="merge",
        )(keep, got)

    def halved(keep, got):
        shape = (keep.shape[0], slabs, keep.shape[2] // 2, LANES)
        return merge(keep, got, 0, [None] * keep.shape[0], [f32(*shape), bf16(*shape)])

    def sorted_by(keep, got, skip, offsets, bit):
        sends = [offset for offset in offsets if offset & bit]
        keeps = [offset for offset in offsets if not offset & bit]
        goals = [
            (0, sends.index(o)) if o in sends else (1, keeps.index(o)) for o in offsets]
        shape = lambda count: (count, slabs, group, LANES)
        shapes = [bf16(*shape(len(sends)))] + ([f32(*shape(len(keeps)))] if keeps else [])
        return merge(keep, got, skip, goals, shapes), keeps

    ctx_bits = list(bits_of("ctx"))[::-1]
    req_bits = list(bits_of("req"))[::-1]
    dims = (heads, page_rows, pages_dev, sub)
    table = page_table.reshape(-1)
    part = req_dev // 2
    cost = lambda scores, values: pl.CostEstimate(
        flops=2 * (scores + values) * rows * columns * LANES,
        transcendentals=values * sub * columns,
        bytes_accessed=(scores + values) * columns * LANES * 2)
    send, queries = lax.optimization_barrier((send, queries))
    got = swap(send, "ctx", ctx_bits[0])

    def score_call(first, copied):
        return pl.pallas_call(
            functools.partial(score_kernel, dims, first, pieces if copied else 0),
            out_shape=(f32(part, sub, columns), f32(part, sub, LANES))
            + (value_out if copied else ()),
            in_specs=[SMEM] * 2 + [VMEM] * 2 + (value_specs if copied else []),
            out_specs=(VMEM,) * (2 + len(value_out) * copied),
            scratch_shapes=value_scratch if copied else [],
            compiler_params=params(4),
            cost_estimate=cost(part, 0),
            name="scores",
        )(table, context_len, queries, kb, *(value_in if copied else ()))

    t, top = score_call(0, False)
    got, top = lax.optimization_barrier((got, top))
    for bit in ctx_bits[1:]:
        keep, send = halved(keep, got)
        send, queries = lax.optimization_barrier((send, queries))
        got = swap(send, "ctx", bit)
    later, later_top, *more = score_call(part, True)
    vbs = [a.reshape(a.shape[0], -1, LANES) for a in vbs + more] if split else [vb]
    got, later_top = lax.optimization_barrier((got, later_top))
    offsets = list(range(1, n_req))
    (send, *kept), offsets = sorted_by(keep, got, 0, offsets, req_bits[0])
    send, later_top = lax.optimization_barrier((send, later_top))
    got = swap(send, "req", req_bits[0])
    arrived = [got]
    own_keep, *own_sends = pl.pallas_call(
        functools.partial(value_kernel, dims, len(vbs)),
        out_shape=(f32(1, slabs, group, LANES),)
        + (bf16(1, slabs, group, LANES),) * (n_ctx - 1),
        in_specs=[SMEM] + [VMEM] * (7 + len(vbs)),
        out_specs=(VMEM,) * n_ctx,
        scratch_shapes=[
            pltpu.VMEM((part, rows, LANES), jnp.float32),
            pltpu.VMEM((part, sub, LANES), jnp.float32)] * 2,
        compiler_params=params(4),
        cost_estimate=cost(0, req_dev),
        name="values",
    )(table, t, top, later, later_top, facc, ftop, ftot, *vbs)
    got, own_keep = lax.optimization_barrier((got, own_keep))
    for bit in req_bits[1:]:
        (send, *kept), offsets = sorted_by(kept[0], got, 1, offsets, bit)
        send, *own_sends = lax.optimization_barrier((send, *own_sends))
        got = swap(send, "req", bit)
        arrived.append(got)
    arrived += [
        swap(one, "ctx", offset) for one, offset in zip(own_sends, ctx_offsets[1:])]
    return pl.pallas_call(
        last_kernel,
        out_shape=bf16(req_dev, heads, group, LANES),
        in_specs=[VMEM] * (1 + len(arrived)),
        out_specs=VMEM,
        compiler_params=params(8),
        name="last",
    )(own_keep, *arrived)


def solution(mesh):
    placed = (
        P("req", "kvh", "ctx", None),
        P(("req", "ctx"), None, "kvh", None),
        P("req", "ctx"),
        P("req"),
        P(("req", "ctx"), None, "kvh", None),
        P(("req", "ctx")),
    )
    return jax.shard_map(
        local, mesh=mesh, in_specs=placed, out_specs=P("req", "kvh", "ctx", None), check_vma=False
    )
```

```python
import functools
import math

import jax
import jax.numpy as jnp
from jax import lax
from jax.experimental import pallas as pl
from jax.experimental.pallas import tpu as pltpu
from jax.sharding import PartitionSpec as P

NEG = -1e30
CAP = 2
LANES = 128
SCALE = math.log2(math.e) / math.sqrt(LANES)
SCORE_WIDE = 512
VALUE_WIDE = 512
VMEM = pl.BlockSpec(memory_space=pltpu.VMEM)
SMEM = pl.BlockSpec(memory_space=pltpu.SMEM)
HBM = pl.BlockSpec(memory_space=pltpu.HBM)


def swap(value, axis, bit):
    return lax.ppermute(value, axis, [(n, n ^ bit) for n in range(lax.axis_size(axis))])


def bits_of(axis):
    bit = lax.axis_size(axis) // 2
    while bit:
        yield bit
        bit //= 2


def half_copies(pool_ref, target, sem, half, pieces, tokens=None):
    each = pool_ref.shape[0] // pieces
    tokens = tokens or pl.ds(0, pool_ref.shape[1])
    return [
        pltpu.make_async_copy(
            pool_ref.at[pl.ds(n * each, each), tokens, :, pl.ds(half * LANES, LANES)],
            target.at[pl.ds(n * each, each)], sem.at[n])
        for n in range(pieces)
    ]


class ValueCopies:
    def __init__(self, refs, part, pieces):
        self.copies = []
        if pieces:
            pool_ref, target, sem = refs
            count = pool_ref.shape[1] // 2
            self.copies = half_copies(
                pool_ref, target, sem, 1, pieces, pl.ds(part * count, count))

    def start(self):
        for one in self.copies:
            one.start()

    def wait(self):
        for one in self.copies:
            one.wait()


def stage_fresh_kernel(query_hbm, fresh_ref, query_ref, kf, vf, sem, query_sem):
    copies = [pltpu.make_async_copy(query_hbm, query_ref, query_sem)]
    for half, to in enumerate((kf, vf)):
        copies += half_copies(fresh_ref, to, sem.at[half], half, sem.shape[1])
    for one in copies:
        one.start()
    for one in copies:
        one.wait()


def stage_keys_kernel(
    n_ctx, slots, bucket_hbm, pool_ref, kb, slots_ref, counts_ref, bucket_ref, sem, bucket_sem,
):
    listed = pltpu.make_async_copy(bucket_hbm, bucket_ref, bucket_sem)
    copies = half_copies(pool_ref, kb, sem, 0, sem.shape[0])
    listed.start()
    for one in copies:
        one.start()
    listed.wait()
    list_fresh(n_ctx, slots, bucket_ref, slots_ref, counts_ref)
    for one in copies:
        one.wait()


def list_kernel(n_ctx, slots, bucket_ref, slots_ref, counts_ref):
    list_fresh(n_ctx, slots, bucket_ref, slots_ref, counts_ref)


def list_fresh(n_ctx, slots, bucket_ref, slots_ref, counts_ref):
    for n in range(counts_ref.shape[0]):
        counts_ref[n] = 0
    for n in range(slots_ref.shape[0]):
        slots_ref[n] = 0

    def put(page, _):
        request = bucket_ref[page] >> (n_ctx.bit_length() - 1)
        count = counts_ref[request]
        slots_ref[request * slots + count] = page
        counts_ref[request] = count + 1
        return 0

    lax.fori_loop(0, bucket_ref.shape[0], put, 0, unroll=16)


def class_reduce(x, op, heads):
    step = heads
    while step < LANES:
        x = op(x, pltpu.roll(x, step, 1))
        step *= 2
    return x


def pages_of(refs, table_ref, first, count):
    pages = [table_ref[first + n] for n in range(count)]
    return jnp.concatenate([ref[page] for page in pages for ref in refs], axis=0)


def score_parts(q, keys, lane, limit, first, heads, sub):
    half = keys.shape[0] // 2
    none = jnp.zeros_like(q)
    pair = jnp.concatenate(
        [jnp.concatenate([q, none], axis=1), jnp.concatenate([none, q], axis=1)], axis=0)
    s = lax.dot_general(
        pair, jnp.concatenate([keys[:half], keys[half:]], axis=1), (((1,), (1,)), ((), ())),
        preferred_element_type=jnp.float32)
    out = []
    for j in range(2 * half // LANES):
        base = 0 if j * LANES < half else q.shape[0]
        at = j * LANES % half
        part = s[base:base + q.shape[0], at:at + LANES]
        one = part[:sub]
        for h in range(1, heads):
            one = jnp.where(lane % heads == h, part[h * sub:(h + 1) * sub], one)
        out.append(jnp.where(lane < limit - (first + j * LANES), one * SCALE, NEG))
    return out


def spread(p, onehots):
    p = p.astype(jnp.bfloat16)
    return jnp.concatenate([p * one for one in onehots], axis=0)


def rows_of(x, h):
    return jnp.broadcast_to(x[:, h:h + 1], x.shape)


def fold_max(parts):
    top = parts[0]
    for part in parts[1:]:
        top = jnp.maximum(top, part)
    return top


def score_request(dims, i, table_ref, len_ref, q_ref, kb, t_ref, top_ref, at):
    heads, page_rows, pages_dev, sub = dims
    columns = pages_dev * page_rows
    wide = min(SCORE_WIDE, columns)
    per = wide // page_rows
    lane = lax.broadcasted_iota(jnp.int32, (sub, LANES), 1)
    top = jnp.full((sub, LANES), NEG, jnp.float32)
    limit = len_ref[i] * heads - lax.axis_index("ctx") * columns
    for c in range(columns // wide):
        keys = pages_of([kb], table_ref, i * pages_dev + c * per, per)
        parts = score_parts(q_ref[i], keys, lane, limit, c * wide, heads, sub)
        for j, part in enumerate(parts):
            t_ref[at, :, c * wide + j * LANES:c * wide + (j + 1) * LANES] = part
        top = jnp.maximum(top, fold_max(parts))
    top_ref[at] = top


def value_request(dims, i, table_ref, t_ref, top_ref, at, vbs, acc_ref, tot_ref):
    heads, page_rows, pages_dev, sub = dims
    columns = pages_dev * page_rows
    wide = min(VALUE_WIDE, columns)
    per = wide // page_rows
    lane = lax.broadcasted_iota(jnp.int32, (sub, LANES), 1)
    onehots = [(lane % heads == h).astype(jnp.bfloat16) for h in range(heads)]
    tot = jnp.zeros((sub, LANES), jnp.float32)
    acc = jnp.zeros((heads * sub, LANES), jnp.float32)
    top = top_ref[at]
    for c in range(columns // wide):
        weights = []
        for j in range(wide // LANES):
            where = c * wide + j * LANES
            p = jnp.exp2(t_ref[at, :, where:where + LANES] - top)
            tot = tot + p
            weights.append(spread(p, onehots))
        values = pages_of(vbs, table_ref, i * pages_dev + c * per, per)
        acc = acc + jnp.dot(
            jnp.concatenate(weights, axis=1), values, preferred_element_type=jnp.float32)
    acc_ref[at] = acc
    tot_ref[at] = tot


def reduce_rows(ref, op, heads):
    flat = ref[...].reshape(ref.shape[0] * ref.shape[1], LANES)
    return class_reduce(flat, op, heads)


def first_kernel(dims, pieces, table_ref, len_ref, q_ref, kb, *refs):
    refs = list(refs)
    pool = [refs.pop(0)] if pieces else []
    t_ref, top_ref, *refs = refs
    copies = ValueCopies(pool + refs, 1, pieces)
    copies.start()

    def step(i, _):
        score_request(dims, i, table_ref, len_ref, q_ref, kb, t_ref, top_ref, i)
        return 0

    lax.fori_loop(0, t_ref.shape[0], step, 0)
    top_ref[...] = reduce_rows(top_ref, jnp.maximum, dims[0]).reshape(top_ref.shape)
    copies.wait()


def middle_kernel(dims, table_ref, len_ref, q_ref, kb, t_ref, top_ref, *refs):
    *vbs, later_ref, later_top_ref, acc_ref, tot_ref = refs
    half = t_ref.shape[0]

    def step(i, _):
        score_request(
            dims, half + i, table_ref, len_ref, q_ref, kb, later_ref, later_top_ref, i)
        value_request(dims, i, table_ref, t_ref, top_ref, i, vbs, acc_ref, tot_ref)
        return 0

    lax.fori_loop(0, half, step, 0)
    later_top_ref[...] = reduce_rows(
        later_top_ref, jnp.maximum, dims[0]).reshape(later_top_ref.shape)


def second_kernel(
    dims, n_vbs, table_ref, t_ref, top_ref, first_top_ref, first_acc_ref, first_tot_ref, facc_ref,
    ftop_ref, ftot_ref, *refs,
):
    heads, page_rows, pages_dev, sub = dims
    half = t_ref.shape[0]
    req_dev = ftop_ref.shape[0]
    vbs, (keep_ref, *send_refs, acc_s, tot_s) = refs[:n_vbs], refs[n_vbs:]
    group = keep_ref.shape[2]

    def put(slab, value, coded=0):
        keep_ref[0, slab] = value[:group]
        for place, ref in enumerate(send_refs):
            send = value[(place + 1) * group:(place + 2) * group]
            ref[0, slab] = pieces_of(send, coded) if coded else send.astype(jnp.bfloat16)

    def step(i, _):
        value_request(dims, half + i, table_ref, t_ref, top_ref, i, vbs, acc_s, tot_s)
        return 0

    lax.fori_loop(0, half, step, 0)
    flat = (req_dev * sub, LANES)
    tots = jnp.concatenate(
        [reduce_rows(ref, jnp.add, heads) for ref in (first_tot_ref, tot_s)], axis=0)
    top = jnp.concatenate(
        [ref[...].reshape(half * sub, LANES) for ref in (first_top_ref, top_ref)], axis=0)
    ftop = ftop_ref[...].reshape(flat)
    both = jnp.maximum(top, ftop)
    fade, ffade = jnp.exp2(top - both), jnp.exp2(ftop - both)
    tots = tots * fade + ftot_ref[...].reshape(flat) * ffade
    fade, ffade = fade / tots, ffade / tots
    lses = both + jnp.log2(tots)
    for i in range(req_dev):
        acc_ref = first_acc_ref if i < half else acc_s
        rows = slice(i * sub, (i + 1) * sub)
        for h in range(heads):
            part = slice(h * sub, (h + 1) * sub)
            some = acc_ref[i % half, part, :] * rows_of(fade[rows], h)
            some = some + facc_ref[i, part, :] * rows_of(ffade[rows], h)
            put(i * heads + h, some)
    put(req_dev * heads, by_request(lses, heads, sub, range(req_dev)), heads)


def put_rows(keep_ref, send_ref, place, value, heads=0):
    half = value.shape[0] // 2
    send = value[half:]
    keep_ref[place] = value[:half]
    send_ref[place] = pieces_of(send, heads) if heads else send.astype(jnp.bfloat16)


def by_request(lses, heads, sub, requests):
    lane = lax.broadcasted_iota(jnp.int32, (sub, LANES), 1)
    out = jnp.zeros((sub, LANES), jnp.float32)
    for i, n in enumerate(requests):
        out = jnp.where(lane // (4 * heads) == i, lses[n * sub:(n + 1) * sub], out)
    return out


def fresh_kernel(dims, pieces, n_req, slots_ref, counts_ref, kf, vf, *refs):
    heads, page_rows, slots, sub = dims
    q_refs, refs = refs[:n_req], list(refs[n_req:])
    req_dev = q_refs[0].shape[0]
    pool = [refs.pop(0)] if pieces else []
    keep_ref, send_ref, acc_ref, top_ref, tot_ref, *refs = refs
    target = [refs.pop(0)] if pieces else []
    t_s, p_s, *sem = refs
    copies = ValueCopies(pool + target + sem, 0, pieces)
    copies.start()
    lane = lax.broadcasted_iota(jnp.int32, (sub, LANES), 1)
    onehots = [(lane % heads == h).astype(jnp.bfloat16) for h in range(heads)]
    columns = slots * page_rows
    wide = min(SCORE_WIDE, columns)
    per = wide // page_rows
    own = lax.axis_index("req")
    requests = [(own ^ k) * req_dev + i for k in range(n_req) for i in range(req_dev)]
    n_reqs = len(requests)
    tops = []
    for n, request in enumerate(requests):
        limit = counts_ref[request] * page_rows
        top = jnp.full((sub, LANES), NEG, jnp.float32)
        for c in range(columns // wide):
            keys = pages_of([kf], slots_ref, request * slots + c * per, per)
            parts = score_parts(
                q_refs[n // req_dev][n % req_dev], keys, lane, limit, c * wide, heads, sub)
            for j, part in enumerate(parts):
                t_s[n, :, c * wide + j * LANES:c * wide + (j + 1) * LANES] = part
            top = jnp.maximum(top, fold_max(parts))
        tops.append(top)
    tops = class_reduce(jnp.concatenate(tops, axis=0), jnp.maximum, heads)
    tots = []
    for n in range(n_reqs):
        tot = jnp.zeros((sub, LANES), jnp.float32)
        for j in range(columns // LANES):
            p = jnp.exp2(
                t_s[n, :, j * LANES:(j + 1) * LANES] - tops[n * sub:(n + 1) * sub])
            tot = tot + p
            p_s[n, :, j * LANES:(j + 1) * LANES] = spread(p, onehots)
        tots.append(tot)
    tots = class_reduce(jnp.concatenate(tots, axis=0), jnp.add, heads)
    whole = 1.0 / tots
    lses = tops + jnp.log2(tots)
    for n, request in enumerate(requests):
        values = pages_of([vf], slots_ref, request * slots, slots)
        acc = jnp.dot(p_s[n], values, preferred_element_type=jnp.float32)
        rows = slice(n * sub, (n + 1) * sub)
        block, i = n // req_dev - 1, n % req_dev
        if block < 0:
            acc_ref[i] = acc
            top_ref[i] = tops[rows]
            tot_ref[i] = tots[rows]
            continue
        for h in range(heads):
            some = acc[h * sub:(h + 1) * sub] * rows_of(whole[rows], h)
            put_rows(keep_ref, send_ref, (block, i * heads + h), some)
    for block in range(n_req - 1):
        first = (block + 1) * req_dev
        lse = by_request(lses, heads, sub, range(first, first + req_dev))
        put_rows(keep_ref, send_ref, (block, req_dev * heads), lse, heads)
    copies.wait()


def pieces_of(lse, heads):
    lane = lax.broadcasted_iota(jnp.int32, lse.shape, 1)
    kind = lane % (4 * heads) // heads
    high = lse.astype(jnp.bfloat16).astype(jnp.float32)
    rest = lse - high
    mid = rest.astype(jnp.bfloat16).astype(jnp.float32)
    both = jnp.where(kind == 1, mid, rest - mid)
    return jnp.where(kind == 0, high, both).astype(jnp.bfloat16)


def whole_of(pieces, heads):
    x = pieces.astype(jnp.float32)
    lane = lax.broadcasted_iota(jnp.int32, x.shape, 1)
    kind = lane % (4 * heads) // heads
    x = x + pltpu.roll(x, LANES - heads, 1) + pltpu.roll(x, LANES - 2 * heads, 1)
    same = x
    for m in (1, 2):
        same = jnp.where(kind == m, pltpu.roll(x, m * heads, 1), same)
    return same


def merge_kernel(heads, skip, goals, keep_ref, got_ref, *outs):
    blocks, slabs, rows, _ = keep_ref.shape
    slabs -= 1

    def put(block, slab, value, coded=0):
        if goals[block] is None:
            put_rows(outs[0], outs[1], (block, slab), value, coded)
        else:
            which, place = goals[block]
            if outs[which].dtype == jnp.bfloat16:
                value = pieces_of(value, coded) if coded else value.astype(jnp.bfloat16)
            outs[which][place, slab] = value

    for block in range(blocks):
        own = keep_ref[block, slabs]
        other = whole_of(got_ref[block + skip, slabs], heads)
        top = jnp.maximum(own, other)
        share = jnp.exp2(own - top)
        tot = share + jnp.exp2(other - top)
        share = share / tot
        for slab in range(slabs):
            at = slab // heads * 4 * heads + slab % heads
            part = jnp.broadcast_to(share[:, at:at + 1], (rows, LANES))
            kept = keep_ref[block, slab]
            got = got_ref[block + skip, slab].astype(jnp.float32)
            put(block, slab, part * kept + (1.0 - part) * got)
        put(block, slabs, top + jnp.log2(tot), heads)


def last_kernel(keep_ref, *refs):
    *got_refs, out_ref = refs
    req_dev, heads, group, _ = out_ref.shape
    slabs = req_dev * heads
    parts = [keep_ref.at[0]] + [ref.at[0] for ref in got_refs]
    lses = [keep_ref[0, slabs]] + [whole_of(ref[0, slabs], heads) for ref in got_refs]
    top = fold_max(lses)
    shares = [jnp.exp2(lse - top) for lse in lses]
    tot = shares[0]
    for share in shares[1:]:
        tot = tot + share
    shares = [share / tot for share in shares]
    for slab in range(slabs):
        at = slab // heads * 4 * heads + slab % heads
        total = jnp.zeros((group, LANES), jnp.float32)
        for part, share in zip(parts, shares):
            total = total + part[slab].astype(jnp.float32) * jnp.broadcast_to(
                share[:, at:at + 1], (group, LANES))
        out_ref[slab // heads, slab % heads] = total.astype(jnp.bfloat16)


def params(mib):
    return pltpu.CompilerParams(vmem_limit_bytes=mib * 2**20)


def local(query, kv_pool, page_table, context_len, fresh_kv, fresh_bucket):
    n_ctx = lax.axis_size("ctx")
    n_req = lax.axis_size("req")
    req_dev, heads, group, head_dim = query.shape
    pool_slots, page = kv_pool.shape[:2]
    new_dev = fresh_kv.shape[0]
    pages_dev = page_table.shape[1]
    n_reqs = n_req * req_dev
    slots = CAP * n_ctx
    sub = n_ctx * group
    rows = heads * sub
    page_rows = page * heads

    smem = lambda count: jax.ShapeDtypeStruct((count,), jnp.int32)
    bf16 = lambda *shape: jax.ShapeDtypeStruct(shape, jnp.bfloat16)
    f32 = lambda *shape: jax.ShapeDtypeStruct(shape, jnp.float32)
    columns = pages_dev * page_rows
    split = heads % 4 == 0
    pieces = 8 if split else 0

    ctx_offsets = [0]
    for bit in bits_of("ctx"):
        ctx_offsets += [offset ^ bit for offset in ctx_offsets]
    near = [swap(query, "ctx", offset) for offset in ctx_offsets[1:]]
    if split:
        in_hbm = lambda a: pltpu.with_memory_space_constraint(a, pltpu.HBM)
        pool = in_hbm(kv_pool)
        half = lambda count: bf16(count, page, heads, LANES)
        query, kf, vf = pl.pallas_call(
            stage_fresh_kernel,
            out_shape=(bf16(*query.shape), half(new_dev), half(new_dev)),
            in_specs=[HBM] * 2,
            out_specs=(VMEM,) * 3,
            scratch_shapes=[pltpu.SemaphoreType.DMA((2, 4)), pltpu.SemaphoreType.DMA],
            compiler_params=params(2),
            cost_estimate=pl.CostEstimate(
                flops=0, transcendentals=0, bytes_accessed=4 * fresh_kv.size),
            name="stage_fresh",
        )(in_hbm(query), in_hbm(fresh_kv))
        kf, *near = lax.optimization_barrier((kf, *near))
        kb, slot_table, counts = pl.pallas_call(
            functools.partial(stage_keys_kernel, n_ctx, slots),
            out_shape=(half(pool_slots), smem(n_reqs * slots), smem(n_reqs)),
            in_specs=[HBM] * 2,
            out_specs=(VMEM, SMEM, SMEM),
            scratch_shapes=[
                pltpu.SMEM((new_dev,), jnp.int32), pltpu.SemaphoreType.DMA((pieces,)),
                pltpu.SemaphoreType.DMA],
            compiler_params=params(2),
            cost_estimate=pl.CostEstimate(
                flops=0, transcendentals=0, bytes_accessed=2 * kv_pool.size),
            name="stage_keys",
        )(in_hbm(fresh_bucket), pool)
        kb, kf, vf = (a.reshape(a.shape[0], page_rows, LANES) for a in (kb, kf, vf))
        value_in, value_specs = (pool,), [HBM]
        value_out = (bf16(pool_slots, page // 2, heads, LANES),)
        value_scratch = [pltpu.SemaphoreType.DMA((pieces,))]
    else:
        kb, vb, kf, vf = (
            a[..., h * LANES:(h + 1) * LANES].reshape(a.shape[0], page_rows, LANES)
            for a in (kv_pool, fresh_kv) for h in (0, 1)
        )
        slot_table, counts = pl.pallas_call(
            functools.partial(list_kernel, n_ctx, slots),
            out_shape=(smem(n_reqs * slots), smem(n_reqs)),
            in_specs=[SMEM],
            out_specs=(SMEM,) * 2,
            name="list",
        )(fresh_bucket)
        value_in, value_specs, value_out, value_scratch = (), [], (), []

    queries = jnp.stack([query] + near).transpose(1, 2, 0, 3, 4).reshape(req_dev, rows, head_dim)
    far = [swap(queries, "req", k) for k in range(n_req - 1, 0, -1)][::-1]

    slabs = req_dev * heads + 1
    left = sub // 2
    keep, send, facc, ftop, ftot, *vbs = pl.pallas_call(
        functools.partial(fresh_kernel, (heads, page_rows, slots, sub), pieces, n_req),
        out_shape=(
            f32(n_req - 1, slabs, left, LANES), bf16(n_req - 1, slabs, left, LANES),
            f32(req_dev, rows, LANES), f32(req_dev, sub, LANES), f32(req_dev, sub, LANES),
        ) + value_out,
        in_specs=[SMEM] * 2 + [VMEM] * (2 + n_req) + value_specs,
        out_specs=(VMEM,) * (5 + len(value_out)),
        scratch_shapes=[
            pltpu.VMEM((n_reqs, sub, slots * page_rows), jnp.float32),
            pltpu.VMEM((n_reqs, rows, slots * page_rows), jnp.bfloat16),
        ] + value_scratch,
        compiler_params=params(8),
        cost_estimate=pl.CostEstimate(
            flops=4 * n_reqs * rows * slots * page_rows * LANES,
            transcendentals=n_reqs * sub * slots * page_rows, bytes_accessed=2 * fresh_kv.size),
        name="fresh",
    )(slot_table, counts, kf, vf, queries, *far, *value_in)

    def merge(keep, got, skip, goals, shapes):
        return pl.pallas_call(
            functools.partial(merge_kernel, heads, skip, goals),
            out_shape=shapes,
            in_specs=[VMEM] * 2,
            out_specs=[VMEM] * len(shapes),
            compiler_params=params(8),
            name="merge",
        )(keep, got)

    def halved(keep, got):
        shape = (keep.shape[0], slabs, keep.shape[2] // 2, LANES)
        return merge(keep, got, 0, [None] * keep.shape[0], [f32(*shape), bf16(*shape)])

    def sorted_by(keep, got, skip, offsets, bit):
        sends = [offset for offset in offsets if offset & bit]
        keeps = [offset for offset in offsets if not offset & bit]
        goals = [
            (0, sends.index(o)) if o in sends else (1, keeps.index(o)) for o in offsets]
        shape = lambda count: (count, slabs, group, LANES)
        shapes = [bf16(*shape(len(sends)))] + ([f32(*shape(len(keeps)))] if keeps else [])
        return merge(keep, got, skip, goals, shapes), keeps

    ctx_bits = list(bits_of("ctx"))[::-1]
    req_bits = list(bits_of("req"))[::-1]
    dims = (heads, page_rows, pages_dev, sub)
    table = page_table.reshape(-1)
    part = req_dev // 2
    cost = lambda scores, values: pl.CostEstimate(
        flops=2 * (scores + values) * rows * columns * LANES,
        transcendentals=values * sub * columns,
        bytes_accessed=(scores + values) * columns * LANES * 2)
    send, queries = lax.optimization_barrier((send, queries))
    got = swap(send, "ctx", ctx_bits[0])
    t, top, *more = pl.pallas_call(
        functools.partial(first_kernel, dims, pieces),
        out_shape=(f32(part, sub, columns), f32(part, sub, LANES)) + value_out,
        in_specs=[SMEM] * 2 + [VMEM] * 2 + value_specs,
        out_specs=(VMEM,) * (2 + len(value_out)),
        scratch_shapes=value_scratch,
        compiler_params=params(4),
        cost_estimate=cost(part, 0),
        name="first",
    )(table, context_len, queries, kb, *value_in)
    vbs = [a.reshape(a.shape[0], -1, LANES) for a in vbs + more] if split else [vb]
    got, top = lax.optimization_barrier((got, top))
    for bit in ctx_bits[1:]:
        keep, send = halved(keep, got)
        send, top = lax.optimization_barrier((send, top))
        got = swap(send, "ctx", bit)
    later, later_top, acc, tot = pl.pallas_call(
        functools.partial(middle_kernel, dims),
        out_shape=(
            f32(part, sub, columns), f32(part, sub, LANES), f32(part, rows, LANES),
            f32(part, sub, LANES)),
        in_specs=[SMEM] * 2 + [VMEM] * (4 + len(vbs)),
        out_specs=(VMEM,) * 4,
        compiler_params=params(4),
        cost_estimate=cost(part, part),
        name="middle",
    )(table, context_len, queries, kb, t, top, *vbs)
    got, later_top = lax.optimization_barrier((got, later_top))
    offsets = list(range(1, n_req))
    (send, *kept), offsets = sorted_by(keep, got, 0, offsets, req_bits[0])
    send, later_top = lax.optimization_barrier((send, later_top))
    got = swap(send, "req", req_bits[0])
    arrived = [got]
    own_keep, *own_sends = pl.pallas_call(
        functools.partial(second_kernel, dims, len(vbs)),
        out_shape=(f32(1, slabs, group, LANES),)
        + (bf16(1, slabs, group, LANES),) * (n_ctx - 1),
        in_specs=[SMEM] + [VMEM] * (8 + len(vbs)),
        out_specs=(VMEM,) * n_ctx,
        scratch_shapes=[
            pltpu.VMEM((part, rows, LANES), jnp.float32),
            pltpu.VMEM((part, sub, LANES), jnp.float32)],
        compiler_params=params(4),
        cost_estimate=cost(0, part),
        name="second",
    )(table, later, later_top, top, acc, tot, facc, ftop, ftot, *vbs)
    got, own_keep = lax.optimization_barrier((got, own_keep))
    arrived += [
        swap(one, "ctx", offset) for one, offset in zip(own_sends, ctx_offsets[1:])]
    for bit in req_bits[1:]:
        (send, *kept), offsets = sorted_by(kept[0], got, 1, offsets, bit)
        got = swap(send, "req", bit)
        arrived.append(got)
    return pl.pallas_call(
        last_kernel,
        out_shape=bf16(req_dev, heads, group, LANES),
        in_specs=[VMEM] * (1 + len(arrived)),
        out_specs=VMEM,
        compiler_params=params(8),
        name="last",
    )(own_keep, *arrived)


def solution(mesh):
    placed = (
        P("req", "kvh", "ctx", None),
        P(("req", "ctx"), None, "kvh", None),
        P("req", "ctx"),
        P("req"),
        P(("req", "ctx"), None, "kvh", None),
        P(("req", "ctx")),
    )
    return jax.shard_map(
        local, mesh=mesh, in_specs=placed, out_specs=P("req", "kvh", "ctx", None), check_vma=False
    )
```

```python
import functools
import math

import jax
import jax.numpy as jnp
from jax import lax
from jax.experimental import pallas as pl
from jax.experimental.pallas import tpu as pltpu
from jax.sharding import PartitionSpec as P

NEG = -1e30
CAP = 2
LANES = 128
SCALE = math.log2(math.e) / math.sqrt(LANES)
SCORE_WIDE = 256
VALUE_WIDE = 512
VMEM = pl.BlockSpec(memory_space=pltpu.VMEM)
SMEM = pl.BlockSpec(memory_space=pltpu.SMEM)
HBM = pl.BlockSpec(memory_space=pltpu.HBM)


def swap(value, axis, bit):
    return lax.ppermute(value, axis, [(n, n ^ bit) for n in range(lax.axis_size(axis))])


def bits_of(axis):
    bit = lax.axis_size(axis) // 2
    while bit:
        yield bit
        bit //= 2


def half_copies(pool_ref, target, sem, half, pieces, tokens=None):
    each = pool_ref.shape[0] // pieces
    tokens = tokens or pl.ds(0, pool_ref.shape[1])
    return [
        pltpu.make_async_copy(
            pool_ref.at[pl.ds(n * each, each), tokens, :, pl.ds(half * LANES, LANES)],
            target.at[pl.ds(n * each, each)], sem.at[n])
        for n in range(pieces)
    ]


class ValueCopies:
    def __init__(self, refs, part, pieces):
        self.copies = []
        if pieces:
            pool_ref, target, sem = refs
            count = pool_ref.shape[1] // 2
            self.copies = half_copies(
                pool_ref, target, sem, 1, pieces, pl.ds(part * count, count))

    def start(self):
        for one in self.copies:
            one.start()

    def wait(self):
        for one in self.copies:
            one.wait()


def stage_fresh_kernel(query_hbm, fresh_ref, query_ref, kf, vf, sem, query_sem):
    copies = [pltpu.make_async_copy(query_hbm, query_ref, query_sem)]
    for half, to in enumerate((kf, vf)):
        copies += half_copies(fresh_ref, to, sem.at[half], half, sem.shape[1])
    for one in copies:
        one.start()
    for one in copies:
        one.wait()


def stage_keys_kernel(
    n_ctx, slots, bucket_hbm, pool_ref, kb, slots_ref, counts_ref, bucket_ref, sem, bucket_sem,
):
    listed = pltpu.make_async_copy(bucket_hbm, bucket_ref, bucket_sem)
    copies = half_copies(pool_ref, kb, sem, 0, sem.shape[0])
    listed.start()
    for one in copies:
        one.start()
    listed.wait()
    list_fresh(n_ctx, slots, bucket_ref, slots_ref, counts_ref)
    for one in copies:
        one.wait()


def list_kernel(n_ctx, slots, bucket_ref, slots_ref, counts_ref):
    list_fresh(n_ctx, slots, bucket_ref, slots_ref, counts_ref)


def list_fresh(n_ctx, slots, bucket_ref, slots_ref, counts_ref):
    for n in range(counts_ref.shape[0]):
        counts_ref[n] = 0
    for n in range(slots_ref.shape[0]):
        slots_ref[n] = 0

    def put(page, _):
        request = bucket_ref[page] >> (n_ctx.bit_length() - 1)
        count = counts_ref[request]
        slots_ref[request * slots + count] = page
        counts_ref[request] = count + 1
        return 0

    lax.fori_loop(0, bucket_ref.shape[0], put, 0, unroll=16)


def class_reduce(x, op, heads):
    step = heads
    while step < LANES:
        x = op(x, pltpu.roll(x, step, 1))
        step *= 2
    return x


def pages_of(refs, table_ref, first, count):
    pages = [table_ref[first + n] for n in range(count)]
    return jnp.concatenate([ref[page] for page in pages for ref in refs], axis=0)


def score_parts(q, keys, lane, limit, first, heads, sub):
    s = lax.dot_general(q, keys, (((1,), (1,)), ((), ())), preferred_element_type=jnp.float32)
    out = []
    for j in range(s.shape[1] // LANES):
        part = s[:, j * LANES:(j + 1) * LANES]
        one = part[:sub]
        for h in range(1, heads):
            one = jnp.where(lane % heads == h, part[h * sub:(h + 1) * sub], one)
        out.append(jnp.where(lane < limit - (first + j * LANES), one * SCALE, NEG))
    return out


def spread(p, onehots):
    p = p.astype(jnp.bfloat16)
    return jnp.concatenate([p * one for one in onehots], axis=0)


def rows_of(x, h):
    return jnp.broadcast_to(x[:, h:h + 1], x.shape)


def fold_max(parts):
    top = parts[0]
    for part in parts[1:]:
        top = jnp.maximum(top, part)
    return top


def score_request(dims, i, table_ref, len_ref, q_ref, kb, t_ref, top_ref, at):
    heads, page_rows, pages_dev, sub = dims
    columns = pages_dev * page_rows
    wide = min(SCORE_WIDE, columns)
    per = wide // page_rows
    lane = lax.broadcasted_iota(jnp.int32, (sub, LANES), 1)
    top = jnp.full((sub, LANES), NEG, jnp.float32)
    limit = len_ref[i] * heads - lax.axis_index("ctx") * columns
    for c in range(columns // wide):
        keys = pages_of([kb], table_ref, i * pages_dev + c * per, per)
        parts = score_parts(q_ref[i], keys, lane, limit, c * wide, heads, sub)
        for j, part in enumerate(parts):
            t_ref[at, :, c * wide + j * LANES:c * wide + (j + 1) * LANES] = part
        top = jnp.maximum(top, fold_max(parts))
    top_ref[at] = top


def value_request(dims, i, table_ref, t_ref, top_ref, at, vbs, acc_ref, tot_ref):
    heads, page_rows, pages_dev, sub = dims
    columns = pages_dev * page_rows
    wide = min(VALUE_WIDE, columns)
    per = wide // page_rows
    lane = lax.broadcasted_iota(jnp.int32, (sub, LANES), 1)
    onehots = [(lane % heads == h).astype(jnp.bfloat16) for h in range(heads)]
    tot = jnp.zeros((sub, LANES), jnp.float32)
    acc = jnp.zeros((heads * sub, LANES), jnp.float32)
    top = top_ref[at]
    for c in range(columns // wide):
        weights = []
        for j in range(wide // LANES):
            where = c * wide + j * LANES
            p = jnp.exp2(t_ref[at, :, where:where + LANES] - top)
            tot = tot + p
            weights.append(spread(p, onehots))
        values = pages_of(vbs, table_ref, i * pages_dev + c * per, per)
        acc = acc + jnp.dot(
            jnp.concatenate(weights, axis=1), values, preferred_element_type=jnp.float32)
    acc_ref[at] = acc
    tot_ref[at] = tot


def reduce_rows(ref, op, heads):
    flat = ref[...].reshape(ref.shape[0] * ref.shape[1], LANES)
    return class_reduce(flat, op, heads)


def first_kernel(dims, pieces, table_ref, len_ref, q_ref, kb, *refs):
    refs = list(refs)
    pool = [refs.pop(0)] if pieces else []
    t_ref, top_ref, *refs = refs
    copies = ValueCopies(pool + refs, 1, pieces)
    copies.start()

    def step(i, _):
        score_request(dims, i, table_ref, len_ref, q_ref, kb, t_ref, top_ref, i)
        return 0

    lax.fori_loop(0, t_ref.shape[0], step, 0, unroll=True)
    top_ref[...] = reduce_rows(top_ref, jnp.maximum, dims[0]).reshape(top_ref.shape)
    copies.wait()


def middle_kernel(dims, table_ref, len_ref, q_ref, kb, t_ref, top_ref, *refs):
    *vbs, later_ref, later_top_ref, acc_ref, tot_ref = refs
    half = t_ref.shape[0]

    def step(i, _):
        score_request(
            dims, half + i, table_ref, len_ref, q_ref, kb, later_ref, later_top_ref, i)
        value_request(dims, i, table_ref, t_ref, top_ref, i, vbs, acc_ref, tot_ref)
        return 0

    lax.fori_loop(0, half, step, 0, unroll=True)
    later_top_ref[...] = reduce_rows(
        later_top_ref, jnp.maximum, dims[0]).reshape(later_top_ref.shape)


def second_kernel(
    dims, n_vbs, table_ref, t_ref, top_ref, first_top_ref, first_acc_ref, first_tot_ref, facc_ref,
    ftop_ref, ftot_ref, *refs,
):
    heads, page_rows, pages_dev, sub = dims
    half = t_ref.shape[0]
    req_dev = ftop_ref.shape[0]
    vbs, (keep_ref, *send_refs, acc_s, tot_s) = refs[:n_vbs], refs[n_vbs:]
    group = keep_ref.shape[2]

    def put(slab, value, coded=0):
        keep_ref[0, slab] = value[:group]
        for place, ref in enumerate(send_refs):
            send = value[(place + 1) * group:(place + 2) * group]
            ref[0, slab] = pieces_of(send, coded) if coded else send.astype(jnp.bfloat16)

    def step(i, _):
        value_request(dims, half + i, table_ref, t_ref, top_ref, i, vbs, acc_s, tot_s)
        return 0

    lax.fori_loop(0, half, step, 0, unroll=True)
    flat = (req_dev * sub, LANES)
    tots = jnp.concatenate(
        [reduce_rows(ref, jnp.add, heads) for ref in (first_tot_ref, tot_s)], axis=0)
    top = jnp.concatenate(
        [ref[...].reshape(half * sub, LANES) for ref in (first_top_ref, top_ref)], axis=0)
    ftop = ftop_ref[...].reshape(flat)
    both = jnp.maximum(top, ftop)
    fade, ffade = jnp.exp2(top - both), jnp.exp2(ftop - both)
    tots = tots * fade + ftot_ref[...].reshape(flat) * ffade
    fade, ffade = fade / tots, ffade / tots
    lses = both + jnp.log2(tots)
    for i in range(req_dev):
        acc_ref = first_acc_ref if i < half else acc_s
        rows = slice(i * sub, (i + 1) * sub)
        for h in range(heads):
            part = slice(h * sub, (h + 1) * sub)
            some = acc_ref[i % half, part, :] * rows_of(fade[rows], h)
            some = some + facc_ref[i, part, :] * rows_of(ffade[rows], h)
            put(i * heads + h, some)
    put(req_dev * heads, by_request(lses, heads, sub, range(req_dev)), heads)


def put_rows(keep_ref, send_ref, place, value, heads=0):
    half = value.shape[0] // 2
    send = value[half:]
    keep_ref[place] = value[:half]
    send_ref[place] = pieces_of(send, heads) if heads else send.astype(jnp.bfloat16)


def by_request(lses, heads, sub, requests):
    lane = lax.broadcasted_iota(jnp.int32, (sub, LANES), 1)
    out = jnp.zeros((sub, LANES), jnp.float32)
    for i, n in enumerate(requests):
        out = jnp.where(lane // (4 * heads) == i, lses[n * sub:(n + 1) * sub], out)
    return out


def fresh_kernel(dims, pieces, n_req, slots_ref, counts_ref, kf, vf, *refs):
    heads, page_rows, slots, sub = dims
    q_refs, refs = refs[:n_req], list(refs[n_req:])
    req_dev = q_refs[0].shape[0]
    pool = [refs.pop(0)] if pieces else []
    keep_ref, send_ref, acc_ref, top_ref, tot_ref, *refs = refs
    target = [refs.pop(0)] if pieces else []
    t_s, p_s, *sem = refs
    copies = ValueCopies(pool + target + sem, 0, pieces)
    copies.start()
    lane = lax.broadcasted_iota(jnp.int32, (sub, LANES), 1)
    onehots = [(lane % heads == h).astype(jnp.bfloat16) for h in range(heads)]
    columns = slots * page_rows
    wide = min(SCORE_WIDE, columns)
    per = wide // page_rows
    own = lax.axis_index("req")
    requests = [(own ^ k) * req_dev + i for k in range(n_req) for i in range(req_dev)]
    n_reqs = len(requests)
    tops = []
    for n, request in enumerate(requests):
        limit = counts_ref[request] * page_rows
        top = jnp.full((sub, LANES), NEG, jnp.float32)
        for c in range(columns // wide):
            keys = pages_of([kf], slots_ref, request * slots + c * per, per)
            parts = score_parts(
                q_refs[n // req_dev][n % req_dev], keys, lane, limit, c * wide, heads, sub)
            for j, part in enumerate(parts):
                t_s[n, :, c * wide + j * LANES:c * wide + (j + 1) * LANES] = part
            top = jnp.maximum(top, fold_max(parts))
        tops.append(top)
    tops = class_reduce(jnp.concatenate(tops, axis=0), jnp.maximum, heads)
    tots = []
    for n in range(n_reqs):
        tot = jnp.zeros((sub, LANES), jnp.float32)
        for j in range(columns // LANES):
            p = jnp.exp2(
                t_s[n, :, j * LANES:(j + 1) * LANES] - tops[n * sub:(n + 1) * sub])
            tot = tot + p
            p_s[n, :, j * LANES:(j + 1) * LANES] = spread(p, onehots)
        tots.append(tot)
    tots = class_reduce(jnp.concatenate(tots, axis=0), jnp.add, heads)
    whole = 1.0 / tots
    lses = tops + jnp.log2(tots)
    for n, request in enumerate(requests):
        values = pages_of([vf], slots_ref, request * slots, slots)
        acc = jnp.dot(p_s[n], values, preferred_element_type=jnp.float32)
        rows = slice(n * sub, (n + 1) * sub)
        block, i = n // req_dev - 1, n % req_dev
        if block < 0:
            acc_ref[i] = acc
            top_ref[i] = tops[rows]
            tot_ref[i] = tots[rows]
            continue
        for h in range(heads):
            some = acc[h * sub:(h + 1) * sub] * rows_of(whole[rows], h)
            put_rows(keep_ref, send_ref, (block, i * heads + h), some)
    for block in range(n_req - 1):
        first = (block + 1) * req_dev
        lse = by_request(lses, heads, sub, range(first, first + req_dev))
        put_rows(keep_ref, send_ref, (block, req_dev * heads), lse, heads)
    copies.wait()


def pieces_of(lse, heads):
    lane = lax.broadcasted_iota(jnp.int32, lse.shape, 1)
    kind = lane % (4 * heads) // heads
    high = lse.astype(jnp.bfloat16).astype(jnp.float32)
    rest = lse - high
    mid = rest.astype(jnp.bfloat16).astype(jnp.float32)
    both = jnp.where(kind == 1, mid, rest - mid)
    return jnp.where(kind == 0, high, both).astype(jnp.bfloat16)


def whole_of(pieces, heads):
    x = pieces.astype(jnp.float32)
    lane = lax.broadcasted_iota(jnp.int32, x.shape, 1)
    kind = lane % (4 * heads) // heads
    x = x + pltpu.roll(x, LANES - heads, 1) + pltpu.roll(x, LANES - 2 * heads, 1)
    same = x
    for m in (1, 2):
        same = jnp.where(kind == m, pltpu.roll(x, m * heads, 1), same)
    return same


def merge_kernel(heads, skip, goals, keep_ref, got_ref, *outs):
    blocks, slabs, rows, _ = keep_ref.shape
    slabs -= 1

    def put(block, slab, value, coded=0):
        if goals[block] is None:
            put_rows(outs[0], outs[1], (block, slab), value, coded)
        else:
            which, place = goals[block]
            if outs[which].dtype == jnp.bfloat16:
                value = pieces_of(value, coded) if coded else value.astype(jnp.bfloat16)
            outs[which][place, slab] = value

    for block in range(blocks):
        own = keep_ref[block, slabs]
        other = whole_of(got_ref[block + skip, slabs], heads)
        top = jnp.maximum(own, other)
        share = jnp.exp2(own - top)
        tot = share + jnp.exp2(other - top)
        share = share / tot
        for slab in range(slabs):
            at = slab // heads * 4 * heads + slab % heads
            part = jnp.broadcast_to(share[:, at:at + 1], (rows, LANES))
            kept = keep_ref[block, slab]
            got = got_ref[block + skip, slab].astype(jnp.float32)
            put(block, slab, part * kept + (1.0 - part) * got)
        put(block, slabs, top + jnp.log2(tot), heads)


def last_kernel(keep_ref, *refs):
    *got_refs, out_ref = refs
    req_dev, heads, group, _ = out_ref.shape
    slabs = req_dev * heads
    parts = [keep_ref.at[0]] + [ref.at[0] for ref in got_refs]
    lses = [keep_ref[0, slabs]] + [whole_of(ref[0, slabs], heads) for ref in got_refs]
    top = fold_max(lses)
    shares = [jnp.exp2(lse - top) for lse in lses]
    tot = shares[0]
    for share in shares[1:]:
        tot = tot + share
    shares = [share / tot for share in shares]
    for slab in range(slabs):
        at = slab // heads * 4 * heads + slab % heads
        total = jnp.zeros((group, LANES), jnp.float32)
        for part, share in zip(parts, shares):
            total = total + part[slab].astype(jnp.float32) * jnp.broadcast_to(
                share[:, at:at + 1], (group, LANES))
        out_ref[slab // heads, slab % heads] = total.astype(jnp.bfloat16)


def params(mib):
    return pltpu.CompilerParams(vmem_limit_bytes=mib * 2**20)


def local(query, kv_pool, page_table, context_len, fresh_kv, fresh_bucket):
    n_ctx = lax.axis_size("ctx")
    n_req = lax.axis_size("req")
    req_dev, heads, group, head_dim = query.shape
    pool_slots, page = kv_pool.shape[:2]
    new_dev = fresh_kv.shape[0]
    pages_dev = page_table.shape[1]
    n_reqs = n_req * req_dev
    slots = CAP * n_ctx
    sub = n_ctx * group
    rows = heads * sub
    page_rows = page * heads

    smem = lambda count: jax.ShapeDtypeStruct((count,), jnp.int32)
    bf16 = lambda *shape: jax.ShapeDtypeStruct(shape, jnp.bfloat16)
    f32 = lambda *shape: jax.ShapeDtypeStruct(shape, jnp.float32)
    columns = pages_dev * page_rows
    split = heads % 4 == 0
    pieces = 8 if split else 0

    ctx_offsets = [0]
    for bit in bits_of("ctx"):
        ctx_offsets += [offset ^ bit for offset in ctx_offsets]
    near = [swap(query, "ctx", offset) for offset in ctx_offsets[1:]]
    if split:
        in_hbm = lambda a: pltpu.with_memory_space_constraint(a, pltpu.HBM)
        pool = in_hbm(kv_pool)
        half = lambda count: bf16(count, page, heads, LANES)
        query, kf, vf = pl.pallas_call(
            stage_fresh_kernel,
            out_shape=(bf16(*query.shape), half(new_dev), half(new_dev)),
            in_specs=[HBM] * 2,
            out_specs=(VMEM,) * 3,
            scratch_shapes=[pltpu.SemaphoreType.DMA((2, 4)), pltpu.SemaphoreType.DMA],
            compiler_params=params(2),
            cost_estimate=pl.CostEstimate(
                flops=0, transcendentals=0, bytes_accessed=4 * fresh_kv.size),
            name="stage_fresh",
        )(in_hbm(query), in_hbm(fresh_kv))
        kf, *near = lax.optimization_barrier((kf, *near))
        kb, slot_table, counts = pl.pallas_call(
            functools.partial(stage_keys_kernel, n_ctx, slots),
            out_shape=(half(pool_slots), smem(n_reqs * slots), smem(n_reqs)),
            in_specs=[HBM] * 2,
            out_specs=(VMEM, SMEM, SMEM),
            scratch_shapes=[
                pltpu.SMEM((new_dev,), jnp.int32), pltpu.SemaphoreType.DMA((pieces,)),
                pltpu.SemaphoreType.DMA],
            compiler_params=params(2),
            cost_estimate=pl.CostEstimate(
                flops=0, transcendentals=0, bytes_accessed=2 * kv_pool.size),
            name="stage_keys",
        )(in_hbm(fresh_bucket), pool)
        kb, kf, vf = (a.reshape(a.shape[0], page_rows, LANES) for a in (kb, kf, vf))
        value_in, value_specs = (pool,), [HBM]
        value_out = (bf16(pool_slots, page // 2, heads, LANES),)
        value_scratch = [pltpu.SemaphoreType.DMA((pieces,))]
    else:
        kb, vb, kf, vf = (
            a[..., h * LANES:(h + 1) * LANES].reshape(a.shape[0], page_rows, LANES)
            for a in (kv_pool, fresh_kv) for h in (0, 1)
        )
        slot_table, counts = pl.pallas_call(
            functools.partial(list_kernel, n_ctx, slots),
            out_shape=(smem(n_reqs * slots), smem(n_reqs)),
            in_specs=[SMEM],
            out_specs=(SMEM,) * 2,
            name="list",
        )(fresh_bucket)
        value_in, value_specs, value_out, value_scratch = (), [], (), []

    queries = jnp.stack([query] + near).transpose(1, 2, 0, 3, 4).reshape(req_dev, rows, head_dim)
    far = [swap(queries, "req", k) for k in range(n_req - 1, 0, -1)][::-1]

    slabs = req_dev * heads + 1
    left = sub // 2
    keep, send, facc, ftop, ftot, *vbs = pl.pallas_call(
        functools.partial(fresh_kernel, (heads, page_rows, slots, sub), pieces, n_req),
        out_shape=(
            f32(n_req - 1, slabs, left, LANES), bf16(n_req - 1, slabs, left, LANES),
            f32(req_dev, rows, LANES), f32(req_dev, sub, LANES), f32(req_dev, sub, LANES),
        ) + value_out,
        in_specs=[SMEM] * 2 + [VMEM] * (2 + n_req) + value_specs,
        out_specs=(VMEM,) * (5 + len(value_out)),
        scratch_shapes=[
            pltpu.VMEM((n_reqs, sub, slots * page_rows), jnp.float32),
            pltpu.VMEM((n_reqs, rows, slots * page_rows), jnp.bfloat16),
        ] + value_scratch,
        compiler_params=params(8),
        cost_estimate=pl.CostEstimate(
            flops=4 * n_reqs * rows * slots * page_rows * LANES,
            transcendentals=n_reqs * sub * slots * page_rows, bytes_accessed=2 * fresh_kv.size),
        name="fresh",
    )(slot_table, counts, kf, vf, queries, *far, *value_in)

    def merge(keep, got, skip, goals, shapes):
        return pl.pallas_call(
            functools.partial(merge_kernel, heads, skip, goals),
            out_shape=shapes,
            in_specs=[VMEM] * 2,
            out_specs=[VMEM] * len(shapes),
            compiler_params=params(8),
            name="merge",
        )(keep, got)

    def halved(keep, got):
        shape = (keep.shape[0], slabs, keep.shape[2] // 2, LANES)
        return merge(keep, got, 0, [None] * keep.shape[0], [f32(*shape), bf16(*shape)])

    def sorted_by(keep, got, skip, offsets, bit):
        sends = [offset for offset in offsets if offset & bit]
        keeps = [offset for offset in offsets if not offset & bit]
        goals = [
            (0, sends.index(o)) if o in sends else (1, keeps.index(o)) for o in offsets]
        shape = lambda count: (count, slabs, group, LANES)
        shapes = [bf16(*shape(len(sends)))] + ([f32(*shape(len(keeps)))] if keeps else [])
        return merge(keep, got, skip, goals, shapes), keeps

    ctx_bits = list(bits_of("ctx"))[::-1]
    req_bits = list(bits_of("req"))[::-1]
    dims = (heads, page_rows, pages_dev, sub)
    table = page_table.reshape(-1)
    part = req_dev // 2
    cost = lambda scores, values: pl.CostEstimate(
        flops=2 * (scores + values) * rows * columns * LANES,
        transcendentals=values * sub * columns,
        bytes_accessed=(scores + values) * columns * LANES * 2)
    send, queries = lax.optimization_barrier((send, queries))
    got = swap(send, "ctx", ctx_bits[0])
    t, top, *more = pl.pallas_call(
        functools.partial(first_kernel, dims, pieces),
        out_shape=(f32(part, sub, columns), f32(part, sub, LANES)) + value_out,
        in_specs=[SMEM] * 2 + [VMEM] * 2 + value_specs,
        out_specs=(VMEM,) * (2 + len(value_out)),
        scratch_shapes=value_scratch,
        compiler_params=params(4),
        cost_estimate=cost(part, 0),
        name="first",
    )(table, context_len, queries, kb, *value_in)
    vbs = [a.reshape(a.shape[0], -1, LANES) for a in vbs + more] if split else [vb]
    got, top = lax.optimization_barrier((got, top))
    for bit in ctx_bits[1:]:
        keep, send = halved(keep, got)
        send, top = lax.optimization_barrier((send, top))
        got = swap(send, "ctx", bit)
    later, later_top, acc, tot = pl.pallas_call(
        functools.partial(middle_kernel, dims),
        out_shape=(
            f32(part, sub, columns), f32(part, sub, LANES), f32(part, rows, LANES),
            f32(part, sub, LANES)),
        in_specs=[SMEM] * 2 + [VMEM] * (4 + len(vbs)),
        out_specs=(VMEM,) * 4,
        compiler_params=params(4),
        cost_estimate=cost(part, part),
        name="middle",
    )(table, context_len, queries, kb, t, top, *vbs)
    got, later_top = lax.optimization_barrier((got, later_top))
    offsets = list(range(1, n_req))
    (send, *kept), offsets = sorted_by(keep, got, 0, offsets, req_bits[0])
    send, later_top = lax.optimization_barrier((send, later_top))
    got = swap(send, "req", req_bits[0])
    arrived = [got]
    own_keep, *own_sends = pl.pallas_call(
        functools.partial(second_kernel, dims, len(vbs)),
        out_shape=(f32(1, slabs, group, LANES),)
        + (bf16(1, slabs, group, LANES),) * (n_ctx - 1),
        in_specs=[SMEM] + [VMEM] * (8 + len(vbs)),
        out_specs=(VMEM,) * n_ctx,
        scratch_shapes=[
            pltpu.VMEM((part, rows, LANES), jnp.float32),
            pltpu.VMEM((part, sub, LANES), jnp.float32)],
        compiler_params=params(4),
        cost_estimate=cost(0, part),
        name="second",
    )(table, later, later_top, top, acc, tot, facc, ftop, ftot, *vbs)
    got, own_keep = lax.optimization_barrier((got, own_keep))
    arrived += [
        swap(one, "ctx", offset) for one, offset in zip(own_sends, ctx_offsets[1:])]
    for bit in req_bits[1:]:
        (send, *kept), offsets = sorted_by(kept[0], got, 1, offsets, bit)
        got = swap(send, "req", bit)
        arrived.append(got)
    return pl.pallas_call(
        last_kernel,
        out_shape=bf16(req_dev, heads, group, LANES),
        in_specs=[VMEM] * (1 + len(arrived)),
        out_specs=VMEM,
        compiler_params=params(8),
        name="last",
    )(own_keep, *arrived)


def solution(mesh):
    placed = (
        P("req", "kvh", "ctx", None),
        P(("req", "ctx"), None, "kvh", None),
        P("req", "ctx"),
        P("req"),
        P(("req", "ctx"), None, "kvh", None),
        P(("req", "ctx")),
    )
    return jax.shard_map(
        local, mesh=mesh, in_specs=placed, out_specs=P("req", "kvh", "ctx", None), check_vma=False
    )
```

```python
import functools
import math

import jax
import jax.numpy as jnp
from jax import lax
from jax.experimental import pallas as pl
from jax.experimental.pallas import tpu as pltpu
from jax.sharding import PartitionSpec as P

NEG = -1e30
CAP = 2
LANES = 128
SCALE = math.log2(math.e) / math.sqrt(LANES)
SCORE_WIDE = 256
VALUE_WIDE = 512
VMEM = pl.BlockSpec(memory_space=pltpu.VMEM)
SMEM = pl.BlockSpec(memory_space=pltpu.SMEM)
HBM = pl.BlockSpec(memory_space=pltpu.HBM)


def swap(value, axis, bit):
    return lax.ppermute(value, axis, [(n, n ^ bit) for n in range(lax.axis_size(axis))])


def bits_of(axis):
    bit = lax.axis_size(axis) // 2
    while bit:
        yield bit
        bit //= 2


def half_copies(pool_ref, target, sem, half, pieces, tokens=None):
    each = pool_ref.shape[0] // pieces
    tokens = tokens or pl.ds(0, pool_ref.shape[1])
    return [
        pltpu.make_async_copy(
            pool_ref.at[pl.ds(n * each, each), tokens, :, pl.ds(half * LANES, LANES)],
            target.at[pl.ds(n * each, each)], sem.at[n])
        for n in range(pieces)
    ]


class ValueCopies:
    def __init__(self, refs, part, pieces):
        self.copies = []
        if pieces:
            pool_ref, target, sem = refs
            count = pool_ref.shape[1] // 2
            self.copies = half_copies(
                pool_ref, target, sem, 1, pieces, pl.ds(part * count, count))

    def start(self):
        for one in self.copies:
            one.start()

    def wait(self):
        for one in self.copies:
            one.wait()


def stage_fresh_kernel(query_hbm, fresh_ref, query_ref, kf, vf, sem, query_sem):
    copies = [pltpu.make_async_copy(query_hbm, query_ref, query_sem)]
    for half, to in enumerate((kf, vf)):
        copies += half_copies(fresh_ref, to, sem.at[half], half, sem.shape[1])
    for one in copies:
        one.start()
    for one in copies:
        one.wait()


def stage_keys_kernel(
    n_ctx, slots, bucket_hbm, pool_ref, kb, slots_ref, counts_ref, bucket_ref, sem, bucket_sem,
):
    listed = pltpu.make_async_copy(bucket_hbm, bucket_ref, bucket_sem)
    copies = half_copies(pool_ref, kb, sem, 0, sem.shape[0])
    listed.start()
    for one in copies:
        one.start()
    listed.wait()
    list_fresh(n_ctx, slots, bucket_ref, slots_ref, counts_ref)
    for one in copies:
        one.wait()


def list_kernel(n_ctx, slots, bucket_ref, slots_ref, counts_ref):
    list_fresh(n_ctx, slots, bucket_ref, slots_ref, counts_ref)


def list_fresh(n_ctx, slots, bucket_ref, slots_ref, counts_ref):
    for n in range(counts_ref.shape[0]):
        counts_ref[n] = 0
    for n in range(slots_ref.shape[0]):
        slots_ref[n] = 0

    def put(page, _):
        request = bucket_ref[page] >> (n_ctx.bit_length() - 1)
        count = counts_ref[request]
        slots_ref[request * slots + count] = page
        counts_ref[request] = count + 1
        return 0

    lax.fori_loop(0, bucket_ref.shape[0], put, 0, unroll=16)


def class_reduce(x, op, heads):
    step = heads
    while step < LANES:
        x = op(x, pltpu.roll(x, step, 1))
        step *= 2
    return x


def pages_of(refs, table_ref, first, count):
    pages = [table_ref[first + n] for n in range(count)]
    return jnp.concatenate([ref[page] for page in pages for ref in refs], axis=0)


def score_parts(q, keys, lane, limit, first, heads, sub):
    s = lax.dot_general(q, keys, (((1,), (1,)), ((), ())), preferred_element_type=jnp.float32)
    out = []
    for j in range(s.shape[1] // LANES):
        part = s[:, j * LANES:(j + 1) * LANES]
        one = part[:sub]
        for h in range(1, heads):
            one = jnp.where(lane % heads == h, part[h * sub:(h + 1) * sub], one)
        out.append(jnp.where(lane < limit - (first + j * LANES), one * SCALE, NEG))
    return out


def spread(p, onehots):
    p = p.astype(jnp.bfloat16)
    return jnp.concatenate([p * one for one in onehots], axis=0)


def rows_of(x, h):
    return jnp.broadcast_to(x[:, h:h + 1], x.shape)


def fold_max(parts):
    top = parts[0]
    for part in parts[1:]:
        top = jnp.maximum(top, part)
    return top


def score_request(dims, i, table_ref, len_ref, q_ref, kb, t_ref, top_ref, at):
    heads, page_rows, pages_dev, sub = dims
    columns = pages_dev * page_rows
    wide = min(SCORE_WIDE, columns)
    per = wide // page_rows
    lane = lax.broadcasted_iota(jnp.int32, (sub, LANES), 1)
    top = jnp.full((sub, LANES), NEG, jnp.float32)
    limit = len_ref[i] * heads - lax.axis_index("ctx") * columns
    for c in range(columns // wide):
        keys = pages_of([kb], table_ref, i * pages_dev + c * per, per)
        parts = score_parts(q_ref[i], keys, lane, limit, c * wide, heads, sub)
        for j, part in enumerate(parts):
            t_ref[at, :, c * wide + j * LANES:c * wide + (j + 1) * LANES] = part
        top = jnp.maximum(top, fold_max(parts))
    top_ref[at] = top


def value_request(dims, i, table_ref, t_ref, top_ref, at, vbs, acc_ref, tot_ref):
    heads, page_rows, pages_dev, sub = dims
    columns = pages_dev * page_rows
    wide = min(VALUE_WIDE, columns)
    per = wide // page_rows
    lane = lax.broadcasted_iota(jnp.int32, (sub, LANES), 1)
    onehots = [(lane % heads == h).astype(jnp.bfloat16) for h in range(heads)]
    tot = jnp.zeros((sub, LANES), jnp.float32)
    acc = jnp.zeros((heads * sub, LANES), jnp.float32)
    top = top_ref[at]
    for c in range(columns // wide):
        weights = []
        for j in range(wide // LANES):
            where = c * wide + j * LANES
            p = jnp.exp2(t_ref[at, :, where:where + LANES] - top)
            tot = tot + p
            weights.append(spread(p, onehots))
        values = pages_of(vbs, table_ref, i * pages_dev + c * per, per)
        acc = acc + jnp.dot(
            jnp.concatenate(weights, axis=1), values, preferred_element_type=jnp.float32)
    acc_ref[at] = acc
    tot_ref[at] = tot


def reduce_rows(ref, op, heads):
    flat = ref[...].reshape(ref.shape[0] * ref.shape[1], LANES)
    return class_reduce(flat, op, heads)


def first_kernel(dims, pieces, table_ref, len_ref, q_ref, kb, *refs):
    refs = list(refs)
    pool = [refs.pop(0)] if pieces else []
    t_ref, top_ref, *refs = refs
    copies = ValueCopies(pool + refs, 1, pieces)
    copies.start()

    def step(i, _):
        score_request(dims, i, table_ref, len_ref, q_ref, kb, t_ref, top_ref, i)
        return 0

    lax.fori_loop(0, t_ref.shape[0], step, 0, unroll=True)
    top_ref[...] = reduce_rows(top_ref, jnp.maximum, dims[0]).reshape(top_ref.shape)
    copies.wait()


def middle_kernel(dims, table_ref, len_ref, q_ref, kb, t_ref, top_ref, *refs):
    *vbs, later_ref, later_top_ref, acc_ref, tot_ref = refs
    half = t_ref.shape[0]

    def step(i, _):
        score_request(
            dims, half + i, table_ref, len_ref, q_ref, kb, later_ref, later_top_ref, i)
        value_request(dims, i, table_ref, t_ref, top_ref, i, vbs, acc_ref, tot_ref)
        return 0

    lax.fori_loop(0, half, step, 0, unroll=True)
    later_top_ref[...] = reduce_rows(
        later_top_ref, jnp.maximum, dims[0]).reshape(later_top_ref.shape)


def second_kernel(
    dims, n_vbs, table_ref, t_ref, top_ref, first_top_ref, first_acc_ref, first_tot_ref, facc_ref,
    ftop_ref, ftot_ref, *refs,
):
    heads, page_rows, pages_dev, sub = dims
    half = t_ref.shape[0]
    req_dev = ftop_ref.shape[0]
    vbs, (keep_ref, *send_refs, acc_s, tot_s) = refs[:n_vbs], refs[n_vbs:]
    group = keep_ref.shape[2]

    def put(slab, value, coded=0):
        keep_ref[0, slab] = value[:group]
        for place, ref in enumerate(send_refs):
            send = value[(place + 1) * group:(place + 2) * group]
            ref[0, slab] = pieces_of(send, coded) if coded else send.astype(jnp.bfloat16)

    def step(i, _):
        value_request(dims, half + i, table_ref, t_ref, top_ref, i, vbs, acc_s, tot_s)
        return 0

    lax.fori_loop(0, half, step, 0, unroll=True)
    flat = (req_dev * sub, LANES)
    tots = jnp.concatenate(
        [reduce_rows(ref, jnp.add, heads) for ref in (first_tot_ref, tot_s)], axis=0)
    top = jnp.concatenate(
        [ref[...].reshape(half * sub, LANES) for ref in (first_top_ref, top_ref)], axis=0)
    ftop = ftop_ref[...].reshape(flat)
    both = jnp.maximum(top, ftop)
    fade, ffade = jnp.exp2(top - both), jnp.exp2(ftop - both)
    tots = tots * fade + ftot_ref[...].reshape(flat) * ffade
    fade, ffade = fade / tots, ffade / tots
    lses = both + jnp.log2(tots)
    for i in range(req_dev):
        acc_ref = first_acc_ref if i < half else acc_s
        rows = slice(i * sub, (i + 1) * sub)
        for h in range(heads):
            part = slice(h * sub, (h + 1) * sub)
            some = acc_ref[i % half, part, :] * rows_of(fade[rows], h)
            some = some + facc_ref[i, part, :] * rows_of(ffade[rows], h)
            put(i * heads + h, some)
    put(req_dev * heads, by_request(lses, heads, sub, range(req_dev)), heads)


def put_rows(keep_ref, send_ref, place, value, heads=0):
    half = value.shape[0] // 2
    send = value[half:]
    keep_ref[place] = value[:half]
    send_ref[place] = pieces_of(send, heads) if heads else send.astype(jnp.bfloat16)


def by_request(lses, heads, sub, requests):
    lane = lax.broadcasted_iota(jnp.int32, (sub, LANES), 1)
    out = jnp.zeros((sub, LANES), jnp.float32)
    for i, n in enumerate(requests):
        out = jnp.where(lane // (4 * heads) == i, lses[n * sub:(n + 1) * sub], out)
    return out


def fresh_kernel(dims, pieces, n_req, slots_ref, counts_ref, kf, vf, *refs):
    heads, page_rows, slots, sub = dims
    q_refs, refs = refs[:1] + refs[1:n_req][::-1], list(refs[n_req:])
    req_dev = q_refs[0].shape[0]
    pool = [refs.pop(0)] if pieces else []
    keep_ref, send_ref, acc_ref, top_ref, tot_ref, *refs = refs
    target = [refs.pop(0)] if pieces else []
    t_s, p_s, *sem = refs
    copies = ValueCopies(pool + target + sem, 0, pieces)
    copies.start()
    lane = lax.broadcasted_iota(jnp.int32, (sub, LANES), 1)
    onehots = [(lane % heads == h).astype(jnp.bfloat16) for h in range(heads)]
    columns = slots * page_rows
    wide = min(SCORE_WIDE, columns)
    per = wide // page_rows
    own = lax.axis_index("req")
    requests = [(own ^ k) * req_dev + i for k in range(n_req) for i in range(req_dev)]
    n_reqs = len(requests)
    tops = []
    for n, request in enumerate(requests):
        limit = counts_ref[request] * page_rows
        top = jnp.full((sub, LANES), NEG, jnp.float32)
        for c in range(columns // wide):
            keys = pages_of([kf], slots_ref, request * slots + c * per, per)
            parts = score_parts(
                q_refs[n // req_dev][n % req_dev], keys, lane, limit, c * wide, heads, sub)
            for j, part in enumerate(parts):
                t_s[n, :, c * wide + j * LANES:c * wide + (j + 1) * LANES] = part
            top = jnp.maximum(top, fold_max(parts))
        tops.append(top)
    tops = class_reduce(jnp.concatenate(tops, axis=0), jnp.maximum, heads)
    tots = []
    for n in range(n_reqs):
        tot = jnp.zeros((sub, LANES), jnp.float32)
        for j in range(columns // LANES):
            p = jnp.exp2(
                t_s[n, :, j * LANES:(j + 1) * LANES] - tops[n * sub:(n + 1) * sub])
            tot = tot + p
            p_s[n, :, j * LANES:(j + 1) * LANES] = spread(p, onehots)
        tots.append(tot)
    tots = class_reduce(jnp.concatenate(tots, axis=0), jnp.add, heads)
    whole = 1.0 / tots
    lses = tops + jnp.log2(tots)
    for n, request in enumerate(requests):
        values = pages_of([vf], slots_ref, request * slots, slots)
        acc = jnp.dot(p_s[n], values, preferred_element_type=jnp.float32)
        rows = slice(n * sub, (n + 1) * sub)
        block, i = n // req_dev - 1, n % req_dev
        if block < 0:
            acc_ref[i] = acc
            top_ref[i] = tops[rows]
            tot_ref[i] = tots[rows]
            continue
        for h in range(heads):
            some = acc[h * sub:(h + 1) * sub] * rows_of(whole[rows], h)
            put_rows(keep_ref, send_ref, (block, i * heads + h), some)
    for block in range(n_req - 1):
        first = (block + 1) * req_dev
        lse = by_request(lses, heads, sub, range(first, first + req_dev))
        put_rows(keep_ref, send_ref, (block, req_dev * heads), lse, heads)
    copies.wait()


def pieces_of(lse, heads):
    lane = lax.broadcasted_iota(jnp.int32, lse.shape, 1)
    kind = lane % (4 * heads) // heads
    high = lse.astype(jnp.bfloat16).astype(jnp.float32)
    rest = lse - high
    mid = rest.astype(jnp.bfloat16).astype(jnp.float32)
    both = jnp.where(kind == 1, mid, rest - mid)
    return jnp.where(kind == 0, high, both).astype(jnp.bfloat16)


def whole_of(pieces, heads):
    x = pieces.astype(jnp.float32)
    lane = lax.broadcasted_iota(jnp.int32, x.shape, 1)
    kind = lane % (4 * heads) // heads
    x = x + pltpu.roll(x, LANES - heads, 1) + pltpu.roll(x, LANES - 2 * heads, 1)
    same = x
    for m in (1, 2):
        same = jnp.where(kind == m, pltpu.roll(x, m * heads, 1), same)
    return same


def merge_kernel(heads, skip, goals, keep_ref, got_ref, *outs):
    blocks, slabs, rows, _ = keep_ref.shape
    slabs -= 1

    def put(block, slab, value, coded=0):
        if goals[block] is None:
            put_rows(outs[0], outs[1], (block, slab), value, coded)
        else:
            which, place = goals[block]
            if outs[which].dtype == jnp.bfloat16:
                value = pieces_of(value, coded) if coded else value.astype(jnp.bfloat16)
            outs[which][place, slab] = value

    for block in range(blocks):
        own = keep_ref[block, slabs]
        other = whole_of(got_ref[block + skip, slabs], heads)
        top = jnp.maximum(own, other)
        share = jnp.exp2(own - top)
        tot = share + jnp.exp2(other - top)
        share = share / tot
        for slab in range(slabs):
            at = slab // heads * 4 * heads + slab % heads
            part = jnp.broadcast_to(share[:, at:at + 1], (rows, LANES))
            kept = keep_ref[block, slab]
            got = got_ref[block + skip, slab].astype(jnp.float32)
            put(block, slab, part * kept + (1.0 - part) * got)
        put(block, slabs, top + jnp.log2(tot), heads)


def last_kernel(keep_ref, *refs):
    *got_refs, out_ref = refs
    req_dev, heads, group, _ = out_ref.shape
    slabs = req_dev * heads
    parts = [keep_ref.at[0]] + [ref.at[0] for ref in got_refs]
    lses = [keep_ref[0, slabs]] + [whole_of(ref[0, slabs], heads) for ref in got_refs]
    top = fold_max(lses)
    shares = [jnp.exp2(lse - top) for lse in lses]
    tot = shares[0]
    for share in shares[1:]:
        tot = tot + share
    shares = [share / tot for share in shares]
    for slab in range(slabs):
        at = slab // heads * 4 * heads + slab % heads
        total = jnp.zeros((group, LANES), jnp.float32)
        for part, share in zip(parts, shares):
            total = total + part[slab].astype(jnp.float32) * jnp.broadcast_to(
                share[:, at:at + 1], (group, LANES))
        out_ref[slab // heads, slab % heads] = total.astype(jnp.bfloat16)


def params(mib):
    return pltpu.CompilerParams(vmem_limit_bytes=mib * 2**20)


def local(query, kv_pool, page_table, context_len, fresh_kv, fresh_bucket):
    n_ctx = lax.axis_size("ctx")
    n_req = lax.axis_size("req")
    req_dev, heads, group, head_dim = query.shape
    pool_slots, page = kv_pool.shape[:2]
    new_dev = fresh_kv.shape[0]
    pages_dev = page_table.shape[1]
    n_reqs = n_req * req_dev
    slots = CAP * n_ctx
    sub = n_ctx * group
    rows = heads * sub
    page_rows = page * heads

    smem = lambda count: jax.ShapeDtypeStruct((count,), jnp.int32)
    bf16 = lambda *shape: jax.ShapeDtypeStruct(shape, jnp.bfloat16)
    f32 = lambda *shape: jax.ShapeDtypeStruct(shape, jnp.float32)
    columns = pages_dev * page_rows
    split = heads % 4 == 0
    pieces = 8 if split else 0

    ctx_offsets = [0]
    for bit in bits_of("ctx"):
        ctx_offsets += [offset ^ bit for offset in ctx_offsets]
    near = [swap(query, "ctx", offset) for offset in ctx_offsets[1:]]
    if split:
        in_hbm = lambda a: pltpu.with_memory_space_constraint(a, pltpu.HBM)
        pool = in_hbm(kv_pool)
        half = lambda count: bf16(count, page, heads, LANES)
        query, kf, vf = pl.pallas_call(
            stage_fresh_kernel,
            out_shape=(bf16(*query.shape), half(new_dev), half(new_dev)),
            in_specs=[HBM] * 2,
            out_specs=(VMEM,) * 3,
            scratch_shapes=[pltpu.SemaphoreType.DMA((2, 4)), pltpu.SemaphoreType.DMA],
            compiler_params=params(2),
            cost_estimate=pl.CostEstimate(
                flops=0, transcendentals=0, bytes_accessed=4 * fresh_kv.size),
            name="stage_fresh",
        )(in_hbm(query), in_hbm(fresh_kv))
        kf, *near = lax.optimization_barrier((kf, *near))
        kb, slot_table, counts = pl.pallas_call(
            functools.partial(stage_keys_kernel, n_ctx, slots),
            out_shape=(half(pool_slots), smem(n_reqs * slots), smem(n_reqs)),
            in_specs=[HBM] * 2,
            out_specs=(VMEM, SMEM, SMEM),
            scratch_shapes=[
                pltpu.SMEM((new_dev,), jnp.int32), pltpu.SemaphoreType.DMA((pieces,)),
                pltpu.SemaphoreType.DMA],
            compiler_params=params(2),
            cost_estimate=pl.CostEstimate(
                flops=0, transcendentals=0, bytes_accessed=2 * kv_pool.size),
            name="stage_keys",
        )(in_hbm(fresh_bucket), pool)
        kb, kf, vf = (a.reshape(a.shape[0], page_rows, LANES) for a in (kb, kf, vf))
        value_in, value_specs = (pool,), [HBM]
        value_out = (bf16(pool_slots, page // 2, heads, LANES),)
        value_scratch = [pltpu.SemaphoreType.DMA((pieces,))]
    else:
        kb, vb, kf, vf = (
            a[..., h * LANES:(h + 1) * LANES].reshape(a.shape[0], page_rows, LANES)
            for a in (kv_pool, fresh_kv) for h in (0, 1)
        )
        slot_table, counts = pl.pallas_call(
            functools.partial(list_kernel, n_ctx, slots),
            out_shape=(smem(n_reqs * slots), smem(n_reqs)),
            in_specs=[SMEM],
            out_specs=(SMEM,) * 2,
            name="list",
        )(fresh_bucket)
        value_in, value_specs, value_out, value_scratch = (), [], (), []

    queries = jnp.stack([query] + near).transpose(1, 2, 0, 3, 4).reshape(req_dev, rows, head_dim)
    far = [swap(queries, "req", k) for k in range(n_req - 1, 0, -1)][::-1]

    slabs = req_dev * heads + 1
    left = sub // 2
    keep, send, facc, ftop, ftot, *vbs = pl.pallas_call(
        functools.partial(fresh_kernel, (heads, page_rows, slots, sub), pieces, n_req),
        out_shape=(
            f32(n_req - 1, slabs, left, LANES), bf16(n_req - 1, slabs, left, LANES),
            f32(req_dev, rows, LANES), f32(req_dev, sub, LANES), f32(req_dev, sub, LANES),
        ) + value_out,
        in_specs=[SMEM] * 2 + [VMEM] * (2 + n_req) + value_specs,
        out_specs=(VMEM,) * (5 + len(value_out)),
        scratch_shapes=[
            pltpu.VMEM((n_reqs, sub, slots * page_rows), jnp.float32),
            pltpu.VMEM((n_reqs, rows, slots * page_rows), jnp.bfloat16),
        ] + value_scratch,
        compiler_params=params(8),
        cost_estimate=pl.CostEstimate(
            flops=4 * n_reqs * rows * slots * page_rows * LANES,
            transcendentals=n_reqs * sub * slots * page_rows, bytes_accessed=2 * fresh_kv.size),
        name="fresh",
    )(slot_table, counts, kf, vf, queries, *far[::-1], *value_in)

    def merge(keep, got, skip, goals, shapes):
        return pl.pallas_call(
            functools.partial(merge_kernel, heads, skip, goals),
            out_shape=shapes,
            in_specs=[VMEM] * 2,
            out_specs=[VMEM] * len(shapes),
            compiler_params=params(8),
            name="merge",
        )(keep, got)

    def halved(keep, got):
        shape = (keep.shape[0], slabs, keep.shape[2] // 2, LANES)
        return merge(keep, got, 0, [None] * keep.shape[0], [f32(*shape), bf16(*shape)])

    def sorted_by(keep, got, skip, offsets, bit):
        sends = [offset for offset in offsets if offset & bit]
        keeps = [offset for offset in offsets if not offset & bit]
        goals = [
            (0, sends.index(o)) if o in sends else (1, keeps.index(o)) for o in offsets]
        shape = lambda count: (count, slabs, group, LANES)
        shapes = [bf16(*shape(len(sends)))] + ([f32(*shape(len(keeps)))] if keeps else [])
        return merge(keep, got, skip, goals, shapes), keeps

    ctx_bits = list(bits_of("ctx"))[::-1]
    req_bits = list(bits_of("req"))[::-1]
    dims = (heads, page_rows, pages_dev, sub)
    table = page_table.reshape(-1)
    part = req_dev // 2
    cost = lambda scores, values: pl.CostEstimate(
        flops=2 * (scores + values) * rows * columns * LANES,
        transcendentals=values * sub * columns,
        bytes_accessed=(scores + values) * columns * LANES * 2)
    send, queries = lax.optimization_barrier((send, queries))
    got = swap(send, "ctx", ctx_bits[0])
    t, top, *more = pl.pallas_call(
        functools.partial(first_kernel, dims, pieces),
        out_shape=(f32(part, sub, columns), f32(part, sub, LANES)) + value_out,
        in_specs=[SMEM] * 2 + [VMEM] * 2 + value_specs,
        out_specs=(VMEM,) * (2 + len(value_out)),
        scratch_shapes=value_scratch,
        compiler_params=params(4),
        cost_estimate=cost(part, 0),
        name="first",
    )(table, context_len, queries, kb, *value_in)
    vbs = [a.reshape(a.shape[0], -1, LANES) for a in vbs + more] if split else [vb]
    got, top = lax.optimization_barrier((got, top))
    for bit in ctx_bits[1:]:
        keep, send = halved(keep, got)
        send, top = lax.optimization_barrier((send, top))
        got = swap(send, "ctx", bit)
    later, later_top, acc, tot = pl.pallas_call(
        functools.partial(middle_kernel, dims),
        out_shape=(
            f32(part, sub, columns), f32(part, sub, LANES), f32(part, rows, LANES),
            f32(part, sub, LANES)),
        in_specs=[SMEM] * 2 + [VMEM] * (4 + len(vbs)),
        out_specs=(VMEM,) * 4,
        compiler_params=params(4),
        cost_estimate=cost(part, part),
        name="middle",
    )(table, context_len, queries, kb, t, top, *vbs)
    got, later_top = lax.optimization_barrier((got, later_top))
    offsets = list(range(1, n_req))
    (send, *kept), offsets = sorted_by(keep, got, 0, offsets, req_bits[0])
    send, later_top = lax.optimization_barrier((send, later_top))
    got = swap(send, "req", req_bits[0])
    arrived = [got]
    own_keep, *own_sends = pl.pallas_call(
        functools.partial(second_kernel, dims, len(vbs)),
        out_shape=(f32(1, slabs, group, LANES),)
        + (bf16(1, slabs, group, LANES),) * (n_ctx - 1),
        in_specs=[SMEM] + [VMEM] * (8 + len(vbs)),
        out_specs=(VMEM,) * n_ctx,
        scratch_shapes=[
            pltpu.VMEM((part, rows, LANES), jnp.float32),
            pltpu.VMEM((part, sub, LANES), jnp.float32)],
        compiler_params=params(4),
        cost_estimate=cost(0, part),
        name="second",
    )(table, later, later_top, top, acc, tot, facc, ftop, ftot, *vbs)
    got, own_keep = lax.optimization_barrier((got, own_keep))
    arrived += [
        swap(one, "ctx", offset) for one, offset in zip(own_sends, ctx_offsets[1:])]
    for bit in req_bits[1:]:
        (send, *kept), offsets = sorted_by(kept[0], got, 1, offsets, bit)
        got = swap(send, "req", bit)
        arrived.append(got)
    return pl.pallas_call(
        last_kernel,
        out_shape=bf16(req_dev, heads, group, LANES),
        in_specs=[VMEM] * (1 + len(arrived)),
        out_specs=VMEM,
        compiler_params=params(8),
        name="last",
    )(own_keep, *arrived)


def solution(mesh):
    placed = (
        P("req", "kvh", "ctx", None),
        P(("req", "ctx"), None, "kvh", None),
        P("req", "ctx"),
        P("req"),
        P(("req", "ctx"), None, "kvh", None),
        P(("req", "ctx")),
    )
    return jax.shard_map(
        local, mesh=mesh, in_specs=placed, out_specs=P("req", "kvh", "ctx", None), check_vma=False
    )
```

```python
import functools
import math

import jax
import jax.numpy as jnp
from jax import lax
from jax.experimental import pallas as pl
from jax.experimental.pallas import tpu as pltpu
from jax.sharding import PartitionSpec as P

NEG = -1e30
CAP = 2
LANES = 128
SCALE = math.log2(math.e) / math.sqrt(LANES)
SCORE_WIDE = 256
VALUE_WIDE = 1024
VMEM = pl.BlockSpec(memory_space=pltpu.VMEM)
SMEM = pl.BlockSpec(memory_space=pltpu.SMEM)
HBM = pl.BlockSpec(memory_space=pltpu.HBM)


def swap(value, axis, bit):
    return lax.ppermute(value, axis, [(n, n ^ bit) for n in range(lax.axis_size(axis))])


def bits_of(axis):
    bit = lax.axis_size(axis) // 2
    while bit:
        yield bit
        bit //= 2


def half_copies(pool_ref, target, sem, half, pieces, tokens=None):
    each = pool_ref.shape[0] // pieces
    tokens = tokens or pl.ds(0, pool_ref.shape[1])
    return [
        pltpu.make_async_copy(
            pool_ref.at[pl.ds(n * each, each), tokens, :, pl.ds(half * LANES, LANES)],
            target.at[pl.ds(n * each, each)], sem.at[n])
        for n in range(pieces)
    ]


class ValueCopies:
    def __init__(self, refs, part, pieces):
        self.copies = []
        if pieces:
            pool_ref, target, sem = refs
            count = pool_ref.shape[1] // 2
            self.copies = half_copies(
                pool_ref, target, sem, 1, pieces, pl.ds(part * count, count))

    def start(self):
        for one in self.copies:
            one.start()

    def wait(self):
        for one in self.copies:
            one.wait()


def stage_fresh_kernel(query_hbm, fresh_ref, query_ref, kf, vf, sem, query_sem):
    copies = [pltpu.make_async_copy(query_hbm, query_ref, query_sem)]
    for half, to in enumerate((kf, vf)):
        copies += half_copies(fresh_ref, to, sem.at[half], half, sem.shape[1])
    for one in copies:
        one.start()
    for one in copies:
        one.wait()


def stage_keys_kernel(
    n_ctx, slots, bucket_hbm, pool_ref, kb, slots_ref, counts_ref, bucket_ref, sem, bucket_sem,
):
    listed = pltpu.make_async_copy(bucket_hbm, bucket_ref, bucket_sem)
    copies = half_copies(pool_ref, kb, sem, 0, sem.shape[0])
    listed.start()
    for one in copies:
        one.start()
    listed.wait()
    list_fresh(n_ctx, slots, bucket_ref, slots_ref, counts_ref)
    for one in copies:
        one.wait()


def list_kernel(n_ctx, slots, bucket_ref, slots_ref, counts_ref):
    list_fresh(n_ctx, slots, bucket_ref, slots_ref, counts_ref)


def list_fresh(n_ctx, slots, bucket_ref, slots_ref, counts_ref):
    for n in range(counts_ref.shape[0]):
        counts_ref[n] = 0
    for n in range(slots_ref.shape[0]):
        slots_ref[n] = 0

    def put(page, _):
        request = bucket_ref[page] >> (n_ctx.bit_length() - 1)
        count = counts_ref[request]
        slots_ref[request * slots + count] = page
        counts_ref[request] = count + 1
        return 0

    lax.fori_loop(0, bucket_ref.shape[0], put, 0, unroll=16)


def class_reduce(x, op, heads):
    step = heads
    while step < LANES:
        x = op(x, pltpu.roll(x, step, 1))
        step *= 2
    return x


def pages_of(refs, table_ref, first, count):
    pages = [table_ref[first + n] for n in range(count)]
    return jnp.concatenate([ref[page] for page in pages for ref in refs], axis=0)


def score_parts(q, keys, lane, limit, first, heads, sub):
    s = lax.dot_general(q, keys, (((1,), (1,)), ((), ())), preferred_element_type=jnp.float32)
    out = []
    for j in range(s.shape[1] // LANES):
        part = s[:, j * LANES:(j + 1) * LANES]
        one = part[:sub]
        for h in range(1, heads):
            one = jnp.where(lane % heads == h, part[h * sub:(h + 1) * sub], one)
        out.append(jnp.where(lane < limit - (first + j * LANES), one * SCALE, NEG))
    return out


def spread(p, onehots):
    p = p.astype(jnp.bfloat16)
    return jnp.concatenate([p * one for one in onehots], axis=0)


def rows_of(x, h):
    return jnp.broadcast_to(x[:, h:h + 1], x.shape)


def fold_max(parts):
    top = parts[0]
    for part in parts[1:]:
        top = jnp.maximum(top, part)
    return top


def score_request(dims, i, table_ref, len_ref, q_ref, kb, t_ref, top_ref, at):
    heads, page_rows, pages_dev, sub = dims
    columns = pages_dev * page_rows
    wide = min(SCORE_WIDE, columns)
    per = wide // page_rows
    lane = lax.broadcasted_iota(jnp.int32, (sub, LANES), 1)
    top = jnp.full((sub, LANES), NEG, jnp.float32)
    limit = len_ref[i] * heads - lax.axis_index("ctx") * columns
    for c in range(columns // wide):
        keys = pages_of([kb], table_ref, i * pages_dev + c * per, per)
        parts = score_parts(q_ref[i], keys, lane, limit, c * wide, heads, sub)
        for j, part in enumerate(parts):
            t_ref[at, :, c * wide + j * LANES:c * wide + (j + 1) * LANES] = part
        top = jnp.maximum(top, fold_max(parts))
    top_ref[at] = top


def value_request(dims, i, table_ref, t_ref, top_ref, at, vbs, acc_ref, tot_ref):
    heads, page_rows, pages_dev, sub = dims
    columns = pages_dev * page_rows
    wide = min(VALUE_WIDE, columns)
    per = wide // page_rows
    lane = lax.broadcasted_iota(jnp.int32, (sub, LANES), 1)
    onehots = [(lane % heads == h).astype(jnp.bfloat16) for h in range(heads)]
    tot = jnp.zeros((sub, LANES), jnp.float32)
    acc = jnp.zeros((heads * sub, LANES), jnp.float32)
    top = top_ref[at]
    for c in range(columns // wide):
        weights = []
        for j in range(wide // LANES):
            where = c * wide + j * LANES
            p = jnp.exp2(t_ref[at, :, where:where + LANES] - top)
            tot = tot + p
            weights.append(spread(p, onehots))
        values = pages_of(vbs, table_ref, i * pages_dev + c * per, per)
        acc = acc + jnp.dot(
            jnp.concatenate(weights, axis=1), values, preferred_element_type=jnp.float32)
    acc_ref[at] = acc
    tot_ref[at] = tot


def reduce_rows(ref, op, heads):
    flat = ref[...].reshape(ref.shape[0] * ref.shape[1], LANES)
    return class_reduce(flat, op, heads)


def first_kernel(dims, pieces, table_ref, len_ref, q_ref, kb, *refs):
    refs = list(refs)
    pool = [refs.pop(0)] if pieces else []
    t_ref, top_ref, *refs = refs
    copies = ValueCopies(pool + refs, 1, pieces)
    copies.start()

    def step(i, _):
        score_request(dims, i, table_ref, len_ref, q_ref, kb, t_ref, top_ref, i)
        return 0

    lax.fori_loop(0, t_ref.shape[0], step, 0, unroll=True)
    top_ref[...] = reduce_rows(top_ref, jnp.maximum, dims[0]).reshape(top_ref.shape)
    copies.wait()


def middle_kernel(dims, table_ref, len_ref, q_ref, kb, t_ref, top_ref, *refs):
    *vbs, later_ref, later_top_ref, acc_ref, tot_ref = refs
    half = t_ref.shape[0]

    def step(i, _):
        score_request(
            dims, half + i, table_ref, len_ref, q_ref, kb, later_ref, later_top_ref, i)
        value_request(dims, i, table_ref, t_ref, top_ref, i, vbs, acc_ref, tot_ref)
        return 0

    lax.fori_loop(0, half, step, 0, unroll=True)
    later_top_ref[...] = reduce_rows(
        later_top_ref, jnp.maximum, dims[0]).reshape(later_top_ref.shape)


def second_kernel(
    dims, n_vbs, table_ref, t_ref, top_ref, first_top_ref, first_acc_ref, first_tot_ref, facc_ref,
    ftop_ref, ftot_ref, *refs,
):
    heads, page_rows, pages_dev, sub = dims
    half = t_ref.shape[0]
    req_dev = ftop_ref.shape[0]
    vbs, (keep_ref, *send_refs, acc_s, tot_s) = refs[:n_vbs], refs[n_vbs:]
    group = keep_ref.shape[2]

    def put(slab, value, coded=0):
        keep_ref[0, slab] = value[:group]
        for place, ref in enumerate(send_refs):
            send = value[(place + 1) * group:(place + 2) * group]
            ref[0, slab] = pieces_of(send, coded) if coded else send.astype(jnp.bfloat16)

    def step(i, _):
        value_request(dims, half + i, table_ref, t_ref, top_ref, i, vbs, acc_s, tot_s)
        return 0

    lax.fori_loop(0, half, step, 0, unroll=True)
    flat = (req_dev * sub, LANES)
    tots = jnp.concatenate(
        [reduce_rows(ref, jnp.add, heads) for ref in (first_tot_ref, tot_s)], axis=0)
    top = jnp.concatenate(
        [ref[...].reshape(half * sub, LANES) for ref in (first_top_ref, top_ref)], axis=0)
    ftop = ftop_ref[...].reshape(flat)
    both = jnp.maximum(top, ftop)
    fade, ffade = jnp.exp2(top - both), jnp.exp2(ftop - both)
    tots = tots * fade + ftot_ref[...].reshape(flat) * ffade
    fade, ffade = fade / tots, ffade / tots
    lses = both + jnp.log2(tots)
    for i in range(req_dev):
        acc_ref = first_acc_ref if i < half else acc_s
        rows = slice(i * sub, (i + 1) * sub)
        for h in range(heads):
            part = slice(h * sub, (h + 1) * sub)
            some = acc_ref[i % half, part, :] * rows_of(fade[rows], h)
            some = some + facc_ref[i, part, :] * rows_of(ffade[rows], h)
            put(i * heads + h, some)
    put(req_dev * heads, by_request(lses, heads, sub, range(req_dev)), heads)


def put_rows(keep_ref, send_ref, place, value, heads=0):
    half = value.shape[0] // 2
    send = value[half:]
    keep_ref[place] = value[:half]
    send_ref[place] = pieces_of(send, heads) if heads else send.astype(jnp.bfloat16)


def by_request(lses, heads, sub, requests):
    lane = lax.broadcasted_iota(jnp.int32, (sub, LANES), 1)
    out = jnp.zeros((sub, LANES), jnp.float32)
    for i, n in enumerate(requests):
        out = jnp.where(lane // (4 * heads) == i, lses[n * sub:(n + 1) * sub], out)
    return out


def fresh_kernel(dims, pieces, n_req, slots_ref, counts_ref, kf, vf, *refs):
    heads, page_rows, slots, sub = dims
    q_refs, refs = refs[:n_req], list(refs[n_req:])
    req_dev = q_refs[0].shape[0]
    pool = [refs.pop(0)] if pieces else []
    keep_ref, send_ref, acc_ref, top_ref, tot_ref, *refs = refs
    target = [refs.pop(0)] if pieces else []
    t_s, p_s, *sem = refs
    copies = ValueCopies(pool + target + sem, 0, pieces)
    copies.start()
    lane = lax.broadcasted_iota(jnp.int32, (sub, LANES), 1)
    onehots = [(lane % heads == h).astype(jnp.bfloat16) for h in range(heads)]
    columns = slots * page_rows
    wide = min(SCORE_WIDE, columns)
    per = wide // page_rows
    own = lax.axis_index("req")
    requests = [(own ^ k) * req_dev + i for k in range(n_req) for i in range(req_dev)]
    n_reqs = len(requests)
    tops = []
    for n, request in enumerate(requests):
        limit = counts_ref[request] * page_rows
        top = jnp.full((sub, LANES), NEG, jnp.float32)
        for c in range(columns // wide):
            keys = pages_of([kf], slots_ref, request * slots + c * per, per)
            parts = score_parts(
                q_refs[n // req_dev][n % req_dev], keys, lane, limit, c * wide, heads, sub)
            for j, part in enumerate(parts):
                t_s[n, :, c * wide + j * LANES:c * wide + (j + 1) * LANES] = part
            top = jnp.maximum(top, fold_max(parts))
        tops.append(top)
    tops = class_reduce(jnp.concatenate(tops, axis=0), jnp.maximum, heads)
    tots = []
    for n in range(n_reqs):
        tot = jnp.zeros((sub, LANES), jnp.float32)
        for j in range(columns // LANES):
            p = jnp.exp2(
                t_s[n, :, j * LANES:(j + 1) * LANES] - tops[n * sub:(n + 1) * sub])
            tot = tot + p
            p_s[n, :, j * LANES:(j + 1) * LANES] = spread(p, onehots)
        tots.append(tot)
    tots = class_reduce(jnp.concatenate(tots, axis=0), jnp.add, heads)
    whole = 1.0 / tots
    lses = tops + jnp.log2(tots)
    for n, request in enumerate(requests):
        values = pages_of([vf], slots_ref, request * slots, slots)
        acc = jnp.dot(p_s[n], values, preferred_element_type=jnp.float32)
        rows = slice(n * sub, (n + 1) * sub)
        block, i = n // req_dev - 1, n % req_dev
        if block < 0:
            acc_ref[i] = acc
            top_ref[i] = tops[rows]
            tot_ref[i] = tots[rows]
            continue
        for h in range(heads):
            some = acc[h * sub:(h + 1) * sub] * rows_of(whole[rows], h)
            put_rows(keep_ref, send_ref, (block, i * heads + h), some)
    for block in range(n_req - 1):
        first = (block + 1) * req_dev
        lse = by_request(lses, heads, sub, range(first, first + req_dev))
        put_rows(keep_ref, send_ref, (block, req_dev * heads), lse, heads)
    copies.wait()


def pieces_of(lse, heads):
    lane = lax.broadcasted_iota(jnp.int32, lse.shape, 1)
    kind = lane % (4 * heads) // heads
    high = lse.astype(jnp.bfloat16).astype(jnp.float32)
    rest = lse - high
    mid = rest.astype(jnp.bfloat16).astype(jnp.float32)
    both = jnp.where(kind == 1, mid, rest - mid)
    return jnp.where(kind == 0, high, both).astype(jnp.bfloat16)


def whole_of(pieces, heads):
    x = pieces.astype(jnp.float32)
    lane = lax.broadcasted_iota(jnp.int32, x.shape, 1)
    kind = lane % (4 * heads) // heads
    x = x + pltpu.roll(x, LANES - heads, 1) + pltpu.roll(x, LANES - 2 * heads, 1)
    same = x
    for m in (1, 2):
        same = jnp.where(kind == m, pltpu.roll(x, m * heads, 1), same)
    return same


def merge_kernel(heads, skip, goals, keep_ref, got_ref, *outs):
    blocks, slabs, rows, _ = keep_ref.shape
    slabs -= 1

    def put(block, slab, value, coded=0):
        if goals[block] is None:
            put_rows(outs[0], outs[1], (block, slab), value, coded)
        else:
            which, place = goals[block]
            if outs[which].dtype == jnp.bfloat16:
                value = pieces_of(value, coded) if coded else value.astype(jnp.bfloat16)
            outs[which][place, slab] = value

    for block in range(blocks):
        own = keep_ref[block, slabs]
        other = whole_of(got_ref[block + skip, slabs], heads)
        top = jnp.maximum(own, other)
        share = jnp.exp2(own - top)
        tot = share + jnp.exp2(other - top)
        share = share / tot
        for slab in range(slabs):
            at = slab // heads * 4 * heads + slab % heads
            part = jnp.broadcast_to(share[:, at:at + 1], (rows, LANES))
            kept = keep_ref[block, slab]
            got = got_ref[block + skip, slab].astype(jnp.float32)
            put(block, slab, part * kept + (1.0 - part) * got)
        put(block, slabs, top + jnp.log2(tot), heads)


def last_kernel(keep_ref, *refs):
    *got_refs, out_ref = refs
    req_dev, heads, group, _ = out_ref.shape
    slabs = req_dev * heads
    parts = [keep_ref.at[0]] + [ref.at[0] for ref in got_refs]
    lses = [keep_ref[0, slabs]] + [whole_of(ref[0, slabs], heads) for ref in got_refs]
    top = fold_max(lses)
    shares = [jnp.exp2(lse - top) for lse in lses]
    tot = shares[0]
    for share in shares[1:]:
        tot = tot + share
    shares = [share / tot for share in shares]
    for slab in range(slabs):
        at = slab // heads * 4 * heads + slab % heads
        total = jnp.zeros((group, LANES), jnp.float32)
        for part, share in zip(parts, shares):
            total = total + part[slab].astype(jnp.float32) * jnp.broadcast_to(
                share[:, at:at + 1], (group, LANES))
        out_ref[slab // heads, slab % heads] = total.astype(jnp.bfloat16)


def params(mib):
    return pltpu.CompilerParams(vmem_limit_bytes=mib * 2**20)


def local(query, kv_pool, page_table, context_len, fresh_kv, fresh_bucket):
    n_ctx = lax.axis_size("ctx")
    n_req = lax.axis_size("req")
    req_dev, heads, group, head_dim = query.shape
    pool_slots, page = kv_pool.shape[:2]
    new_dev = fresh_kv.shape[0]
    pages_dev = page_table.shape[1]
    n_reqs = n_req * req_dev
    slots = CAP * n_ctx
    sub = n_ctx * group
    rows = heads * sub
    page_rows = page * heads

    smem = lambda count: jax.ShapeDtypeStruct((count,), jnp.int32)
    bf16 = lambda *shape: jax.ShapeDtypeStruct(shape, jnp.bfloat16)
    f32 = lambda *shape: jax.ShapeDtypeStruct(shape, jnp.float32)
    columns = pages_dev * page_rows
    split = heads % 4 == 0
    pieces = 8 if split else 0

    ctx_offsets = [0]
    for bit in bits_of("ctx"):
        ctx_offsets += [offset ^ bit for offset in ctx_offsets]
    near = [swap(query, "ctx", offset) for offset in ctx_offsets[1:]]
    if split:
        in_hbm = lambda a: pltpu.with_memory_space_constraint(a, pltpu.HBM)
        pool = in_hbm(kv_pool)
        half = lambda count: bf16(count, page, heads, LANES)
        query, kf, vf = pl.pallas_call(
            stage_fresh_kernel,
            out_shape=(bf16(*query.shape), half(new_dev), half(new_dev)),
            in_specs=[HBM] * 2,
            out_specs=(VMEM,) * 3,
            scratch_shapes=[pltpu.SemaphoreType.DMA((2, 4)), pltpu.SemaphoreType.DMA],
            compiler_params=params(2),
            cost_estimate=pl.CostEstimate(
                flops=0, transcendentals=0, bytes_accessed=4 * fresh_kv.size),
            name="stage_fresh",
        )(in_hbm(query), in_hbm(fresh_kv))
        kf, *near = lax.optimization_barrier((kf, *near))
        kb, slot_table, counts = pl.pallas_call(
            functools.partial(stage_keys_kernel, n_ctx, slots),
            out_shape=(half(pool_slots), smem(n_reqs * slots), smem(n_reqs)),
            in_specs=[HBM] * 2,
            out_specs=(VMEM, SMEM, SMEM),
            scratch_shapes=[
                pltpu.SMEM((new_dev,), jnp.int32), pltpu.SemaphoreType.DMA((pieces,)),
                pltpu.SemaphoreType.DMA],
            compiler_params=params(2),
            cost_estimate=pl.CostEstimate(
                flops=0, transcendentals=0, bytes_accessed=2 * kv_pool.size),
            name="stage_keys",
        )(in_hbm(fresh_bucket), pool)
        kb, kf, vf = (a.reshape(a.shape[0], page_rows, LANES) for a in (kb, kf, vf))
        value_in, value_specs = (pool,), [HBM]
        value_out = (bf16(pool_slots, page // 2, heads, LANES),)
        value_scratch = [pltpu.SemaphoreType.DMA((pieces,))]
    else:
        kb, vb, kf, vf = (
            a[..., h * LANES:(h + 1) * LANES].reshape(a.shape[0], page_rows, LANES)
            for a in (kv_pool, fresh_kv) for h in (0, 1)
        )
        slot_table, counts = pl.pallas_call(
            functools.partial(list_kernel, n_ctx, slots),
            out_shape=(smem(n_reqs * slots), smem(n_reqs)),
            in_specs=[SMEM],
            out_specs=(SMEM,) * 2,
            name="list",
        )(fresh_bucket)
        value_in, value_specs, value_out, value_scratch = (), [], (), []

    queries = jnp.stack([query] + near).transpose(1, 2, 0, 3, 4).reshape(req_dev, rows, head_dim)
    far = [swap(queries, "req", k) for k in range(n_req - 1, 0, -1)][::-1]

    slabs = req_dev * heads + 1
    left = sub // 2
    keep, send, facc, ftop, ftot, *vbs = pl.pallas_call(
        functools.partial(fresh_kernel, (heads, page_rows, slots, sub), pieces, n_req),
        out_shape=(
            f32(n_req - 1, slabs, left, LANES), bf16(n_req - 1, slabs, left, LANES),
            f32(req_dev, rows, LANES), f32(req_dev, sub, LANES), f32(req_dev, sub, LANES),
        ) + value_out,
        in_specs=[SMEM] * 2 + [VMEM] * (2 + n_req) + value_specs,
        out_specs=(VMEM,) * (5 + len(value_out)),
        scratch_shapes=[
            pltpu.VMEM((n_reqs, sub, slots * page_rows), jnp.float32),
            pltpu.VMEM((n_reqs, rows, slots * page_rows), jnp.bfloat16),
        ] + value_scratch,
        compiler_params=params(8),
        cost_estimate=pl.CostEstimate(
            flops=4 * n_reqs * rows * slots * page_rows * LANES,
            transcendentals=n_reqs * sub * slots * page_rows, bytes_accessed=2 * fresh_kv.size),
        name="fresh",
    )(slot_table, counts, kf, vf, queries, *far, *value_in)

    def merge(keep, got, skip, goals, shapes):
        return pl.pallas_call(
            functools.partial(merge_kernel, heads, skip, goals),
            out_shape=shapes,
            in_specs=[VMEM] * 2,
            out_specs=[VMEM] * len(shapes),
            compiler_params=params(8),
            name="merge",
        )(keep, got)

    def halved(keep, got):
        shape = (keep.shape[0], slabs, keep.shape[2] // 2, LANES)
        return merge(keep, got, 0, [None] * keep.shape[0], [f32(*shape), bf16(*shape)])

    def sorted_by(keep, got, skip, offsets, bit):
        sends = [offset for offset in offsets if offset & bit]
        keeps = [offset for offset in offsets if not offset & bit]
        goals = [
            (0, sends.index(o)) if o in sends else (1, keeps.index(o)) for o in offsets]
        shape = lambda count: (count, slabs, group, LANES)
        shapes = [bf16(*shape(len(sends)))] + ([f32(*shape(len(keeps)))] if keeps else [])
        return merge(keep, got, skip, goals, shapes), keeps

    ctx_bits = list(bits_of("ctx"))[::-1]
    req_bits = list(bits_of("req"))[::-1]
    dims = (heads, page_rows, pages_dev, sub)
    table = page_table.reshape(-1)
    part = req_dev // 2
    cost = lambda scores, values: pl.CostEstimate(
        flops=2 * (scores + values) * rows * columns * LANES,
        transcendentals=values * sub * columns,
        bytes_accessed=(scores + values) * columns * LANES * 2)
    send, queries = lax.optimization_barrier((send, queries))
    got = swap(send, "ctx", ctx_bits[0])
    t, top, *more = pl.pallas_call(
        functools.partial(first_kernel, dims, pieces),
        out_shape=(f32(part, sub, columns), f32(part, sub, LANES)) + value_out,
        in_specs=[SMEM] * 2 + [VMEM] * 2 + value_specs,
        out_specs=(VMEM,) * (2 + len(value_out)),
        scratch_shapes=value_scratch,
        compiler_params=params(4),
        cost_estimate=cost(part, 0),
        name="first",
    )(table, context_len, queries, kb, *value_in)
    vbs = [a.reshape(a.shape[0], -1, LANES) for a in vbs + more] if split else [vb]
    got, top = lax.optimization_barrier((got, top))
    for bit in ctx_bits[1:]:
        keep, send = halved(keep, got)
        send, top = lax.optimization_barrier((send, top))
        got = swap(send, "ctx", bit)
    later, later_top, acc, tot = pl.pallas_call(
        functools.partial(middle_kernel, dims),
        out_shape=(
            f32(part, sub, columns), f32(part, sub, LANES), f32(part, rows, LANES),
            f32(part, sub, LANES)),
        in_specs=[SMEM] * 2 + [VMEM] * (4 + len(vbs)),
        out_specs=(VMEM,) * 4,
        compiler_params=params(4),
        cost_estimate=cost(part, part),
        name="middle",
    )(table, context_len, queries, kb, t, top, *vbs)
    got, later_top = lax.optimization_barrier((got, later_top))
    offsets = list(range(1, n_req))
    (send, *kept), offsets = sorted_by(keep, got, 0, offsets, req_bits[0])
    send, later_top = lax.optimization_barrier((send, later_top))
    got = swap(send, "req", req_bits[0])
    arrived = [got]
    own_keep, *own_sends = pl.pallas_call(
        functools.partial(second_kernel, dims, len(vbs)),
        out_shape=(f32(1, slabs, group, LANES),)
        + (bf16(1, slabs, group, LANES),) * (n_ctx - 1),
        in_specs=[SMEM] + [VMEM] * (8 + len(vbs)),
        out_specs=(VMEM,) * n_ctx,
        scratch_shapes=[
            pltpu.VMEM((part, rows, LANES), jnp.float32),
            pltpu.VMEM((part, sub, LANES), jnp.float32)],
        compiler_params=params(4),
        cost_estimate=cost(0, part),
        name="second",
    )(table, later, later_top, top, acc, tot, facc, ftop, ftot, *vbs)
    got, own_keep = lax.optimization_barrier((got, own_keep))
    arrived += [
        swap(one, "ctx", offset) for one, offset in zip(own_sends, ctx_offsets[1:])]
    for bit in req_bits[1:]:
        (send, *kept), offsets = sorted_by(kept[0], got, 1, offsets, bit)
        got = swap(send, "req", bit)
        arrived.append(got)
    return pl.pallas_call(
        last_kernel,
        out_shape=bf16(req_dev, heads, group, LANES),
        in_specs=[VMEM] * (1 + len(arrived)),
        out_specs=VMEM,
        compiler_params=params(8),
        name="last",
    )(own_keep, *arrived)


def solution(mesh):
    placed = (
        P("req", "kvh", "ctx", None),
        P(("req", "ctx"), None, "kvh", None),
        P("req", "ctx"),
        P("req"),
        P(("req", "ctx"), None, "kvh", None),
        P(("req", "ctx")),
    )
    return jax.shard_map(
        local, mesh=mesh, in_specs=placed, out_specs=P("req", "kvh", "ctx", None), check_vma=False
    )
```
